32 devices in a mesh: section: 2 (over core), clip: 4 (over z), tm: 4 (over y, x).
Axes of the slice: x: 2, y: 2, z: 4, core: 2. Of those that a mesh axis runs over, the one named last changes fastest.
Arguments:
- slow_input: float32 [2, 4, 16, 1024, 196], P(None, 'tm', 'clip'), may hold values from -6 to 6
- fast_input: float32 [2, 4, 64, 128, 196], P(None, 'tm', 'clip'), may hold values from -6 to 6
- frame_counts: int32 [2, 4], P(None, 'tm'), may hold values from 4 to 16, as said below
- fast_reduce: float32 [2, 3, 32, 128], P('section'), may hold values from -0.3125 to 0.3125
- fast_spatial: float32 [2, 9, 32, 32], P('section'), may hold values from -0.375 to 0.375
- fast_expand: float32 [2, 128, 32], P('section'), may hold values from -1 to 1
- lateral_conv: float32 [2, 5, 256, 128], P('section'), may hold values from -0.25 to 0.25
- slow_reduce: float32 [2, 3, 256, 1280], P('section'), may hold values from -0.09375 to 0.09375
- slow_spatial: float32 [2, 9, 256, 256], P('section'), may hold values from -0.125 to 0.125
- slow_expand: float32 [2, 1024, 256], P('section'), may hold values from -0.375 to 0.375
- shortcut: float32 [2, 1024, 1280], P('section'), may hold values from -0.15625 to 0.15625
- norm_gain: float32 [2, 3008], P('section'), may hold values from 0.25 to 1.75
- norm_bias: float32 [2, 3008], P('section'), may hold values from -3 to 3
- slow_cotangent: float32 [2, 4, 16, 1024, 196], P(None, 'tm', 'clip'), may hold values from -6 to 6
- fast_cotangent: float32 [2, 4, 64, 128, 196], P(None, 'tm', 'clip'), may hold values from -6 to 6
Outputs:
- slow_output: float32 [2, 2, 4, 16, 1024, 196], P('section', None, 'tm', 'clip')
- fast_output: float32 [2, 2, 4, 64, 128, 196], P('section', None, 'tm', 'clip')
- slow_input_grad: float32 [2, 2, 4, 16, 1024, 196], P('section', None, 'tm', 'clip')
- fast_input_grad: float32 [2, 2, 4, 64, 128, 196], P('section', None, 'tm', 'clip')
- grad_fast_reduce: float32 [2, 3, 32, 128], P('section')
- grad_fast_spatial: float32 [2, 9, 32, 32], P('section')
- grad_fast_expand: float32 [2, 128, 32], P('section')
- grad_lateral_conv: float32 [2, 5, 256, 128], P('section')
- grad_slow_reduce: float32 [2, 3, 256, 1280], P('section')
- grad_slow_spatial: float32 [2, 9, 256, 256], P('section')
- grad_slow_expand: float32 [2, 1024, 256], P('section')
- grad_shortcut: float32 [2, 1024, 1280], P('section')
- grad_norm_gain: float32 [2, 3008], P('section')
- grad_norm_bias: float32 [2, 3008], P('section')
The draws below stay inside these ranges and needn't reach their ends.
Inputs may be any that keep to these rules, and one draw needn't show every extreme that they name: `frame_counts`: in each micro-batch one of the 4 clips has 16 valid slow frames and another one 4; frames at or after a clip's count are padding.
All inputs are finite; a program needn't handle non-finite values.
Results may differ from the reference program's by a relative error of at most 0.0003.
Values sent between devices are 32-bit elements; how exact they have to be, the bound alone decides.
No kernel may reach another device: no remote copies, remote signals or barrier semaphores. Data moves between devices by JAX's collectives and lax.ppermute only.
A program may use at most 448 MiB of HBM per device.

```python
import jax
import jax.numpy as jnp
from jax import lax

C_SLOW = 1024
C_FAST = 128
FAST_INNER = 32
SLOW_INNER = 256
C_LATERAL = 256
SIDE = 14
TS = 16
MIN_FRAMES = 4
MICRO = 2
CLIPS = 4
TF = 64
POSITIONS = 196
C_JOINED = 1280
NORM_WIDTH = 3008


def draw_frame_counts(key, part):
    key = jax.random.fold_in(key, 7)
    subkeys = jax.random.split(key, 3)
    counts = jax.random.randint(subkeys[0], (MICRO, CLIPS), MIN_FRAMES, TS + 1)
    longest = jax.random.randint(subkeys[1], (MICRO, 1), 0, CLIPS)
    offset = jax.random.randint(subkeys[2], (MICRO, 1), 1, CLIPS)
    shortest = (longest + offset) % CLIPS
    slot_index = jnp.arange(CLIPS, dtype=jnp.int32)[None, :]
    counts = jnp.where(slot_index == longest, TS, counts)
    counts = jnp.where(slot_index == shortest, MIN_FRAMES, counts)
    return counts.astype(jnp.int32)


def block_scale(stream_key, dims, cuts, least, largest):
    gain, own = 1.0, jax.random.fold_in(stream_key, 6)
    for position, blocks in cuts:
        draws = jnp.exp(jax.random.uniform(jax.random.fold_in(own, position), (blocks,), jnp.float32, least / len(cuts), largest / len(cuts)))
        gain = gain * jnp.repeat(draws, dims[position] // blocks).reshape([-1 if axis == position else 1 for axis in range(len(dims))])
    return gain


def normal_values(rng, shape, width, bound, cuts=(), kind=jnp.bfloat16):
    entries = jax.random.normal(rng, shape, jnp.float32) * width
    if len(cuts) > 0:
        entries = block_scale(rng, shape, cuts, -0.22, 0.18) * entries
    return jnp.clip(entries, min=-bound, max=bound).astype(kind)


def setup_inputs(seed: int = 0) -> dict:
    seeds = jax.random.split(jax.random.key(seed), 16)
    return {
        "slow_input": normal_values(seeds[0], (MICRO, CLIPS, TS, C_SLOW, POSITIONS), 1.0, 6.0, ((1, 4), (2, 4)), jnp.float32),
        "fast_input": normal_values(seeds[1], (MICRO, CLIPS, TF, C_FAST, POSITIONS), 1.0, 6.0, ((1, 4), (2, 4)), jnp.float32),
        "frame_counts": draw_frame_counts(jax.random.fold_in(seeds[15], 71), 0),
        "fast_reduce": normal_values(seeds[3], (2, 3, FAST_INNER, C_FAST), (3 * C_FAST) ** -0.5, 0.3125, ((0, 2),), jnp.float32),
        "fast_spatial": normal_values(seeds[4], (2, 9, FAST_INNER, FAST_INNER), (9 * FAST_INNER) ** -0.5, 0.375, ((0, 2),), jnp.float32),
        "fast_expand": normal_values(seeds[5], (2, C_FAST, FAST_INNER), FAST_INNER ** -0.5, 1.0, ((0, 2),), jnp.float32),
        "lateral_conv": normal_values(seeds[6], (2, 5, C_LATERAL, C_FAST), (5 * C_FAST) ** -0.5, 0.25, ((0, 2),), jnp.float32),
        "slow_reduce": normal_values(seeds[7], (2, 3, SLOW_INNER, C_JOINED), (3 * C_JOINED) ** -0.5, 0.09375, ((0, 2),), jnp.float32),
        "slow_spatial": normal_values(seeds[8], (2, 9, SLOW_INNER, SLOW_INNER), (9 * SLOW_INNER) ** -0.5, 0.125, ((0, 2),), jnp.float32),
        "slow_expand": normal_values(seeds[9], (2, C_SLOW, SLOW_INNER), SLOW_INNER ** -0.5, 0.375, ((0, 2),), jnp.float32),
        "shortcut": normal_values(seeds[10], (2, C_SLOW, C_JOINED), C_JOINED ** -0.5, 0.15625, ((0, 2),), jnp.float32),
        "norm_gain": jnp.clip(1.0 + 0.15 * jax.random.normal(seeds[11], (2, NORM_WIDTH), jnp.float32), 0.25, 1.75),
        "norm_bias": normal_values(seeds[12], (2, NORM_WIDTH), 0.5, 3.0, ((0, 2),), jnp.float32),
        "slow_cotangent": normal_values(seeds[13], (MICRO, CLIPS, TS, C_SLOW, POSITIONS), 1.0, 6.0, ((1, 4), (2, 4)), jnp.float32),
        "fast_cotangent": normal_values(seeds[14], (MICRO, CLIPS, TF, C_FAST, POSITIONS), 1.0, 6.0, ((1, 4), (2, 4)), jnp.float32),
    }


EPSILON = 1e-05
PRECISE = lax.Precision.HIGHEST

@jax.custom_vjp
def low(v):
    return lax.optimization_barrier(v.astype(jnp.bfloat16)).astype(jnp.float32)

@jax.custom_vjp
def low_back(v):
    return v

def low_keep(v):
    return (low(v), None)

def low_pass(kept, grad):
    return (grad,)

def back_keep(v):
    return (v, None)

def back_low(kept, grad):
    return (low(grad),)
low.defvjp(low_keep, low_pass)
low_back.defvjp(back_keep, back_low)

def shift_table(grid_side):
    places = jnp.arange(grid_side * grid_side, dtype=jnp.int32)
    row_index = places // grid_side
    columns = places % grid_side
    tables = []
    for row_step in (-1, 0, 1):
        for column_step in (-1, 0, 1):
            source_row = row_index + row_step
            source_column = columns + column_step
            inside = (source_row >= 0) & (source_row < grid_side) & (source_column >= 0) & (source_column < grid_side)
            source = source_row * grid_side + source_column
            matched = (places[:, None] == source[None, :]) & inside[None, :]
            tables.append(matched.astype(jnp.float32))
    return jnp.stack(tables)

def pointwise(weight, values):
    return jnp.einsum('oc,btcp->btop', weight, values, precision=PRECISE)

def temporal(padded, weight, stride):
    tap_count = weight.shape[0]
    frames = (padded.shape[1] - tap_count) // stride + 1
    reach_span = stride * (frames - 1) + 1
    result = pointwise(weight[0], padded[:, 0:reach_span:stride])
    for offset in range(1, tap_count):
        result = result + pointwise(weight[offset], padded[:, offset:offset + reach_span:stride])
    return result

def spatial(values, weight, shift_map):
    shifted = jnp.einsum('btcp,kpq->btkcq', values, shift_map, precision=PRECISE)
    return jnp.einsum('btkcq,koc->btoq', shifted, weight, precision=PRECISE)

def frame_pad(values, span_width):
    return jnp.pad(values, ((0, 0), (span_width, span_width), (0, 0), (0, 0)))

def expand_channel(vector):
    return vector[None, None, :, None]

def normalize(values, frame_mask, count_total, gain_part, bias_part):
    weighted = values * frame_mask
    mean_value = lax.optimization_barrier(jnp.sum(weighted, axis=(0, 1, 3))) / count_total
    square = lax.optimization_barrier(jnp.sum(weighted * values, axis=(0, 1, 3))) / count_total
    reciprocal = lax.rsqrt(square - mean_value * mean_value + EPSILON)
    normed = (values - expand_channel(mean_value)) * expand_channel(reciprocal)
    return frame_mask * (expand_channel(gain_part) * normed + expand_channel(bias_part))

def norm_widths(weights):
    fast_reduce, fast_spatial, fast_expand, lateral_conv, slow_reduce, slow_spatial, slow_expand, shortcut = weights
    return [fast_reduce.shape[1], fast_spatial.shape[1], fast_expand.shape[0], lateral_conv.shape[1], slow_reduce.shape[1], slow_spatial.shape[1], slow_expand.shape[0], shortcut.shape[0]]

def norm_pieces(vector, widths):
    pieces = []
    cursor = 0
    for span_width in widths:
        pieces.append(vector[cursor:cursor + span_width])
        cursor = cursor + span_width
    return pieces

def slowfast_block(slow_data, fast_data, counts, weights, gain_vector, bias_vector, shift_map):
    fast_reduce, fast_spatial, fast_expand, lateral_conv, slow_reduce, slow_spatial, slow_expand, shortcut = weights
    widths = norm_widths(weights)
    gain_parts = norm_pieces(gain_vector, widths)
    bias_parts = norm_pieces(bias_vector, widths)
    frames = slow_data.shape[1]
    places = jnp.arange(frames, dtype=jnp.int32)
    slow_mask = (places[None, :] < counts[:, None]).astype(jnp.float32)[:, :, None, None]
    fast_mask = jnp.repeat(slow_mask, 4, axis=1)
    positions = slow_data.shape[3]
    slow_count = jnp.sum(slow_mask) * positions
    fast_count = jnp.sum(fast_mask) * positions
    fast_in = fast_data * fast_mask
    slow_in = slow_data * slow_mask
    hidden = temporal(frame_pad(fast_in, 1), fast_reduce, 1)
    hidden = jax.nn.silu(normalize(hidden, fast_mask, fast_count, gain_parts[0], bias_parts[0]))
    hidden = spatial(hidden, fast_spatial, shift_map)
    hidden = jax.nn.silu(normalize(hidden, fast_mask, fast_count, gain_parts[1], bias_parts[1]))
    hidden = pointwise(fast_expand, hidden)
    fast_out = jax.nn.silu(normalize(hidden, fast_mask, fast_count, gain_parts[2], bias_parts[2]) + fast_in)
    lateral = temporal(frame_pad(fast_out, 2), lateral_conv, 4)
    lateral = jax.nn.silu(normalize(lateral, slow_mask, slow_count, gain_parts[3], bias_parts[3]))
    joined = jnp.concatenate([slow_in, lateral], axis=2)
    inner_act = temporal(frame_pad(joined, 1), slow_reduce, 1)
    inner_act = jax.nn.silu(normalize(inner_act, slow_mask, slow_count, gain_parts[4], bias_parts[4]))
    inner_act = spatial(inner_act, slow_spatial, shift_map)
    inner_act = jax.nn.silu(normalize(inner_act, slow_mask, slow_count, gain_parts[5], bias_parts[5]))
    inner_act = pointwise(slow_expand, inner_act)
    skipped = pointwise(shortcut, joined)
    slow_out = jax.nn.silu(normalize(inner_act, slow_mask, slow_count, gain_parts[6], bias_parts[6]) + normalize(skipped, slow_mask, slow_count, gain_parts[7], bias_parts[7]))
    return (slow_out, fast_out)

def reference(slow_input, fast_input, frame_counts, fast_reduce, fast_spatial, fast_expand, lateral_conv, slow_reduce, slow_spatial, slow_expand, shortcut, norm_gain, norm_bias, slow_cotangent, fast_cotangent):
    shift_map = shift_table(SIDE)
    stacked = (fast_reduce, fast_spatial, fast_expand, lateral_conv, slow_reduce, slow_spatial, slow_expand, shortcut)
    slow_outputs = [[], []]
    fast_outputs = [[], []]
    slow_grads = [[], []]
    fast_grads = [[], []]
    weight_sums = [[jnp.zeros_like(member[0]) for member in stacked] for section_index in range(2)]
    gain_sums = [jnp.zeros_like(norm_gain[0]) for section_index in range(2)]
    bias_sums = [jnp.zeros_like(norm_bias[0]) for section_index in range(2)]
    for micro_index in range(MICRO):
        counts = frame_counts[micro_index]
        slow_data = slow_input[micro_index]
        fast_data = fast_input[micro_index]
        pullbacks = []
        for section_index in range(2):

            def run_block(slow_values, fast_values, weights, gain_vector, bias_vector):
                return slowfast_block(slow_values, fast_values, counts, weights, gain_vector, bias_vector, shift_map)
            weights = tuple((member[section_index] for member in stacked))
            (slow_data, fast_data), pullback = jax.vjp(run_block, slow_data, fast_data, weights, norm_gain[section_index], norm_bias[section_index])
            slow_outputs[section_index].append(slow_data)
            fast_outputs[section_index].append(fast_data)
            pullbacks.append(pullback)
        slow_back = slow_cotangent[micro_index]
        fast_back = fast_cotangent[micro_index]
        for section_index in (1, 0):
            slow_back, fast_back, weight_grads, gain_grad, bias_grad = pullbacks[section_index]((slow_back, fast_back))
            slow_grads[section_index].append(slow_back)
            fast_grads[section_index].append(fast_back)
            weight_sums[section_index] = [total + update for total, update in zip(weight_sums[section_index], weight_grads)]
            gain_sums[section_index] = gain_sums[section_index] + gain_grad
            bias_sums[section_index] = bias_sums[section_index] + bias_grad
    return (jnp.stack([jnp.stack(slow_outputs[0]), jnp.stack(slow_outputs[1])]), jnp.stack([jnp.stack(fast_outputs[0]), jnp.stack(fast_outputs[1])]), jnp.stack([jnp.stack(slow_grads[0]), jnp.stack(slow_grads[1])]), jnp.stack([jnp.stack(fast_grads[0]), jnp.stack(fast_grads[1])]), jnp.stack([weight_sums[0][0], weight_sums[1][0]]), jnp.stack([weight_sums[0][1], weight_sums[1][1]]), jnp.stack([weight_sums[0][2], weight_sums[1][2]]), jnp.stack([weight_sums[0][3], weight_sums[1][3]]), jnp.stack([weight_sums[0][4], weight_sums[1][4]]), jnp.stack([weight_sums[0][5], weight_sums[1][5]]), jnp.stack([weight_sums[0][6], weight_sums[1][6]]), jnp.stack([weight_sums[0][7], weight_sums[1][7]]), jnp.stack([gain_sums[0], gain_sums[1]]), jnp.stack([bias_sums[0], bias_sums[1]]))
```

```python
import math

import jax
import jax.numpy as jnp
from jax import lax
from jax.sharding import PartitionSpec as P

EPSILON = 1e-05
FINE = lax.Precision.HIGH
GROUP = 4
AXES = ("clip", "tm")


def dot_nn(a, b):
    return lax.dot_general(a, b, (((1,), (0,)), ((), ())), precision=FINE)


def dot_nt(a, b):
    return lax.dot_general(a, b, (((1,), (1,)), ((), ())), precision=FINE)


def dot_tn(a, b):
    return lax.dot_general(a, b, (((0,), (0,)), ((), ())), precision=FINE)


def sum_everywhere(vector):
    count = lax.axis_size("clip") * lax.axis_size("tm")
    copies = jnp.broadcast_to(vector[None], (count,) + vector.shape)
    return jnp.sum(lax.all_to_all(copies, AXES, 0, 0), axis=0)


def from_previous(edge):
    count = lax.axis_size("clip")
    return lax.ppermute(edge, "clip", [(i, i + 1) for i in range(count - 1)])


def from_next(edge):
    count = lax.axis_size("clip")
    return lax.ppermute(edge, "clip", [(i + 1, i) for i in range(count - 1)])


def swap(values):
    return lax.ppermute(values, "section", [(0, 1), (1, 0)])


def later(values, edge, frames):
    grid = values.reshape(-1, frames, values.shape[1])
    return jnp.concatenate([edge[:, None], grid[:, :-1]], axis=1).reshape(values.shape)


def earlier(values, edge, frames):
    grid = values.reshape(-1, frames, values.shape[1])
    return jnp.concatenate([grid[:, 1:], edge[:, None]], axis=1).reshape(values.shape)


def first_frame(values, frames):
    return values.reshape(-1, frames, values.shape[1])[:, 0]


def last_frame(values, frames):
    return values.reshape(-1, frames, values.shape[1])[:, -1]


def conv_grid(values, kernel, frames):
    side = math.isqrt(values.shape[0] // frames)
    grid = values.reshape(side, side, frames, values.shape[1])
    out = lax.conv_general_dilated(
        grid, kernel, (1, 1), "SAME", dimension_numbers=("HWNC", "HWIO", "HWNC"), precision=FINE
    )
    return out.reshape(values.shape[0], kernel.shape[3])


def conv_grid_back(values, kernel, grad, frames):
    out, pull = jax.vjp(lambda x, k: conv_grid(x, k, frames), values, kernel)
    return pull(grad)


def silu(v):
    return v * jax.nn.sigmoid(v)


def silu_slope(v):
    s = jax.nn.sigmoid(v)
    return s * (1.0 + v * (1.0 - s))


def fold(vector, channels):
    return jnp.sum(vector.reshape(-1, channels), axis=0)


def spread(vector, width):
    return jnp.tile(vector, width // vector.shape[0])


class Norm:
    def __init__(self, gain, bias):
        self.gain, self.bias, self.channels = gain, bias, gain.shape[0]

    def sums(self, values, mask):
        weighted = values * mask
        return jnp.concatenate(
            [
                fold(jnp.sum(weighted, axis=0), self.channels),
                fold(jnp.sum(weighted * values, axis=0), self.channels),
            ]
        )

    def learn(self, values, totals, count):
        self.values = values
        self.count = count
        self.mean = totals[: self.channels] / count
        square = totals[self.channels :] / count
        self.rstd = lax.rsqrt(square - self.mean * self.mean + EPSILON)

    def normed(self):
        width = self.values.shape[1]
        return (self.values - spread(self.mean, width)) * spread(self.rstd, width)

    def apply(self, mask):
        width = self.values.shape[1]
        return mask * (spread(self.gain, width) * self.normed() + spread(self.bias, width))

    def back_sums(self, grad):
        return jnp.concatenate(
            [
                fold(jnp.sum(grad, axis=0), self.channels),
                fold(jnp.sum(grad * self.normed(), axis=0), self.channels),
            ]
        )

    def back(self, grad, totals, mask):
        width = self.values.shape[1]
        self.bias_grad = totals[: self.channels]
        self.gain_grad = totals[self.channels :]
        scale = spread(self.gain * self.rstd, width)
        low = spread(self.bias_grad / self.count, width)
        slope = spread(self.gain_grad / self.count, width)
        return mask * (scale * (grad - low - self.normed() * slope))


class Section:
    def __init__(self, weights, gain, bias):
        reduce_, spatial, expand, lateral, slow_reduce, slow_spatial, slow_expand, shortcut = weights
        inner, wide = reduce_.shape[1], reduce_.shape[2]
        self.inner, self.wide = inner, wide
        taps = [
            [[float(r == q + k - 1) for k in range(3)] for q in range(GROUP)] for r in range(GROUP)
        ]
        near = jnp.einsum("rqk,koi->riqo", jnp.array(taps, jnp.float32), reduce_, precision="highest")
        far = [
            [[float((r, q, k) in ((3, 0, 0), (0, 3, 2))) for k in range(3)] for q in range(GROUP)]
            for r in range(GROUP)
        ]
        edge = jnp.einsum("rqk,koi->riqo", jnp.array(far, jnp.float32), reduce_, precision="highest")
        self.fast_reduce = jnp.concatenate(
            [near.reshape(GROUP * wide, GROUP * inner), edge.reshape(GROUP * wide, GROUP * inner)], axis=1
        )
        eye = jnp.eye(GROUP, dtype=jnp.float32)
        side = math.isqrt(spatial.shape[0])
        blocks = jnp.einsum("rq,koi->kriqo", eye, spatial, precision="highest")
        self.fast_spatial = blocks.reshape(side, side, GROUP * inner, GROUP * inner)
        self.fast_expand = jnp.einsum("rq,oi->riqo", eye, expand, precision="highest").reshape(
            GROUP * inner, GROUP * wide
        )
        self.lateral_here = lateral[2:5]
        self.lateral_next = lateral[0:2]
        self.joined = jnp.concatenate(
            [slow_reduce.reshape(-1, slow_reduce.shape[2]), shortcut], axis=0
        )
        self.slow_spatial = jnp.swapaxes(slow_spatial, 1, 2).reshape(
            side, side, slow_spatial.shape[2], slow_spatial.shape[1]
        )
        self.slow_expand = slow_expand
        self.depth = slow_reduce.shape[1]
        widths = [
            inner,
            inner,
            wide,
            lateral.shape[1],
            slow_reduce.shape[1],
            slow_spatial.shape[1],
            slow_expand.shape[0],
            shortcut.shape[0],
        ]
        self.norms, cursor = [], 0
        for width in widths:
            self.norms.append(Norm(gain[cursor : cursor + width], bias[cursor : cursor + width]))
            cursor += width


class Block:
    def __init__(self, section, mask, frames):
        self.s, self.mask, self.frames = section, mask, frames
        self.grads = {}

    def fast_forward(self, fast_in, shared):
        s, mask, frames, norms = self.s, self.mask, self.frames, self.s.norms
        self.fast_in = fast_in
        width = GROUP * s.inner
        both = dot_nn(fast_in, s.fast_reduce)
        here, edge = both[:, :width], both[:, width:]
        lane = lax.broadcasted_iota(jnp.int32, (1, width), 1)
        before = later(edge, from_previous(last_frame(edge, frames)), frames)
        after = earlier(edge, from_next(first_frame(edge, frames)), frames)
        first = here + jnp.where(
            lane < s.inner, before, jnp.where(lane >= width - s.inner, after, 0.0)
        )
        totals = yield norms[0].sums(first, mask)
        norms[0].learn(first, totals, 4.0 * shared["count"])
        self.first_act = silu(norms[0].apply(mask))
        second = conv_grid(self.first_act, s.fast_spatial, frames)
        totals = yield norms[1].sums(second, mask)
        norms[1].learn(second, totals, 4.0 * shared["count"])
        self.second_act = silu(norms[1].apply(mask))
        third = dot_nn(self.second_act, s.fast_expand)
        totals = yield norms[2].sums(third, mask)
        norms[2].learn(third, totals, 4.0 * shared["count"])
        self.fast_pre = norms[2].apply(mask) + fast_in
        self.fast_out = silu(self.fast_pre)
        wide = s.wide
        parts = [self.fast_out[:, r * wide : (r + 1) * wide] for r in range(GROUP)]
        here = dot_nt(parts[0], s.lateral_here[0])
        here += dot_nt(parts[1], s.lateral_here[1])
        here += dot_nt(parts[2], s.lateral_here[2])
        onward = dot_nt(parts[2], s.lateral_next[0]) + dot_nt(parts[3], s.lateral_next[1])
        lateral = here + later(onward, from_previous(last_frame(onward, frames)), frames)
        totals = yield norms[3].sums(lateral, mask)
        norms[3].learn(lateral, totals, shared["count"])
        self.lateral_act = silu(norms[3].apply(mask))

    def slow_forward(self, slow_in, shared):
        s, mask, frames, norms = self.s, self.mask, self.frames, self.s.norms
        self.joined = jnp.concatenate([slow_in, self.lateral_act], axis=1)
        depth = s.depth
        reduced = dot_nt(self.joined, s.joined[: 3 * depth])
        skipped = dot_nt(self.joined, s.joined[3 * depth :])
        low, mid, high = reduced[:, :depth], reduced[:, depth : 2 * depth], reduced[:, 2 * depth :]
        inner = (
            mid
            + later(low, from_previous(last_frame(low, frames)), frames)
            + earlier(high, from_next(first_frame(high, frames)), frames)
        )
        sums = [norms[4].sums(inner, mask), norms[7].sums(skipped, mask)]
        totals = yield jnp.concatenate(sums)
        norms[4].learn(inner, totals[: 2 * depth], shared["count"])
        norms[7].learn(skipped, totals[2 * depth :], shared["count"])
        self.inner_act = silu(norms[4].apply(mask))
        middle = conv_grid(self.inner_act, s.slow_spatial, frames)
        totals = yield norms[5].sums(middle, mask)
        norms[5].learn(middle, totals, shared["count"])
        self.middle_act = silu(norms[5].apply(mask))
        expanded = dot_nt(self.middle_act, s.slow_expand)
        totals = yield norms[6].sums(expanded, mask)
        norms[6].learn(expanded, totals, shared["count"])
        self.slow_pre = norms[6].apply(mask) + norms[7].apply(mask)
        self.slow_out = silu(self.slow_pre)

    def slow_backward(self, slow_grad):
        s, mask, frames, norms = self.s, self.mask, self.frames, self.s.norms
        depth = s.depth
        pre = mask * slow_grad * silu_slope(self.slow_pre)
        wide = pre.shape[1]
        totals = yield jnp.concatenate(
            [norms[6].back_sums(pre), jnp.sum(pre * norms[7].normed(), axis=0)]
        )
        expand_grad = norms[6].back(pre, totals[: 2 * wide], mask)
        skip_grad = norms[7].back(
            pre, jnp.concatenate([totals[:wide], totals[2 * wide :]]), mask
        )
        middle_act_grad = dot_nn(expand_grad, s.slow_expand)
        self.grads["slow_expand"] = dot_tn(expand_grad, self.middle_act)
        pre = mask * middle_act_grad * silu_slope(norms[5].apply(mask))
        totals = yield norms[5].back_sums(pre)
        middle_grad = norms[5].back(pre, totals, mask)
        inner_act_grad, kernel_grad = conv_grid_back(
            self.inner_act, s.slow_spatial, middle_grad, frames
        )
        self.grads["slow_spatial"] = jnp.swapaxes(
            kernel_grad.reshape((-1,) + kernel_grad.shape[2:]), 1, 2
        )
        pre = mask * inner_act_grad * silu_slope(norms[4].apply(mask))
        totals = yield norms[4].back_sums(pre)
        inner_grad = norms[4].back(pre, totals, mask)
        low = earlier(inner_grad, from_next(first_frame(inner_grad, frames)), frames)
        high = later(inner_grad, from_previous(last_frame(inner_grad, frames)), frames)
        reduced_grad = jnp.concatenate([low, inner_grad, high], axis=1)
        joined_grad = dot_nn(reduced_grad, s.joined[: 3 * depth]) + dot_nn(
            skip_grad, s.joined[3 * depth :]
        )
        self.grads["slow_reduce"] = dot_tn(reduced_grad, self.joined)
        self.grads["shortcut"] = dot_tn(skip_grad, self.joined)
        self.slow_in_grad = mask * joined_grad[:, :wide]
        self.lateral_act_grad = joined_grad[:, wide:]

    def fast_backward(self, fast_grad):
        s, mask, frames, norms = self.s, self.mask, self.frames, self.s.norms
        wide = s.wide
        pre = mask * self.lateral_act_grad * silu_slope(norms[3].apply(mask))
        totals = yield norms[3].back_sums(pre)
        here = norms[3].back(pre, totals, mask)
        onward = earlier(here, from_next(first_frame(here, frames)), frames)
        parts = [
            dot_nn(here, s.lateral_here[0]),
            dot_nn(here, s.lateral_here[1]),
            dot_nn(here, s.lateral_here[2]) + dot_nn(onward, s.lateral_next[0]),
            dot_nn(onward, s.lateral_next[1]),
        ]
        outs = [self.fast_out[:, r * wide : (r + 1) * wide] for r in range(GROUP)]
        self.grads["lateral"] = jnp.stack(
            [
                dot_tn(onward, outs[2]),
                dot_tn(onward, outs[3]),
                dot_tn(here, outs[0]),
                dot_tn(here, outs[1]),
                dot_tn(here, outs[2]),
            ]
        )
        out_grad = fast_grad() + jnp.concatenate(parts, axis=1)
        fast_pre_grad = mask * out_grad * silu_slope(self.fast_pre)
        totals = yield norms[2].back_sums(fast_pre_grad)
        third_grad = norms[2].back(fast_pre_grad, totals, mask)
        second_act_grad = dot_nt(third_grad, s.fast_expand)
        inner = s.inner
        grid = dot_tn(third_grad, self.second_act).reshape(GROUP, wide, GROUP, inner)
        self.grads["fast_expand"] = sum(grid[r, :, r] for r in range(GROUP))
        pre = mask * second_act_grad * silu_slope(norms[1].apply(mask))
        totals = yield norms[1].back_sums(pre)
        second_grad = norms[1].back(pre, totals, mask)
        first_act_grad, kernel_grad = conv_grid_back(
            self.first_act, s.fast_spatial, second_grad, frames
        )
        grid = kernel_grad.reshape(-1, GROUP, inner, GROUP, inner)
        self.grads["fast_spatial"] = jnp.swapaxes(
            sum(grid[:, r, :, r] for r in range(GROUP)), 1, 2
        )
        pre = mask * first_act_grad * silu_slope(norms[0].apply(mask))
        totals = yield norms[0].back_sums(pre)
        first_grad = norms[0].back(pre, totals, mask)
        width = GROUP * inner
        lane = lax.broadcasted_iota(jnp.int32, (1, width), 1)
        after = earlier(first_grad, from_next(first_frame(first_grad, frames)), frames)
        before = later(first_grad, from_previous(last_frame(first_grad, frames)), frames)
        edge = jnp.where(lane < inner, after, jnp.where(lane >= width - inner, before, 0.0))
        both = jnp.concatenate([first_grad, edge], axis=1)
        self.fast_in_grad = mask * (dot_nt(both, s.fast_reduce) + fast_pre_grad)
        grid = dot_tn(both, self.fast_in).reshape(2, GROUP, inner, GROUP, wide)
        near, far = grid[0], grid[1]
        self.grads["fast_reduce"] = jnp.stack(
            [
                near[1, :, 0] + near[2, :, 1] + near[3, :, 2] + far[0, :, 3],
                near[0, :, 0] + near[1, :, 1] + near[2, :, 2] + near[3, :, 3],
                near[0, :, 1] + near[1, :, 2] + near[2, :, 3] + far[3, :, 0],
            ]
        )


class Task:
    def __init__(self, steps):
        self.steps, self.done = steps, False
        self.wanted = next(steps)

    def resume(self, totals):
        try:
            self.wanted = self.steps.send(totals)
        except StopIteration:
            self.done = True


def advance(*tasks, extra=None):
    wanted = [task.wanted for task in tasks]
    if extra is not None:
        wanted.append(extra)
    totals = sum_everywhere(jnp.concatenate(wanted))
    pieces, cursor = [], 0
    for part in wanted:
        pieces.append(totals[cursor : cursor + part.shape[0]])
        cursor += part.shape[0]
    return pieces


def rows_of(values, own):
    picked = lax.dynamic_index_in_dim(values, own, 0, keepdims=False)[0]
    return jnp.transpose(picked, (2, 0, 1))


def body(
    slow_input,
    fast_input,
    frame_counts,
    fast_reduce,
    fast_spatial,
    fast_expand,
    lateral_conv,
    slow_reduce,
    slow_spatial,
    slow_expand,
    shortcut,
    norm_gain,
    norm_bias,
    slow_cotangent,
    fast_cotangent,
):
    own = lax.axis_index("section")
    lower = own == 0
    frames, positions = slow_input.shape[2], slow_input.shape[4]
    rows = frames * positions
    wide = fast_input.shape[3]

    def slow_rows(values):
        return rows_of(values, own).reshape(rows, -1)

    def fast_rows(values):
        return rows_of(values, own).reshape(rows, GROUP * wide)

    mine = [
        fast_reduce[0],
        fast_spatial[0],
        fast_expand[0],
        lateral_conv[0],
        slow_reduce[0],
        slow_spatial[0],
        slow_expand[0],
        shortcut[0],
        norm_gain[0],
        norm_bias[0],
    ]
    small = [0, 1, 2, 8, 9]
    packed = swap(jnp.concatenate([mine[i].reshape(-1) for i in small]))
    other, cursor = [None] * len(mine), 0
    for i in small:
        other[i] = packed[cursor : cursor + mine[i].size].reshape(mine[i].shape)
        cursor += mine[i].size
    for i in (3, 4, 7, 5, 6):
        other[i] = swap(mine[i])
    sections = []
    for index in range(2):
        both = [jnp.where(own == index, a, b) for a, b in zip(mine, other)]
        sections.append(Section(both[:8], both[8], both[9]))

    count_here = lax.dynamic_index_in_dim(frame_counts, own, 0, keepdims=False)
    frame = lax.axis_index("clip") * frames + lax.broadcasted_iota(jnp.int32, (positions, frames), 1)
    mask = (frame < count_here).astype(jnp.float32).reshape(rows, 1)
    blocks = [Block(section, mask, frames) for section in sections]
    shared = {}

    fast = [Task(blocks[0].fast_forward(mask * fast_rows(fast_input), shared)), None]
    got = advance(fast[0], extra=jnp.sum(mask, axis=0))
    shared["count"] = got[1][0]
    fast[0].resume(got[0])
    for step in range(2):
        fast[0].resume(advance(fast[0])[0])
    fast[1] = Task(blocks[1].fast_forward(blocks[0].fast_out, shared))
    got = advance(fast[0], fast[1])
    fast[0].resume(got[0])
    fast[1].resume(got[1])
    slow = [Task(blocks[0].slow_forward(mask * slow_rows(slow_input), shared)), None]
    for step in range(3):
        got = advance(slow[0], fast[1])
        slow[0].resume(got[0])
        fast[1].resume(got[1])
    slow[1] = Task(blocks[1].slow_forward(blocks[0].slow_out, shared))
    for step in range(3):
        slow[1].resume(advance(slow[1])[0])

    tasks = Task(blocks[1].slow_backward(slow_rows(slow_cotangent)))
    for step in range(3):
        tasks.resume(advance(tasks)[0])
    late = Task(blocks[1].fast_backward(lambda: fast_rows(fast_cotangent)))
    soon = Task(blocks[0].slow_backward(blocks[1].slow_in_grad))
    for step in range(3):
        got = advance(late, soon)
        late.resume(got[0])
        soon.resume(got[1])
    last = Task(blocks[0].fast_backward(lambda: blocks[1].fast_in_grad))
    got = advance(late, last)
    late.resume(got[0])
    last.resume(got[1])
    for step in range(3):
        last.resume(advance(last)[0])

    def assembled(first, second, channels, native):
        to_zero = lax.ppermute(first, "section", [(1, 0)])
        to_one = lax.ppermute(second, "section", [(0, 1)])
        pair = jnp.stack([jnp.where(lower, first, to_one), jnp.where(lower, to_zero, second)])
        grid = pair.reshape(2, positions, native, channels)
        return jnp.transpose(grid, (0, 2, 3, 1))[None, :, None]

    zero, one = blocks
    slow_wide = slow_input.shape[3]
    names = (
        "fast_reduce",
        "fast_spatial",
        "fast_expand",
        "lateral",
        "slow_reduce",
        "slow_spatial",
        "slow_expand",
        "shortcut",
    )
    norm_grads = []
    for block in blocks:
        norm_grads.append(
            jnp.stack(
                [
                    jnp.concatenate([norm.gain_grad for norm in block.s.norms]),
                    jnp.concatenate([norm.bias_grad for norm in block.s.norms]),
                ]
            )
        )
    kept = jnp.where(lower, norm_grads[0], norm_grads[1])
    kept = kept + swap(jnp.where(lower, norm_grads[1], norm_grads[0]))
    sent = [jnp.where(lower, one.grads[n], zero.grads[n]) for n in names]
    held = [jnp.where(lower, zero.grads[n], one.grads[n]) for n in names]
    partial = [h + swap(x) for h, x in zip(held, sent)]
    totals = lax.psum(tuple(partial), AXES)
    shapes = [w.shape for w in mine[:8]]
    totals = [t.reshape((1,) + s) for t, s in zip(totals, shapes)]
    return (
        assembled(zero.slow_out, one.slow_out, slow_wide, frames),
        assembled(zero.fast_out, one.fast_out, wide, GROUP * frames),
        assembled(zero.slow_in_grad, one.slow_in_grad, slow_wide, frames),
        assembled(zero.fast_in_grad, one.fast_in_grad, wide, GROUP * frames),
        *totals,
        kept[None, 0],
        kept[None, 1],
    )


def solution(mesh):
    acts = P(None, "tm", "clip", None, None)
    outs = P("section", None, "tm", "clip", None, None)
    four, three, two = P("section", None, None, None), P("section", None, None), P("section", None)
    weights = (four, four, three, four, four, four, three, three)
    return jax.shard_map(
        body,
        mesh=mesh,
        in_specs=(acts, acts, P(None, "tm"), *weights, two, two, acts, acts),
        out_specs=(outs, outs, outs, outs, *weights, two, two),
        check_vma=False,
    )
```

```python
from functools import partial
import math

import jax
import jax.numpy as jnp
from jax import lax
from jax.experimental import pallas as pl
from jax.experimental.pallas import tpu as pltpu
from jax.sharding import PartitionSpec as P

EPSILON = 1e-05
FINE = lax.Precision.HIGH
GROUP = 4
AXES = ("clip", "tm")


def dot_nn(a, b):
    return lax.dot_general(a, b, (((1,), (0,)), ((), ())), precision=FINE)


def dot_nt(a, b):
    return lax.dot_general(a, b, (((1,), (1,)), ((), ())), precision=FINE)


def dot_tn(a, b):
    return lax.dot_general(a, b, (((0,), (0,)), ((), ())), precision=FINE)


def sums_everywhere(vector):
    count = lax.axis_size("clip") * lax.axis_size("tm")
    copies = jnp.broadcast_to(vector, (count, vector.shape[1]))
    return lax.all_to_all(copies, AXES, 0, 0)


def from_previous(edge):
    count = lax.axis_size("clip")
    return lax.ppermute(edge, "clip", [(i, i + 1) for i in range(count - 1)])


def from_next(edge):
    count = lax.axis_size("clip")
    return lax.ppermute(edge, "clip", [(i + 1, i) for i in range(count - 1)])


def swap(values):
    return lax.ppermute(values, "section", [(0, 1), (1, 0)])


def silu(v):
    return v * jax.nn.sigmoid(v)


def silu_slope(v):
    s = jax.nn.sigmoid(v)
    return s * (1.0 + v * (1.0 - s))


VMEM_BYTES = 56 * 2**20


def rowwise(mask, width):
    return jnp.concatenate([mask] * (width // mask.shape[1]), axis=1)


def moments(r_ref, offset, width, count, fold=0):
    total = jnp.sum(r_ref[:, offset : offset + width], axis=0, keepdims=True)
    square = jnp.sum(r_ref[:, offset + width : offset + 2 * width], axis=0, keepdims=True)
    if fold:
        total, square = around(total, fold), around(square, fold)
    mean = total / count
    return mean, lax.rsqrt(square / count - mean * mean + EPSILON)


def around(row, fold):
    out = row
    for step in range(fold, row.shape[1], fold):
        out = out + pltpu.roll(row, step, 1)
    return out


def repeat(row, times):
    return row if times == 1 else jnp.concatenate([row] * times, axis=1)


def store_sums(st_ref, values, mask, fold=1):
    weighted = values * mask
    total = jnp.sum(weighted, axis=0, keepdims=True)
    square = jnp.sum(weighted * values, axis=0, keepdims=True)
    width = total.shape[1] // fold
    st_ref[:, :width] = sum(total[:, k * width : (k + 1) * width] for k in range(fold))
    st_ref[:, width:] = sum(square[:, k * width : (k + 1) * width] for k in range(fold))


class Stacked:
    def __init__(self, both, index):
        self.both, self.index, self.shape = both, index, both.shape[1:]

    def block(self, shape, place):
        def where(*step):
            return (self.index,) + place(*step)

        return pl.BlockSpec((None,) + shape, where)

    def whole(self):
        zeros = (0,) * len(self.shape)
        return self.block(self.shape, lambda *step: zeros)


def array_of(value):
    return value.both if isinstance(value, Stacked) else value


def call(kernel, outs, ins, scratch=(), **static):
    vmem = pl.BlockSpec(memory_space=pltpu.VMEM)
    return pl.pallas_call(
        partial(kernel, **static),
        grid=(1,),
        out_shape=[jax.ShapeDtypeStruct(s, jnp.float32) for s in outs],
        in_specs=[x.whole() if isinstance(x, Stacked) else vmem for x in ins],
        out_specs=[vmem] * len(outs),
        scratch_shapes=[pltpu.VMEM(s, jnp.float32) for s in scratch],
        compiler_params=pltpu.CompilerParams(vmem_limit_bytes=VMEM_BYTES),
    )(*[array_of(x) for x in ins])


def fixed(shape):
    return pl.BlockSpec(shape, lambda j: (0,) * len(shape))


def columns(rows, width):
    return pl.BlockSpec((rows, width), lambda j: (0, j))


def bands(height, width):
    return pl.BlockSpec((height, width), lambda j: (j, 0))


def call_steps(kernel, steps, outs, out_specs, ins, in_specs, scratch=(), **static):
    return pl.pallas_call(
        partial(kernel, **static),
        grid=(steps,),
        out_shape=[jax.ShapeDtypeStruct(s, jnp.float32) for s in outs],
        in_specs=in_specs,
        out_specs=out_specs,
        scratch_shapes=[pltpu.VMEM(s, jnp.float32) for s in scratch],
        compiler_params=pltpu.CompilerParams(
            dimension_semantics=("arbitrary",), vmem_limit_bytes=VMEM_BYTES
        ),
    )(*[array_of(x) for x in ins])


def take_rows(out_ref, values, first, frames, scratch):
    for k in range(out_ref.shape[1] // 128):
        scratch[k] = values[:, k * 128 : (k + 1) * 128]
        out_ref[:, k * 128 : (k + 1) * 128] = scratch[k, pl.ds(first, out_ref.shape[0], stride=frames), :]


def put_rows(values, first, frames, edge, scratch):
    pieces = []
    for k in range(edge.shape[1] // 128):
        scratch[k] = values[:, k * 128 : (k + 1) * 128]
        scratch[k, pl.ds(first, edge.shape[0], stride=frames), :] = edge[:, k * 128 : (k + 1) * 128]
        pieces.append(scratch[k])
    return jnp.concatenate(pieces, axis=1) if len(pieces) > 1 else pieces[0]


def before_rows(scratch, values, edge, frames):
    return put_rows(pltpu.roll(values, 1, 0), 0, frames, edge, scratch)


def after_rows(scratch, values, edge, frames):
    return put_rows(pltpu.roll(values, values.shape[0] - 1, 0), frames - 1, frames, edge, scratch)


def banded(w_ref, matrix):
    taps, inner, wide = w_ref.shape
    matrix[...] = jnp.zeros(matrix.shape, jnp.float32)
    for q in range(GROUP):
        for k in range(taps):
            r = q + k - 1
            start = q * inner + (0 if 0 <= r < GROUP else GROUP * inner)
            r = r % GROUP
            matrix[start : start + inner, r * wide : (r + 1) * wide] = w_ref[k]
    return matrix[...]


def fast_first_kernel(
    own_ref, x_ref, m_ref, w_ref, x_out, y_ref, low_ref, high_ref, scratch, matrix, *, frames
):
    rows, wide = m_ref.shape[0], x_ref.shape[1]
    for r in range(GROUP):
        x_out[:, r * wide : (r + 1) * wide] = (
            x_ref[pl.ds(r, rows, stride=GROUP), :] * rowwise(m_ref[...], wide)
        )
    y = dot_nt(x_out[...], banded(w_ref, matrix))
    y_ref[...] = y
    take_rows(low_ref, y[:, y.shape[1] // 2 :], 0, frames, scratch)
    take_rows(high_ref, y[:, y.shape[1] // 2 :], frames - 1, frames, scratch)


def fast_join_kernel(y_ref, p_ref, n_ref, m_ref, o_ref, st_ref, sp_ref, sn_ref, *, frames, inner):
    width = o_ref.shape[1]
    edge = y_ref[:, width:]
    before = before_rows(sp_ref, edge, p_ref[...], frames)
    after = after_rows(sn_ref, edge, n_ref[...], frames)
    lane = lax.broadcasted_iota(jnp.int32, (1, width), 1)
    out = y_ref[:, :width] + jnp.where(
        lane < inner, before, jnp.where(lane >= width - inner, after, 0.0)
    )
    o_ref[...] = out
    store_sums(st_ref, out, m_ref[...])


def fill_shifts(values, x0, xl, xr, side, frames):
    rows, width = values.shape
    pad = (x0.shape[0] - rows) // 2
    blank = jnp.zeros((pad + 8, width), jnp.float32)
    for ref in (x0, xl, xr):
        ref[0 : pad + 8] = blank
        ref[pad + rows - 8 : 2 * pad + rows] = blank
    row = lax.broadcasted_iota(jnp.int32, (rows, 1), 0)
    column = lax.rem(lax.div(row, frames), side)
    x0[pad : pad + rows] = values
    xl[pad + frames : pad + frames + rows] = jnp.where(column == side - 1, 0.0, values)
    xr[pad - frames : pad - frames + rows] = jnp.where(column == 0, 0.0, values)


def shifted(k, x0, xl, xr, rows, side, frames):
    pad = (x0.shape[0] - rows) // 2
    start = pad + (k // 3 - 1) * side * frames
    return (xl, x0, xr)[k % 3][start : start + rows]


def conv_kernel(
    v_ref, r_ref, c_ref, g_ref, b_ref, m_ref, k_ref, o_ref, act_ref, st_ref, x0, xl, xr,
    *, offset, fold, side, frames
):
    rows, width = v_ref.shape
    mean, rstd = moments(r_ref, offset, width, c_ref[...], fold)
    mask = rowwise(m_ref[...], width)
    act = mask * silu(g_ref[...] * ((v_ref[...] - mean) * rstd) + b_ref[...])
    act_ref[...] = act
    fill_shifts(act, x0, xl, xr, side, frames)
    total = dot_nt(shifted(0, x0, xl, xr, rows, side, frames), k_ref[0])
    for k in range(1, k_ref.shape[0]):
        total += dot_nt(shifted(k, x0, xl, xr, rows, side, frames), k_ref[k])
    o_ref[...] = total
    store_sums(st_ref, total, rowwise(m_ref[...], total.shape[1]))


def fast_expand_kernel(
    v_ref, r_ref, c_ref, g_ref, b_ref, m_ref, w_ref, o_ref, act_ref, st_ref, *, offset, fold
):
    width = v_ref.shape[1]
    mean, rstd = moments(r_ref, offset, width, c_ref[...], fold)
    act = rowwise(m_ref[...], width) * silu(g_ref[...] * ((v_ref[...] - mean) * rstd) + b_ref[...])
    act_ref[...] = act
    out = dot_nn(act, w_ref[...])
    o_ref[...] = out
    store_sums(st_ref, out, rowwise(m_ref[...], out.shape[1]), GROUP)


def fast_out_kernel(
    v_ref, x_ref, r_ref, c_ref, g_ref, b_ref, m_ref, l_ref, w_ref,
    out_ref, here_ref, next_ref, edge_ref, y_ref, low_ref, high_ref, scratch, matrix, *, offset, frames, more
):
    width = v_ref.shape[1]
    wide = width // GROUP
    mean, rstd = moments(r_ref, offset, wide, c_ref[...])
    mean, rstd = repeat(mean, GROUP), repeat(rstd, GROUP)
    pre = g_ref[...] * ((v_ref[...] - mean) * rstd) + b_ref[...] + x_ref[...]
    out = rowwise(m_ref[...], width) * silu(pre)
    out_ref[...] = out
    one, two, three, four = [out[:, r * wide : (r + 1) * wide] for r in range(GROUP)]
    here_ref[...] = dot_nt(one, l_ref[2]) + dot_nt(two, l_ref[3]) + dot_nt(three, l_ref[4])
    onward = dot_nt(three, l_ref[0]) + dot_nt(four, l_ref[1])
    next_ref[...] = onward
    take_rows(edge_ref, onward, frames - 1, frames, scratch)
    if more:
        y = dot_nt(out, banded(w_ref, matrix))
        y_ref[...] = y
        half = y.shape[1] // 2
        take_rows(low_ref, y[:, half:], 0, frames, scratch)
        take_rows(high_ref, y[:, half:], frames - 1, frames, scratch)
    else:
        for ref in (y_ref, low_ref, high_ref):
            ref[...] = jnp.zeros(ref.shape, jnp.float32)


def lateral_join_kernel(h_ref, n_ref, e_ref, m_ref, o_ref, st_ref, sp_ref, *, frames):
    out = h_ref[...] + before_rows(sp_ref, n_ref[...], e_ref[...], frames)
    o_ref[...] = out
    store_sums(st_ref, out, rowwise(m_ref[...], out.shape[1]))


def reduce_kernel(
    x_ref, v_ref, r_ref, c_ref, g_ref, b_ref, m_ref, w_ref, y_ref, low_ref, high_ref, act_ref, joined,
    scratch, *, offset, frames
):
    step = pl.program_id(0)
    wide, lateral = x_ref.shape[1], v_ref.shape[1]

    @pl.when(step == 0)
    def _():
        mean, rstd = moments(r_ref, offset, lateral, c_ref[...])
        joined[:, :wide] = x_ref[...]
        act = silu(g_ref[...] * ((v_ref[...] - mean) * rstd) + b_ref[...])
        act = act * rowwise(m_ref[...], lateral)
        joined[:, wide:] = act
        act_ref[...] = act

    y = dot_nt(joined[...], w_ref[...])
    y_ref[...] = y

    @pl.when(step == 0)
    def _():
        take_rows(high_ref, y, frames - 1, frames, scratch)

    @pl.when(step == 2)
    def _():
        take_rows(low_ref, y, 0, frames, scratch)


def shortcut_kernel(x_ref, a_ref, m_ref, w_ref, y_ref, s_ref, q_ref):
    wide = x_ref.shape[1]
    out = dot_nt(x_ref[...], w_ref[:, :wide])
    out += dot_nt(a_ref[...], w_ref[:, wide:])
    y_ref[...] = out
    weighted = out * rowwise(m_ref[...], out.shape[1])
    s_ref[...] = jnp.sum(weighted, axis=0, keepdims=True)
    q_ref[...] = jnp.sum(weighted * out, axis=0, keepdims=True)


def inner_join_kernel(y_ref, p_ref, n_ref, m_ref, o_ref, st_ref, sp_ref, sn_ref, *, frames):
    depth = o_ref.shape[1]
    out = y_ref[:, depth : 2 * depth]
    out += before_rows(sp_ref, y_ref[:, :depth], p_ref[...], frames)
    out += after_rows(sn_ref, y_ref[:, 2 * depth : 3 * depth], n_ref[...], frames)
    o_ref[...] = out
    store_sums(st_ref, out, rowwise(m_ref[...], depth))


def expand_kernel(
    v_ref, r_ref, c_ref, g_ref, b_ref, m_ref, w_ref, o_ref, act_ref, s_ref, q_ref, *, offset
):
    width = v_ref.shape[1]

    @pl.when(pl.program_id(0) == 0)
    def _():
        mean, rstd = moments(r_ref, offset, width, c_ref[...])
        act = silu(g_ref[...] * ((v_ref[...] - mean) * rstd) + b_ref[...])
        act_ref[...] = act * rowwise(m_ref[...], width)

    out = dot_nt(act_ref[...], w_ref[...])
    o_ref[...] = out
    weighted = out * rowwise(m_ref[...], out.shape[1])
    s_ref[...] = jnp.sum(weighted, axis=0, keepdims=True)
    q_ref[...] = jnp.sum(weighted * out, axis=0, keepdims=True)


def slow_out_kernel(
    e_ref, k_ref, r6_ref, r7_ref, c_ref, g6_ref, b6_ref, g7_ref, b7_ref, m_ref, o_ref,
    *, offset6, offset7, total
):
    pre, _, _ = slow_pre(
        e_ref, k_ref, r6_ref, r7_ref, c_ref, g6_ref, b6_ref, g7_ref, b7_ref, offset6, offset7, total
    )
    o_ref[...] = rowwise(m_ref[...], pre.shape[1]) * silu(pre)


def part(r_ref, offset, width):
    start = pl.multiple_of(offset + pl.program_id(0) * width, 128)
    return jnp.sum(r_ref[:, pl.ds(start, width)], axis=0, keepdims=True)


def moments_part(r_ref, offset, total, width, count):
    mean = part(r_ref, offset, width) / count
    square = part(r_ref, offset + total, width) / count
    return mean, lax.rsqrt(square - mean * mean + EPSILON)


def slow_pre(
    e_ref, k_ref, r6_ref, r7_ref, c_ref, g6_ref, b6_ref, g7_ref, b7_ref, offset6, offset7, total
):
    width = e_ref.shape[1]
    mean6, rstd6 = moments_part(r6_ref, offset6, total, width, c_ref[...])
    mean7, rstd7 = moments_part(r7_ref, offset7, total, width, c_ref[...])
    n6 = (e_ref[...] - mean6) * rstd6
    n7 = (k_ref[...] - mean7) * rstd7
    pre = (g6_ref[...] * n6 + b6_ref[...]) + (g7_ref[...] * n7 + b7_ref[...])
    return pre, (n6, rstd6), (n7, rstd7)


def slow_slope_kernel(
    d_ref, e_ref, k_ref, r6_ref, r7_ref, c_ref, g6_ref, b6_ref, g7_ref, b7_ref, m_ref,
    p_ref, s_ref, q6_ref, q7_ref, *, offset6, offset7, total
):
    pre, (n6, _), (n7, _) = slow_pre(
        e_ref, k_ref, r6_ref, r7_ref, c_ref, g6_ref, b6_ref, g7_ref, b7_ref, offset6, offset7, total
    )
    grad = rowwise(m_ref[...], pre.shape[1]) * d_ref[...] * silu_slope(pre)
    p_ref[...] = grad
    s_ref[...] = jnp.sum(grad, axis=0, keepdims=True)
    q6_ref[...] = jnp.sum(grad * n6, axis=0, keepdims=True)
    q7_ref[...] = jnp.sum(grad * n7, axis=0, keepdims=True)


def expand_back_kernel(
    p_ref, e_ref, k_ref, r6_ref, r7_ref, rb_ref, c_ref, g6_ref, g7_ref, m_ref, w_ref, act_ref,
    v_ref, r5_ref, g5_ref, b5_ref,
    skip_ref, dw_ref, o_ref, st_ref, acc, *, offset6, offset7, offsetb, offset5, total
):
    step, steps = pl.program_id(0), pl.num_programs(0)
    width, depth = p_ref.shape[1], v_ref.shape[1]
    count, mask = c_ref[...], rowwise(m_ref[...], width)
    mean6, rstd6 = moments_part(r6_ref, offset6, total, width, count)
    mean7, rstd7 = moments_part(r7_ref, offset7, total, width, count)
    low = part(rb_ref, offsetb, width) / count
    q6 = part(rb_ref, offsetb + total, width) / count
    q7 = part(rb_ref, offsetb + 2 * total, width) / count
    pre = p_ref[...]
    grad = mask * ((g6_ref[...] * rstd6) * (pre - low - (e_ref[...] - mean6) * rstd6 * q6))
    skip_ref[...] = mask * ((g7_ref[...] * rstd7) * (pre - low - (k_ref[...] - mean7) * rstd7 * q7))
    dw_ref[...] = dot_tn(grad, act_ref[...])
    product = dot_nn(grad, w_ref[...])

    @pl.when(step == 0)
    def _():
        acc[...] = product

    @pl.when(step > 0)
    def _():
        acc[...] += product

    @pl.when(step == steps - 1)
    def _():
        mean, rstd = moments(r5_ref, offset5, depth, count)
        normed = (v_ref[...] - mean) * rstd
        out = rowwise(m_ref[...], depth) * acc[...]
        out = out * silu_slope(g5_ref[...] * normed + b5_ref[...])
        o_ref[...] = out
        st_ref[:, :depth] = jnp.sum(out, axis=0, keepdims=True)
        st_ref[:, depth:] = jnp.sum(out * normed, axis=0, keepdims=True)


def store_weight(dw_ref, grad, x_ref, a_ref):
    count, _, width = dw_ref.shape
    for k in range(count - 1):
        dw_ref[k] = dot_tn(grad, x_ref[:, k * width : (k + 1) * width])
    dw_ref[count - 1] = dot_tn(grad, a_ref[...])


def shortcut_back_kernel(d_ref, w_ref, x_ref, a_ref, dw_ref, o_ref):
    step = pl.program_id(0)
    grad = d_ref[...]
    store_weight(dw_ref, grad, x_ref, a_ref)

    @pl.when(step == 0)
    def _():
        o_ref[...] = dot_nn(grad, w_ref[...])

    @pl.when(step > 0)
    def _():
        o_ref[...] += dot_nn(grad, w_ref[...])


def back_sums(rb_ref, offset, width, count, fold=0):
    low = jnp.sum(rb_ref[:, offset : offset + width], axis=0, keepdims=True)
    slope = jnp.sum(rb_ref[:, offset + width : offset + 2 * width], axis=0, keepdims=True)
    if fold:
        low, slope = around(low, fold), around(slope, fold)
    return low / count, slope / count


def norm_back(pre, values, mean, rstd, gain, low, slope, mask):
    return mask * ((gain * rstd) * (pre - low - (values - mean) * rstd * slope))


def store_back_sums(st_ref, grad, normed, fold=1):
    low = jnp.sum(grad, axis=0, keepdims=True)
    slope = jnp.sum(grad * normed, axis=0, keepdims=True)
    width = low.shape[1] // fold
    st_ref[:, :width] = sum(low[:, k * width : (k + 1) * width] for k in range(fold))
    st_ref[:, width:] = sum(slope[:, k * width : (k + 1) * width] for k in range(fold))


def conv_back_kernel(
    p_ref, v_ref, r_ref, rb_ref, c_ref, g_ref, u_ref, ru_ref, gu_ref, bu_ref, m_ref, k_ref,
    d_ref, o_ref, st_ref, x0, xl, xr, *, offset, offsetb, offsetu, fold, side, frames
):
    rows, width = v_ref.shape
    count, mask = c_ref[...], rowwise(m_ref[...], width)
    mean, rstd = moments(r_ref, offset, width, count, fold)
    low, slope = back_sums(rb_ref, offsetb, width, count, fold)
    grad = norm_back(p_ref[...], v_ref[...], mean, rstd, g_ref[...], low, slope, mask)
    d_ref[...] = grad
    fill_shifts(grad, x0, xl, xr, side, frames)
    last = k_ref.shape[0] - 1
    total = dot_nn(shifted(0, x0, xl, xr, rows, side, frames), k_ref[last])
    for k in range(1, last + 1):
        total += dot_nn(shifted(k, x0, xl, xr, rows, side, frames), k_ref[last - k])
    mean, rstd = moments(ru_ref, offsetu, u_ref.shape[1], count, fold)
    normed = (u_ref[...] - mean) * rstd
    out = rowwise(m_ref[...], u_ref.shape[1]) * total
    out = out * silu_slope(gu_ref[...] * normed + bu_ref[...])
    o_ref[...] = out
    store_back_sums(st_ref, out, normed)


def conv_weight_kernel(x_ref, d_ref, dw_ref, x0, xl, xr, *, side, frames):
    rows = x_ref.shape[0]
    fill_shifts(x_ref[...], x0, xl, xr, side, frames)
    grad = d_ref[...]
    for k in range(dw_ref.shape[0]):
        dw_ref[k] = dot_tn(grad, shifted(k, x0, xl, xr, rows, side, frames))


def norm_back_kernel(
    p_ref, v_ref, r_ref, rb_ref, c_ref, g_ref, m_ref, o_ref, low_ref, high_ref, scratch,
    *, offset, offsetb, fold, frames
):
    width = v_ref.shape[1]
    count = c_ref[...]
    mean, rstd = moments(r_ref, offset, width, count, fold)
    low, slope = back_sums(rb_ref, offsetb, width, count, fold)
    mask = rowwise(m_ref[...], width)
    out = norm_back(p_ref[...], v_ref[...], mean, rstd, g_ref[...], low, slope, mask)
    o_ref[...] = out
    take_rows(low_ref, out, 0, frames, scratch)
    take_rows(high_ref, out, frames - 1, frames, scratch)


def joined_back_kernel(
    d_ref, p_ref, n_ref, j_ref, w_ref, m_ref, v_ref, r_ref, c_ref, g_ref, b_ref,
    x_ref, o_ref, all_ref, st_ref, scratch, *, offset, frames
):
    step, steps = pl.program_id(0), pl.num_programs(0)
    depth = d_ref.shape[1]

    @pl.when(step == 0)
    def _():
        grad = d_ref[...]
        all_ref[:, :depth] = after_rows(scratch, grad, n_ref[...], frames)
        all_ref[:, depth : 2 * depth] = grad
        all_ref[:, 2 * depth :] = before_rows(scratch, grad, p_ref[...], frames)

    mask = rowwise(m_ref[...], o_ref.shape[1])
    out = mask * (dot_nn(all_ref[...], w_ref[...]) + j_ref[...])

    @pl.when(step < steps - 1)
    def _():
        x_ref[...] = out

    @pl.when(step == steps - 1)
    def _():
        mean, rstd = moments(r_ref, offset, v_ref.shape[1], c_ref[...])
        normed = (v_ref[...] - mean) * rstd
        grad = out * silu_slope(g_ref[...] * normed + b_ref[...])
        o_ref[...] = grad
        store_back_sums(st_ref, grad, normed)


def reduce_weight_kernel(d_ref, x_ref, a_ref, dw_ref):
    store_weight(dw_ref, d_ref[...], x_ref, a_ref)


def lateral_back_kernel(
    d_ref, n_ref, f_ref, v_ref, x_ref, r_ref, c_ref, g_ref, b_ref, m_ref, l_ref,
    o_ref, on_ref, st_ref, scratch, *, offset, frames
):
    width = v_ref.shape[1]
    wide = width // GROUP
    here = d_ref[...]
    onward = after_rows(scratch, here, n_ref[...], frames)
    on_ref[...] = onward
    back = jnp.concatenate(
        [
            dot_nn(here, l_ref[2]),
            dot_nn(here, l_ref[3]),
            dot_nn(here, l_ref[4]) + dot_nn(onward, l_ref[0]),
            dot_nn(onward, l_ref[1]),
        ],
        axis=1,
    )
    mean, rstd = moments(r_ref, offset, wide, c_ref[...])
    normed = (v_ref[...] - repeat(mean, GROUP)) * repeat(rstd, GROUP)
    mask = rowwise(m_ref[...], width)
    pre = g_ref[...] * normed + b_ref[...] + x_ref[...]
    grad = mask * (f_ref[...] + back) * silu_slope(pre)
    o_ref[...] = grad
    store_back_sums(st_ref, grad, normed, GROUP)


def lateral_weight_kernel(d_ref, on_ref, x_ref, dw_ref):
    wide = dw_ref.shape[2]
    here, onward = d_ref[...], on_ref[...]
    for k, (grad, r) in enumerate(((onward, 2), (onward, 3), (here, 0), (here, 1), (here, 2))):
        dw_ref[k] = dot_tn(grad, x_ref[:, r * wide : (r + 1) * wide])


def fast_expand_back_kernel(
    p_ref, v_ref, r_ref, rb_ref, c_ref, g_ref, u_ref, ru_ref, gu_ref, bu_ref, m_ref, w_ref,
    d_ref, o_ref, st_ref, *, offset, offsetb, offsetu, fold
):
    width = v_ref.shape[1]
    wide, inner = width // GROUP, u_ref.shape[1]
    count = c_ref[...]
    mean, rstd = moments(r_ref, offset, wide, count)
    low, slope = back_sums(rb_ref, offsetb, wide, count)
    mean, rstd, low, slope = [repeat(row, GROUP) for row in (mean, rstd, low, slope)]
    mask = rowwise(m_ref[...], width)
    grad = norm_back(p_ref[...], v_ref[...], mean, rstd, g_ref[...], low, slope, mask)
    d_ref[...] = grad
    mean, rstd = moments(ru_ref, offsetu, inner, count, fold)
    normed = (u_ref[...] - mean) * rstd
    out = rowwise(m_ref[...], inner) * dot_nt(grad, w_ref[...])
    out = out * silu_slope(gu_ref[...] * normed + bu_ref[...])
    o_ref[...] = out
    store_back_sums(st_ref, out, normed)


def transposed_product_kernel(d_ref, x_ref, dw_ref):
    dw_ref[...] = dot_tn(d_ref[...], x_ref[...])


def fast_first_back_kernel(
    d_ref, p_ref, n_ref, res_ref, w_ref, m_ref, x_ref, o_ref, dw_ref, sp_ref, sn_ref,
    matrix, *, frames, inner
):
    grad = d_ref[...]
    width = grad.shape[1]
    before = before_rows(sp_ref, grad, p_ref[...], frames)
    after = after_rows(sn_ref, grad, n_ref[...], frames)
    lane = lax.broadcasted_iota(jnp.int32, (1, width), 1)
    edge = jnp.where(lane < inner, after, jnp.where(lane >= width - inner, before, 0.0))
    both = jnp.concatenate([grad, edge], axis=1)
    mask = rowwise(m_ref[...], o_ref.shape[1])
    o_ref[...] = mask * (dot_nn(both, banded(w_ref, matrix)) + res_ref[...])
    dw_ref[...] = dot_tn(both, x_ref[...])


def load_rows_kernel(own_ref, x_ref, m_ref, o_ref):
    o_ref[...] = x_ref[...].reshape(o_ref.shape) * rowwise(m_ref[...], o_ref.shape[1])


def load_packed_kernel(own_ref, x_ref, o_ref):
    wide = x_ref.shape[1]
    for r in range(GROUP):
        o_ref[:, r * wide : (r + 1) * wide] = x_ref[pl.ds(r, o_ref.shape[0], stride=GROUP), :]


def place_rows_kernel(own_ref, a_ref, b_ref, c_ref, d_ref, o_ref):
    for slot, refs in ((0, (a_ref, c_ref)), (1, (b_ref, d_ref))):
        for own in range(2):

            @pl.when((pl.program_id(0) == slot) & (own_ref[0] == own))
            def _():
                o_ref[...] = refs[own][...].reshape(o_ref.shape)


def place_packed_kernel(own_ref, a_ref, b_ref, c_ref, d_ref, o_ref):
    wide = o_ref.shape[1]
    for slot, refs in ((0, (a_ref, c_ref)), (1, (b_ref, d_ref))):
        for own in range(2):

            @pl.when((pl.program_id(0) == slot) & (own_ref[0] == own))
            def _():
                for r in range(GROUP):
                    o_ref[pl.ds(r, refs[own].shape[0], stride=GROUP), :] = refs[own][
                        :, r * wide : (r + 1) * wide
                    ]


def chosen(kernel, own, grid, ins, in_specs, out, out_spec):
    return pl.pallas_call(
        kernel,
        out_shape=jax.ShapeDtypeStruct(out, jnp.float32),
        grid_spec=pltpu.PrefetchScalarGridSpec(
            num_scalar_prefetch=1, grid=grid, in_specs=in_specs, out_specs=out_spec
        ),
        compiler_params=pltpu.CompilerParams(vmem_limit_bytes=VMEM_BYTES),
    )(own, *ins)


def place_weight_kernel(own_ref, a_ref, b_ref, c_ref, d_ref, o_ref):
    count, rows, width = a_ref.shape
    for own, refs in enumerate(((a_ref, b_ref), (c_ref, d_ref))):

        @pl.when(own_ref[0] == own)
        def _():
            for half, ref in enumerate(refs):
                for k in range(count):
                    o_ref[half * rows : (half + 1) * rows, k * width : (k + 1) * width] = ref[k]


def place_weight(low, high, own):
    to_zero, to_one = cross(low, high)
    count, rows, width = low.shape
    return chosen(
        place_weight_kernel,
        own,
        (1,),
        [low, to_zero, to_one, high],
        [pl.BlockSpec(low.shape, lambda j, o: (0, 0, 0))] * 4,
        (2 * rows, count * width),
        pl.BlockSpec((2 * rows, count * width), lambda j, o: (0, 0)),
    )


def pieces_of(places):
    return max(n for n in range(1, 9) if places % (4 * n) == 0 or n == 1)


def load_rows(values, mask, own):
    grid = jnp.transpose(values[:, 0], (0, 3, 1, 2))
    _, places, frames, wide = grid.shape
    steps = pieces_of(places)
    size = places // steps
    return chosen(
        load_rows_kernel,
        own,
        (steps,),
        [grid, mask],
        [
            pl.BlockSpec((None, size, frames, wide), lambda j, o: (o[0], j, 0, 0)),
            pl.BlockSpec((size * frames, 128), lambda j, o: (j, 0)),
        ],
        (places * frames, wide),
        pl.BlockSpec((size * frames, wide), lambda j, o: (j, 0)),
    )


def packed_view(values):
    grid = jnp.transpose(values[:, 0], (0, 3, 1, 2))
    return grid.reshape(grid.shape[0], -1, grid.shape[3])


def load_packed(values, own):
    grid = packed_view(values)
    _, rows, wide = grid.shape
    out = (rows // GROUP, GROUP * wide)
    return chosen(
        load_packed_kernel,
        own,
        (1,),
        [grid],
        [pl.BlockSpec((None, rows, wide), lambda j, o: (o[0], 0, 0))],
        out,
        pl.BlockSpec(out, lambda j, o: (0, 0)),
    )


def cross(first, second):
    return (
        lax.ppermute(first, "section", [(1, 0)]),
        lax.ppermute(second, "section", [(0, 1)]),
    )


def place_rows(first, second, own, frames):
    to_zero, to_one = cross(first, second)
    rows, wide = first.shape
    places = rows // frames
    steps = pieces_of(places)
    size = places // steps

    def spec(slot, core):
        def where(t, j, o):
            used = (t == slot) & (o[0] == core)
            return (jnp.where(used, j, jnp.where(t > slot, steps - 1, 0)), 0)

        return pl.BlockSpec((size * frames, wide), where)

    out = chosen(
        place_rows_kernel,
        own,
        (2, steps),
        [first, to_zero, to_one, second],
        [spec(0, 0), spec(1, 0), spec(0, 1), spec(1, 1)],
        (2, places, frames, wide),
        pl.BlockSpec((None, size, frames, wide), lambda t, j, o: (t, j, 0, 0)),
    )
    return jnp.transpose(out, (0, 2, 3, 1))[None, :, None]


def place_packed(first, second, own, frames):
    to_zero, to_one = cross(first, second)
    rows, full = first.shape
    wide = full // GROUP
    out = chosen(
        place_packed_kernel,
        own,
        (2,),
        [first, to_zero, to_one, second],
        [pl.BlockSpec((rows, full), lambda t, o: (0, 0))] * 4,
        (2, rows * GROUP, wide),
        pl.BlockSpec((None, rows * GROUP, wide), lambda t, o: (t, 0, 0)),
    )
    grid = out.reshape(2, rows // frames, GROUP * frames, wide)
    return jnp.transpose(grid, (0, 2, 3, 1))[None, :, None]


def bits_of(axis):
    size, stride, found = lax.axis_size(axis), 1, []
    while stride < size:
        found.append((axis, stride))
        stride *= 2
    return found


def routes():
    near, far, deep = bits_of("tm"), [], bits_of("clip")
    middle = len(near) // 2
    near, far = near[:middle], near[middle:]
    one, two, three = near + far + deep, far + deep + near, deep + near + far
    return [list(zip(one, two)), list(zip(two, three)), list(zip(three, one))]


def halves(values, bit, axis=0):
    rows = values.shape[axis] // 2
    kept = lax.dynamic_slice_in_dim(values, bit * rows, rows, axis)
    return kept, lax.dynamic_slice_in_dim(values, (1 - bit) * rows, rows, axis)


def core_half(arrays):
    core = lax.axis_index("section")
    pairs = [halves(x, core, 1) for x in arrays]
    kept, sent = [
        jnp.concatenate([p[k].reshape(-1, p[k].shape[2]) for p in pairs]) for k in range(2)
    ]
    return kept + swap(sent)


def half_pieces(total, arrays):
    pieces, cursor = [], 0
    for x in arrays:
        shape = (x.shape[0], x.shape[1] // 2, x.shape[2])
        rows = shape[0] * shape[1]
        pieces.append(total[cursor : cursor + rows].reshape(shape))
        cursor += rows
    return pieces


def reduction(arrays, route):
    arrays = yield arrays
    total = core_half(arrays)
    bits = [side_of(pair) for pair in route]
    for pair, bit in zip(route, bits):
        (total,) = yield (total,)
        kept, sent = halves(total, bit)
        total = kept + trade(sent, pair)
    for pair, bit in reversed(list(zip(route, bits))):
        (total,) = yield (total,)
        taken = trade(total, pair)
        low, high = jnp.where(bit == 0, total, taken), jnp.where(bit == 0, taken, total)
        total = jnp.concatenate([low, high], axis=0)
    return half_pieces(total, arrays)


def summed(arrays):
    arrays = yield arrays
    total = core_half(arrays)
    (total,) = yield (total,)
    return half_pieces(lax.psum(total, AXES), arrays)


def held_grads(block, names):
    found = yield [block.grads[n] for n in names]
    for name, value in zip(names, found):
        block.grads[name] = value


def side_of(pair):
    sides = [(lax.axis_index(axis) // stride) % 2 for axis, stride in pair]
    return jnp.where(lax.axis_index("section") == 0, sides[0], sides[1])


def trade(values, pair):
    sizes = {axis: lax.axis_size(axis) for axis in AXES}
    partners = []
    for core, (axis, stride) in enumerate(pair):
        for clip in range(sizes["clip"]):
            for tm in range(sizes["tm"]):
                to = {"clip": clip, "tm": tm}
                to[axis] ^= stride
                partners.append(
                    tuple(
                        (core * sizes["clip"] + c) * sizes["tm"] + t
                        for c, t in ((clip, tm), (to["clip"], to["tm"]))
                    )
                )
    return lax.ppermute(values, ("section",) + AXES, partners)


def small_reduction(values):
    axes = ("section",) + AXES
    count = lax.axis_size("section") * lax.axis_size("clip") * lax.axis_size("tm")
    rows = -(-values.shape[0] // count) * count
    shares = jnp.pad(values, ((0, rows - values.shape[0]), (0, 0))).reshape(count, -1, values.shape[1])
    (shares,) = yield (shares,)
    share = jnp.sum(lax.all_to_all(shares, axes, 0, 0), axis=0)
    (share,) = yield (share,)
    copies = jnp.broadcast_to(share[None], (count,) + share.shape)
    out = lax.all_to_all(copies, axes, 0, 0).reshape(rows, -1)
    return out[: values.shape[0]]


class Job:
    def __init__(self, steps, paces=(1,)):
        self.steps, self.paces, self.result = steps, list(paces), None
        self.held = next(steps)

    def resume(self, held):
        for _ in range(self.paces.pop(0) if len(self.paces) > 1 else self.paces[0]):
            try:
                held = self.steps.send(held)
            except StopIteration as end:
                self.held, self.result = None, end.value
                return
        self.held = held

    def finish(self):
        while self.held is not None:
            self.resume(self.held)
        return self.result


class Section:
    def __init__(self, index, small, large):
        self.fast_reduce, spatial, expand, gain, bias = [x[index] for x in small]
        inner, wide = self.fast_reduce.shape[1], self.fast_reduce.shape[2]
        self.lateral, self.slow_reduce, self.slow_spatial, self.slow_expand, self.shortcut = [
            Stacked(x, index) for x in large
        ]
        self.inner, self.wide, self.depth = inner, wide, self.slow_expand.shape[1]
        eye = jnp.eye(GROUP, dtype=jnp.float32)
        self.fast_spatial = jnp.einsum("rq,koi->kqori", eye, spatial, precision="highest").reshape(
            spatial.shape[0], GROUP * inner, GROUP * inner
        )
        self.fast_expand = jnp.einsum("rq,oi->riqo", eye, expand, precision="highest").reshape(
            GROUP * inner, GROUP * wide
        )
        widths = [
            inner, inner, wide, self.lateral.shape[1], self.depth, self.depth,
            self.slow_expand.shape[0], self.shortcut.shape[0],
        ]
        repeats = [GROUP, GROUP, GROUP, 1, 1, 1, 1, 1]
        self.widths, self.gains, self.biases, cursor = widths, [], [], 0
        for width, times in zip(widths, repeats):
            self.gains.append(jnp.tile(gain[None, cursor : cursor + width], (1, times)))
            self.biases.append(jnp.tile(bias[None, cursor : cursor + width], (1, times)))
            cursor += width


class Block:
    def __init__(self, section, mask, frames, shared):
        self.s, self.mask, self.frames, self.shared = section, mask, frames, shared
        self.rows = mask.shape[0]
        self.places = self.rows // frames
        self.side = math.isqrt(self.places)
        self.pad = -(-(self.side + 1) * frames // 8) * 8
        self.grads, self.sums, self.back = {}, {}, {}

    def window(self, width):
        return [(self.rows + 2 * self.pad, width)] * 3

    def lanes(self, width):
        return (width // 128, self.rows, 128)

    def fast_first(self, fast_input, own):
        rows, places, width = self.rows, self.places, GROUP * self.s.inner
        grid, full = packed_view(fast_input), GROUP * self.s.wide
        outs = [(rows, full), (rows, 2 * width), (places, width), (places, width)]
        return pl.pallas_call(
            partial(fast_first_kernel, frames=self.frames),
            out_shape=[jax.ShapeDtypeStruct(s, jnp.float32) for s in outs],
            grid_spec=pltpu.PrefetchScalarGridSpec(
                num_scalar_prefetch=1,
                grid=(1,),
                in_specs=[
                    pl.BlockSpec((None,) + grid.shape[1:], lambda j, o: (o[0], 0, 0)),
                    pl.BlockSpec((rows, 128), lambda j, o: (0, 0)),
                    pl.BlockSpec(self.s.fast_reduce.shape, lambda j, o: (0, 0, 0)),
                ],
                out_specs=[pl.BlockSpec(s, lambda j, o: (0, 0)) for s in outs],
                scratch_shapes=[
                    pltpu.VMEM(self.lanes(width), jnp.float32),
                    pltpu.VMEM((2 * width, full), jnp.float32),
                ],
            ),
            compiler_params=pltpu.CompilerParams(vmem_limit_bytes=VMEM_BYTES),
        )(own, grid, self.mask, self.s.fast_reduce)

    def fast_forward(self, fast_in, parts):
        s, mask, frames, rows, places = self.s, self.mask, self.frames, self.rows, self.places
        c4 = self.shared
        self.fast_in = fast_in
        width, full = GROUP * s.inner, GROUP * s.wide
        both, low, high = parts
        self.first, sums = call(
            fast_join_kernel,
            [(rows, width), (1, 2 * width)],
            [both, from_previous(high), from_next(low), mask],
            [self.lanes(width)] * 2,
            frames=frames,
            inner=s.inner,
        )
        self.sums[0] = yield sums
        second, self.first_act, sums = call(
            conv_kernel,
            [(rows, width), (rows, width), (1, 2 * width)],
            [self.first, self.sums[0][0], c4["fast"], s.gains[0], s.biases[0], mask, s.fast_spatial],
            self.window(width),
            offset=self.sums[0][1], fold=s.inner, side=self.side, frames=frames,
        )
        self.second = second
        self.sums[1] = yield sums
        self.third, self.second_act, sums = call(
            fast_expand_kernel,
            [(rows, full), (rows, width), (1, 2 * s.wide)],
            [second, self.sums[1][0], c4["fast"], s.gains[1], s.biases[1], mask, s.fast_expand],
            offset=self.sums[1][1], fold=s.inner,
        )
        self.sums[2] = yield sums
        following = (self.following or self).s.fast_reduce
        lateral = s.widths[3]
        shapes = [(rows, full), (rows, lateral), (rows, lateral), (places, lateral)]
        if self.following:
            shapes += [(rows, 2 * width), (places, width), (places, width)]
        else:
            shapes += [(8, 256), (8, 128), (8, 128)]
        self.fast_out, here, onward, edge, *self.parts = call(
            fast_out_kernel,
            shapes,
            [
                self.third, fast_in, self.sums[2][0], c4["fast"], s.gains[2], s.biases[2], mask,
                s.lateral, following,
            ],
            [self.lanes(lateral), (2 * width, full)],
            offset=self.sums[2][1], frames=frames, more=self.following is not None,
        )
        self.lateral, sums = call(
            lateral_join_kernel,
            [(rows, lateral), (1, 2 * lateral)],
            [here, onward, from_previous(edge), mask],
            [self.lanes(lateral)],
            frames=frames,
        )
        self.sums[3] = yield sums

    def slow_forward(self, slow_in):
        s, mask, frames, rows, places = self.s, self.mask, self.frames, self.rows, self.places
        count = self.shared["slow"]
        depth, lateral, wide, out_wide = s.depth, s.widths[3], slow_in.shape[1], s.widths[7]
        full = wide + lateral
        self.slow_in = slow_in
        r3, offset = self.sums[3]
        reduced, low, high, self.lateral_act = call_steps(
            reduce_kernel,
            3,
            [(rows, 3 * depth), (places, depth), (places, depth), (rows, lateral)],
            [columns(rows, depth), fixed((places, depth)), fixed((places, depth)), fixed((rows, lateral))],
            [slow_in, self.lateral, r3, count, s.gains[3], s.biases[3], mask, s.slow_reduce],
            [
                fixed((rows, wide)), fixed((rows, lateral)), fixed(r3.shape), fixed((1, 1)),
                fixed((1, lateral)), fixed((1, lateral)), fixed((rows, 128)),
                s.slow_reduce.block((depth, full), lambda j: (j, 0)),
            ],
            [(rows, full), self.lanes(depth)],
            offset=offset, frames=frames,
        )
        steps = out_wide // depth
        self.skipped, skip_sum, skip_square = call_steps(
            shortcut_kernel,
            steps,
            [(rows, out_wide), (1, out_wide), (1, out_wide)],
            [columns(rows, depth), columns(1, depth), columns(1, depth)],
            [slow_in, self.lateral_act, mask, s.shortcut],
            [
                fixed((rows, wide)), fixed((rows, lateral)), fixed((rows, 128)),
                s.shortcut.block((depth, full), lambda j: (j, 0)),
            ],
        )
        self.inner, sums = call(
            inner_join_kernel,
            [(rows, depth), (1, 2 * depth)],
            [reduced, from_previous(high), from_next(low), mask],
            [self.lanes(depth)] * 2,
            frames=frames,
        )
        r, offset = yield jnp.concatenate([sums, skip_sum, skip_square], axis=1)
        self.sums[4], self.sums[7] = (r, offset), (r, offset + 2 * depth)
        self.middle, self.inner_act, sums = call(
            conv_kernel,
            [(rows, depth), (rows, depth), (1, 2 * depth)],
            [self.inner, r, count, s.gains[4], s.biases[4], mask, s.slow_spatial],
            self.window(depth),
            offset=offset, fold=0, side=self.side, frames=frames,
        )
        self.sums[5] = yield sums
        r5, offset = self.sums[5]
        self.expanded, self.middle_act, total, square = call_steps(
            expand_kernel,
            steps,
            [(rows, out_wide), (rows, depth), (1, out_wide), (1, out_wide)],
            [columns(rows, depth), fixed((rows, depth)), columns(1, depth), columns(1, depth)],
            [self.middle, r5, count, s.gains[5], s.biases[5], mask, s.slow_expand],
            [
                fixed((rows, depth)), fixed(r5.shape), fixed((1, 1)), fixed((1, depth)),
                fixed((1, depth)), fixed((rows, 128)),
                s.slow_expand.block((depth, depth), lambda j: (j, 0)),
            ],
            offset=offset,
        )
        self.sums[6] = yield jnp.concatenate([total, square], axis=1)
        self.slow_out = call_steps(
            slow_out_kernel,
            steps,
            [(rows, out_wide)],
            [columns(rows, depth)],
            *self.slow_pre_inputs(),
            offset6=self.sums[6][1], offset7=self.sums[7][1], total=out_wide,
        )[0]

    def slow_pre_inputs(self):
        s, rows, depth = self.s, self.rows, self.s.depth
        r6, r7 = self.sums[6][0], self.sums[7][0]
        wide, row = columns(rows, depth), columns(1, depth)
        return (
            [
                self.expanded, self.skipped, r6, r7, self.shared["slow"], s.gains[6], s.biases[6],
                s.gains[7], s.biases[7], self.mask,
            ],
            [
                wide, wide, fixed(r6.shape), fixed(r7.shape), fixed((1, 1)), row, row, row, row,
                fixed((rows, 128)),
            ],
        )

    def slow_backward(self, slow_grad):
        s, mask, frames, rows, places = self.s, self.mask, self.frames, self.rows, self.places
        count = self.shared["slow"]
        depth, lateral, out_wide, wide = s.depth, s.widths[3], s.widths[7], self.slow_in.shape[1]
        full, steps = wide + lateral, out_wide // depth
        (r6, offset6), (r7, offset7) = self.sums[6], self.sums[7]
        ins, specs = self.slow_pre_inputs()
        pre, low, slope6, slope7 = call_steps(
            slow_slope_kernel,
            steps,
            [(rows, out_wide)] + [(1, out_wide)] * 3,
            [columns(rows, depth)] + [columns(1, depth)] * 3,
            [slow_grad] + ins,
            [columns(rows, depth)] + specs,
            offset6=offset6, offset7=offset7, total=out_wide,
        )
        rb, offsetb = yield jnp.concatenate([low, slope6, slope7], axis=1)
        self.back[6], self.back[7] = (rb, offsetb, offsetb + out_wide), (rb, offsetb, offsetb + 2 * out_wide)
        r5, offset5 = self.sums[5]
        skip_grad, self.grads["slow_expand"], pre, sums = call_steps(
            expand_back_kernel,
            steps,
            [(rows, out_wide), (out_wide, depth), (rows, depth), (1, 2 * depth)],
            [columns(rows, depth), bands(depth, depth), fixed((rows, depth)), fixed((1, 2 * depth))],
            [
                pre, self.expanded, self.skipped, r6, r7, rb, count, s.gains[6], s.gains[7], mask,
                s.slow_expand, self.middle_act, self.middle, r5, s.gains[5], s.biases[5],
            ],
            [columns(rows, depth)] * 3
            + [fixed(r6.shape), fixed(r7.shape), fixed(rb.shape), fixed((1, 1))]
            + [columns(1, depth)] * 2
            + [fixed((rows, 128)), s.slow_expand.block((depth, depth), lambda j: (j, 0))]
            + [fixed((rows, depth)), fixed((rows, depth))]
            + [fixed(r5.shape), fixed((1, depth)), fixed((1, depth))],
            [(rows, depth)],
            offset6=offset6, offset7=offset7, offsetb=offsetb, offset5=offset5, total=out_wide,
        )
        self.grads["shortcut"], joined_grad = call_steps(
            shortcut_back_kernel,
            steps,
            [(full // lateral, out_wide, lateral), (rows, full)],
            [pl.BlockSpec((full // lateral, depth, lateral), lambda j: (0, j, 0)), fixed((rows, full))],
            [skip_grad, s.shortcut, self.slow_in, self.lateral_act],
            [
                columns(rows, depth), s.shortcut.block((depth, full), lambda j: (j, 0)),
                fixed((rows, wide)), fixed((rows, lateral)),
            ],
        )
        rb, offsetb = yield sums
        self.back[5] = (rb, offsetb, offsetb + depth)
        r4, offset4 = self.sums[4]
        middle_grad, pre, sums = call(
            conv_back_kernel,
            [(rows, depth), (rows, depth), (1, 2 * depth)],
            [
                pre, self.middle, r5, rb, count, s.gains[5], self.inner, r4, s.gains[4], s.biases[4],
                mask, s.slow_spatial,
            ],
            self.window(depth),
            offset=offset5, offsetb=offsetb, offsetu=offset4, fold=0, side=self.side, frames=frames,
        )
        self.grads["slow_spatial"] = call(
            conv_weight_kernel,
            [s.slow_spatial.shape],
            [self.inner_act, middle_grad],
            self.window(depth),
            side=self.side, frames=frames,
        )[0]
        rb, offsetb = yield sums
        self.back[4] = (rb, offsetb, offsetb + depth)
        inner_grad, low, high = call(
            norm_back_kernel,
            [(rows, depth), (places, depth), (places, depth)],
            [pre, self.inner, r4, rb, count, s.gains[4], mask],
            [self.lanes(depth)],
            offset=offset4, offsetb=offsetb, fold=0, frames=frames,
        )
        r3, offset3 = self.sums[3]
        last = wide // lateral
        self.slow_in_grad, self.lateral_pre, reduced_grad, self.lateral_sums = call_steps(
            joined_back_kernel,
            last + 1,
            [(rows, wide), (rows, lateral), (rows, 3 * depth), (1, 2 * lateral)],
            [
                pl.BlockSpec((rows, lateral), lambda j: (0, jnp.minimum(j, last - 1))),
                fixed((rows, lateral)), fixed((rows, 3 * depth)), fixed((1, 2 * lateral)),
            ],
            [
                inner_grad, from_previous(high), from_next(low), joined_grad, s.slow_reduce, mask,
                self.lateral, r3, count, s.gains[3], s.biases[3],
            ],
            [
                fixed((rows, depth)), fixed((places, depth)), fixed((places, depth)),
                columns(rows, lateral), s.slow_reduce.block((3 * depth, lateral), lambda j: (0, j)),
                fixed((rows, 128)),
                fixed((rows, lateral)), fixed(r3.shape), fixed((1, 1)), fixed((1, lateral)),
                fixed((1, lateral)),
            ],
            [self.lanes(depth)],
            offset=offset3, frames=frames,
        )
        self.grads["slow_reduce"] = call_steps(
            reduce_weight_kernel,
            3,
            [(full // lateral, 3 * depth, lateral)],
            [pl.BlockSpec((full // lateral, depth, lateral), lambda j: (0, j, 0))],
            [reduced_grad, self.slow_in, self.lateral_act],
            [columns(rows, depth), fixed((rows, wide)), fixed((rows, lateral))],
        )[0]

    def fast_backward(self, fast_grad):
        s, mask, frames, rows, places = self.s, self.mask, self.frames, self.rows, self.places
        count, count4 = self.shared["slow"], self.shared["fast"]
        wide, inner, lateral = s.wide, s.inner, s.widths[3]
        width, full = GROUP * inner, GROUP * wide
        rb, offsetb = yield self.lateral_sums
        self.back[3] = (rb, offsetb, offsetb + lateral)
        r3, offset3 = self.sums[3]
        here, low, _ = call(
            norm_back_kernel,
            [(rows, lateral), (places, lateral), (places, lateral)],
            [self.lateral_pre, self.lateral, r3, rb, count, s.gains[3], mask],
            [self.lanes(lateral)],
            offset=offset3, offsetb=offsetb, fold=0, frames=frames,
        )
        r2, offset2 = self.sums[2]
        residual, onward, sums = call(
            lateral_back_kernel,
            [(rows, full), (rows, lateral), (1, 2 * wide)],
            [
                here, from_next(low), fast_grad(), self.third, self.fast_in, r2, count4, s.gains[2],
                s.biases[2], mask, s.lateral,
            ],
            [self.lanes(lateral)],
            offset=offset2, frames=frames,
        )
        self.grads["lateral"] = call(
            lateral_weight_kernel, [(5, lateral, wide)], [here, onward, self.fast_out]
        )[0]
        rb, offsetb = yield sums
        self.back[2] = (rb, offsetb, offsetb + wide)
        r1, offset1 = self.sums[1]
        third_grad, pre, sums = call(
            fast_expand_back_kernel,
            [(rows, full), (rows, width), (1, 2 * width)],
            [
                residual, self.third, r2, rb, count4, s.gains[2], self.second, r1, s.gains[1],
                s.biases[1], mask, s.fast_expand,
            ],
            offset=offset2, offsetb=offsetb, offsetu=offset1, fold=inner,
        )
        grid = call(transposed_product_kernel, [(full, width)], [third_grad, self.second_act])[0]
        grid = grid.reshape(GROUP, wide, GROUP, inner)
        self.grads["fast_expand"] = sum(grid[r, :, r] for r in range(GROUP))
        rb, offsetb = yield sums
        self.back[1] = (rb, offsetb, offsetb + width)
        r0, offset0 = self.sums[0]
        second_grad, pre, sums = call(
            conv_back_kernel,
            [(rows, width), (rows, width), (1, 2 * width)],
            [
                pre, self.second, r1, rb, count4, s.gains[1], self.first, r0, s.gains[0], s.biases[0],
                mask, s.fast_spatial,
            ],
            self.window(width),
            offset=offset1, offsetb=offsetb, offsetu=offset0, fold=inner, side=self.side,
            frames=frames,
        )
        grid = call(
            conv_weight_kernel,
            [s.fast_spatial.shape],
            [self.first_act, second_grad],
            self.window(width),
            side=self.side, frames=frames,
        )[0]
        grid = grid.reshape(-1, GROUP, inner, GROUP, inner)
        self.grads["fast_spatial"] = sum(grid[:, r, :, r] for r in range(GROUP))
        rb, offsetb = yield sums
        self.back[0] = (rb, offsetb, offsetb + width)
        first_grad, low, high = call(
            norm_back_kernel,
            [(rows, width), (places, width), (places, width)],
            [pre, self.first, r0, rb, count4, s.gains[0], mask],
            [self.lanes(width)],
            offset=offset0, offsetb=offsetb, fold=inner, frames=frames,
        )
        self.fast_in_grad, grid = call(
            fast_first_back_kernel,
            [(rows, full), (2 * width, full)],
            [
                first_grad, from_previous(high), from_next(low), residual, s.fast_reduce, mask,
                self.fast_in,
            ],
            [self.lanes(width)] * 2 + [(2 * width, full)],
            frames=frames, inner=inner,
        )
        grid = grid.reshape(2, GROUP, inner, GROUP, wide)
        near, far = grid[0], grid[1]
        self.grads["fast_reduce"] = jnp.stack(
            [
                near[1, :, 0] + near[2, :, 1] + near[3, :, 2] + far[0, :, 3],
                near[0, :, 0] + near[1, :, 1] + near[2, :, 2] + near[3, :, 3],
                near[0, :, 1] + near[1, :, 2] + near[2, :, 3] + far[3, :, 0],
            ]
        )

    def blocked(self, name):
        grad = self.grads[name]
        if name == "lateral":
            taps, depth, wide = grad.shape
            grad = jnp.pad(grad, ((0, taps % 2), (0, 0), (0, 0))).reshape(-1, 2, depth, wide)
            return jnp.swapaxes(grad, 1, 2).reshape(-1, depth, 2 * wide)
        return grad if grad.ndim == 3 else grad[None]

    def fast_flat(self):
        names = ("fast_reduce", "fast_spatial", "fast_expand")
        flat = jnp.concatenate([self.grads[n].reshape(-1) for n in names])
        return jnp.pad(flat, (0, -flat.shape[0] % 1024)).reshape(-1, 128)

    def norm_grads(self):
        gains, biases = [], []
        for j, width in enumerate(self.s.widths):
            rb, low, slope = self.back[j]
            span = GROUP * width if j < 2 else width
            for start, found in ((slope, gains), (low, biases)):
                total = jnp.sum(rb[:, start : start + span], axis=0)
                found.append(jnp.sum(total.reshape(-1, width), axis=0))
        return jnp.stack([jnp.concatenate(gains), jnp.concatenate(biases)])


class Task:
    def __init__(self, steps):
        self.steps = steps
        self.wanted = next(steps)

    def resume(self, totals):
        self.wanted = next(self.steps, None) if totals is None else self.send(totals)

    def send(self, totals):
        try:
            return self.steps.send(totals)
        except StopIteration:
            return None


def advance(*tasks, extra=None, jobs=()):
    wanted = [task.wanted for task in tasks] + ([] if extra is None else [extra])
    r = sums_everywhere(jnp.concatenate(wanted, axis=1))
    jobs = [job for job in jobs if job.held is not None]
    if jobs:
        r, held = lax.optimization_barrier((r, [job.held for job in jobs]))
        for job, values in zip(jobs, held):
            job.resume(values)
    offsets = [sum(w.shape[1] for w in wanted[:k]) for k in range(len(wanted))]
    return [(r, offset) for offset in offsets]


def body(
    slow_input,
    fast_input,
    frame_counts,
    fast_reduce,
    fast_spatial,
    fast_expand,
    lateral_conv,
    slow_reduce,
    slow_spatial,
    slow_expand,
    shortcut,
    norm_gain,
    norm_bias,
    slow_cotangent,
    fast_cotangent,
):
    own = lax.axis_index("section")
    lower = own == 0
    frames, positions = slow_input.shape[2], slow_input.shape[4]
    rows = frames * positions
    wide = fast_input.shape[3]

    which = jnp.reshape(own, (1,)).astype(jnp.int32)
    small = [fast_reduce[0], fast_spatial[0], fast_expand[0], norm_gain[0], norm_bias[0]]
    flat = jnp.concatenate([x.reshape(-1) for x in small])
    flat = jnp.pad(flat, (0, -flat.shape[0] % 1024)).reshape(-1, 128)
    flat = lax.all_gather(flat, "section").reshape(2, -1)
    gathered, cursor = [], 0
    for x in small:
        gathered.append(flat[:, cursor : cursor + x.size].reshape((2,) + x.shape))
        cursor += x.size
    large = [
        lateral_conv[0],
        slow_reduce[0].reshape(-1, slow_reduce.shape[3]),
        slow_spatial[0],
        slow_expand[0],
        shortcut[0],
    ]
    large = [lax.all_gather(x, "section") for x in large]
    sections = [Section(index, gathered, large) for index in range(2)]

    count_here = lax.dynamic_index_in_dim(frame_counts, own, 0, keepdims=False)
    frame = lax.axis_index("clip") * frames + lax.broadcasted_iota(
        jnp.int32, (positions, frames, 128), 1
    )
    mask = (frame < count_here).astype(jnp.float32).reshape(rows, 128)
    shared = {}
    blocks = [Block(section, mask, frames, shared) for section in sections]
    blocks[0].following, blocks[1].following = blocks[1], None

    fast_in, *parts = blocks[0].fast_first(fast_input, which)
    fast = [Task(blocks[0].fast_forward(fast_in, parts)), None]
    got = advance(fast[0], extra=jnp.sum(mask, axis=0, keepdims=True))
    r, offset = got[1]
    shared["slow"] = jnp.sum(r[:, offset : offset + 1], axis=0, keepdims=True)
    shared["fast"] = GROUP * shared["slow"]
    fast[0].resume(got[0])
    for step in range(2):
        fast[0].resume(advance(fast[0])[0])
    fast[1] = Task(blocks[1].fast_forward(blocks[0].fast_out, blocks[0].parts))
    got = advance(fast[0], fast[1])
    fast[0].resume(got[0])
    fast[1].resume(got[1])
    slow = [Task(blocks[0].slow_forward(load_rows(slow_input, mask, which))), None]
    for step in range(3):
        got = advance(slow[0], fast[1])
        slow[0].resume(got[0])
        fast[1].resume(got[1])
    slow[1] = Task(blocks[1].slow_forward(blocks[0].slow_out))
    for step in range(3):
        slow[1].resume(advance(slow[1])[0])

    zero, one = blocks
    ways = routes()
    jobs = []

    def start(steps, paces=(1,)):
        jobs.append(Job(steps, paces))
        return jobs[-1]

    tasks = Task(one.slow_backward(load_rows(slow_cotangent, mask, which)))
    tasks.resume(advance(tasks)[0])
    soonest = start(
        reduction([one.blocked(n) for n in ("shortcut", "slow_expand")], ways[0]), (2, 2, 2, 2, 1)
    )
    tasks.resume(advance(tasks, jobs=jobs)[0])
    start(held_grads(one, ("slow_spatial",)))
    tasks.resume(advance(tasks, jobs=jobs)[0])
    start(held_grads(one, ("slow_reduce",)))
    late = Task(one.fast_backward(lambda: load_packed(fast_cotangent, which)))
    soon = Task(zero.slow_backward(one.slow_in_grad))
    for step in range(3):
        got = advance(late, soon, jobs=jobs)
        late.resume(got[0])
        soon.resume(got[1])
        if step == 0:
            whole = start(
                reduction(
                    [one.blocked(n) for n in ("slow_spatial", "slow_reduce", "lateral")], ways[1]
                ),
                (2, 2, 2, 2, 1),
            )
            early = start(
                reduction([zero.blocked(n) for n in ("shortcut", "slow_expand")], ways[2]),
                (1, 1, 2, 2, 2, 1),
            )
        if step == 1:
            start(held_grads(zero, ("slow_spatial",)))
        if step == 2:
            start(held_grads(zero, ("slow_reduce",)))
    last = Task(zero.fast_backward(lambda: one.fast_in_grad))
    got = advance(late, last, jobs=jobs)
    late.resume(got[0])
    last.resume(got[1])
    middle = start(
        reduction([zero.blocked(n) for n in ("slow_spatial", "slow_reduce", "lateral")], ways[0]),
        (2, 2, 2, 1),
    )
    middle.resume(middle.held)
    for step in range(3):
        last.resume(advance(last, jobs=jobs)[0])
    rest = Job(small_reduction(jnp.concatenate([zero.fast_flat(), one.fast_flat()]))).finish()

    totals = {}
    halves_one = dict(zip(("shortcut", "slow_expand"), soonest.finish()))
    halves_one.update(zip(("slow_spatial", "slow_reduce", "lateral"), whole.finish()))
    halves_zero = dict(zip(("shortcut", "slow_expand"), early.finish()))
    halves_zero.update(zip(("slow_spatial", "slow_reduce", "lateral"), middle.finish()))
    for name in ("shortcut", "slow_reduce", "slow_expand"):
        totals[name] = place_weight(halves_zero[name], halves_one[name], which)
    for name in ("slow_spatial", "lateral"):
        low, high = halves_zero[name], halves_one[name]
        to_zero, to_one = cross(low, high)
        totals[name] = jnp.concatenate(
            [jnp.where(lower, low, to_one), jnp.where(lower, to_zero, high)], axis=1
        )
    pairs, depth, double = totals["lateral"].shape
    lateral = totals["lateral"].reshape(pairs, depth, 2, double // 2)
    lateral = jnp.swapaxes(lateral, 1, 2).reshape(2 * pairs, depth, -1)
    totals["lateral"] = lateral[: lateral_conv.shape[1]]
    rows = rest.shape[0] // 2
    flat, cursor = jnp.where(lower, rest[:rows], rest[rows:]).reshape(-1), 0
    for name, x in zip(("fast_reduce", "fast_spatial", "fast_expand"), small):
        totals[name] = flat[cursor : cursor + x.size]
        cursor += x.size
    names = (
        "fast_reduce",
        "fast_spatial",
        "fast_expand",
        "lateral",
        "slow_reduce",
        "slow_spatial",
        "slow_expand",
        "shortcut",
    )
    norm_grads = [block.norm_grads() for block in blocks]
    kept = jnp.where(lower, norm_grads[0], norm_grads[1])
    kept = kept + swap(jnp.where(lower, norm_grads[1], norm_grads[0]))
    shapes = [
        x.shape
        for x in (
            fast_reduce, fast_spatial, fast_expand, lateral_conv, slow_reduce, slow_spatial,
            slow_expand, shortcut,
        )
    ]
    totals = [totals[name].reshape(shape) for name, shape in zip(names, shapes)]
    return (
        place_rows(zero.slow_out, one.slow_out, which, frames),
        place_packed(zero.fast_out, one.fast_out, which, frames),
        place_rows(zero.slow_in_grad, one.slow_in_grad, which, frames),
        place_packed(zero.fast_in_grad, one.fast_in_grad, which, frames),
        *totals,
        kept[None, 0],
        kept[None, 1],
    )


def solution(mesh):
    acts = P(None, "tm", "clip", None, None)
    outs = P("section", None, "tm", "clip", None, None)
    four, three, two = P("section", None, None, None), P("section", None, None), P("section", None)
    weights = (four, four, three, four, four, four, three, three)
    return jax.shard_map(
        body,
        mesh=mesh,
        in_specs=(acts, acts, P(None, "tm"), *weights, two, two, acts, acts),
        out_specs=(outs, outs, outs, outs, *weights, two, two),
        check_vma=False,
    )
```

```python
from functools import partial
import math

import jax
import jax.numpy as jnp
from jax import lax
from jax.experimental import pallas as pl
from jax.experimental.pallas import tpu as pltpu
from jax.sharding import PartitionSpec as P

EPSILON = 1e-05
PLANS = ((0, 0, 0, 0, 0, 0), (1, 2, 2, 2, 2, 0), (2, 3, 3, 0))
FINE = lax.Precision.HIGH
GROUP = 4
AXES = ("clip", "tm")
NORM_ORDER = (2, 0, 1, 3, 4, 5, 6, 7)


def dot_nn(a, b):
    return lax.dot_general(a, b, (((1,), (0,)), ((), ())), precision=FINE)


def dot_nt(a, b):
    return lax.dot_general(a, b, (((1,), (1,)), ((), ())), precision=FINE)


def dot_tn(a, b):
    return lax.dot_general(a, b, (((0,), (0,)), ((), ())), precision=FINE)


def sums_everywhere(vector):
    return lax.all_to_all(vector, AXES, 0, 0)


def from_previous(edge):
    count = lax.axis_size("clip")
    return lax.ppermute(edge, "clip", [(i, i + 1) for i in range(count - 1)])


def from_next(edge):
    count = lax.axis_size("clip")
    return lax.ppermute(edge, "clip", [(i + 1, i) for i in range(count - 1)])


def swap(values):
    return lax.ppermute(values, "section", [(0, 1), (1, 0)])


def silu(v):
    return v * jax.nn.sigmoid(v)


def silu_slope(v):
    s = jax.nn.sigmoid(v)
    return s * (1.0 + v * (1.0 - s))


VMEM_BYTES = 36 * 2**20


def rowwise(mask, width):
    return jnp.concatenate([mask] * (width // mask.shape[1]), axis=1)


def moments(r_ref, offset, width, count, fold=0):
    total = jnp.sum(r_ref[:, offset : offset + width], axis=0, keepdims=True)
    square = jnp.sum(r_ref[:, offset + width : offset + 2 * width], axis=0, keepdims=True)
    if fold:
        total, square = around(total, fold), around(square, fold)
    mean = total / count
    return mean, lax.rsqrt(square / count - mean * mean + EPSILON)


def around(row, fold):
    out = row
    for step in range(fold, row.shape[1], fold):
        out = out + pltpu.roll(row, step, 1)
    return out


def repeat(row, times):
    return row if times == 1 else jnp.concatenate([row] * times, axis=1)


def put_sums(st_ref, start, row):
    st_ref[:, start : start + row.shape[1]] = jnp.broadcast_to(row, (st_ref.shape[0], row.shape[1]))


def put_part(st_ref, offset, row):
    width = row.shape[1]
    start = pl.multiple_of(offset + pl.program_id(0) * width, 128)
    st_ref[:, pl.ds(start, width)] = jnp.broadcast_to(row, (st_ref.shape[0], width))


def folded(row, fold):
    width = row.shape[1] // fold
    return sum(row[:, k * width : (k + 1) * width] for k in range(fold))


def store_sums(st_ref, values, mask, fold=1):
    weighted = values * mask
    total = folded(jnp.sum(weighted, axis=0, keepdims=True), fold)
    put_sums(st_ref, 0, total)
    square = folded(jnp.sum(weighted * values, axis=0, keepdims=True), fold)
    put_sums(st_ref, total.shape[1], square)


class Stacked:
    def __init__(self, both, index):
        self.both, self.index, self.shape = both, index, both.shape[1:]

    def block(self, shape, place):
        def where(*step):
            return (self.index,) + place(*step)

        return pl.BlockSpec((None,) + shape, where)

    def whole(self):
        zeros = (0,) * len(self.shape)
        return self.block(self.shape, lambda *step: zeros)


class Window:
    def __init__(self, both, place, offset, shape):
        self.both, self.place, self.offset, self.shape = both, place, offset, shape

    def whole(self):
        lead = (None,) * len(self.place)
        if self.shape[0] == 1:
            where = self.place + (0, self.offset // self.shape[1])
        else:
            where = self.place + (self.offset // self.shape[0], 0)
        return pl.BlockSpec(lead + self.shape, lambda *step: where)

    def parts(self, width):
        lead = (None,) * len(self.place)
        first = self.offset // width
        return pl.BlockSpec(lead + (1, width), lambda j: self.place + (0, first + j))


def array_of(value):
    if isinstance(value, Stacked):
        return pltpu.with_memory_space_constraint(value.both, pltpu.HBM)
    return value.both if isinstance(value, Window) else value


def call(kernel, outs, ins, scratch=(), **static):
    vmem = pl.BlockSpec(memory_space=pltpu.VMEM)
    return pl.pallas_call(
        partial(kernel, **static),
        grid=(1,),
        out_shape=[jax.ShapeDtypeStruct(s, jnp.float32) for s in outs],
        in_specs=[x.whole() if isinstance(x, (Stacked, Window)) else vmem for x in ins],
        out_specs=[vmem] * len(outs),
        scratch_shapes=[pltpu.VMEM(s, jnp.float32) for s in scratch],
        compiler_params=pltpu.CompilerParams(vmem_limit_bytes=VMEM_BYTES),
    )(*[array_of(x) for x in ins])


def fixed(shape):
    return pl.BlockSpec(shape, lambda j: (0,) * len(shape))


def columns(rows, width):
    return pl.BlockSpec((rows, width), lambda j: (0, j))


def bands(height, width):
    return pl.BlockSpec((height, width), lambda j: (j, 0))


def streamed(value, spec):
    value = array_of(value)
    pieces = [n for n in spec.block_shape if n is not None]
    if math.prod(pieces) < value.size and value.size * 4 > 2**20:
        return pltpu.with_memory_space_constraint(value, pltpu.HBM)
    return value


def call_steps(kernel, steps, outs, out_specs, ins, in_specs, scratch=(), **static):
    return pl.pallas_call(
        partial(kernel, **static),
        grid=(steps,),
        out_shape=[jax.ShapeDtypeStruct(s, jnp.float32) for s in outs],
        in_specs=in_specs,
        out_specs=out_specs,
        scratch_shapes=[pltpu.VMEM(s, jnp.float32) for s in scratch],
        compiler_params=pltpu.CompilerParams(
            dimension_semantics=("arbitrary",), vmem_limit_bytes=VMEM_BYTES
        ),
    )(*[streamed(x, spec) for x, spec in zip(ins, in_specs)])


def take_rows(out_ref, values, first, frames, scratch):
    for k in range(out_ref.shape[1] // 128):
        scratch[k] = values[:, k * 128 : (k + 1) * 128]
        out_ref[:, k * 128 : (k + 1) * 128] = scratch[k, pl.ds(first, out_ref.shape[0], stride=frames), :]


def put_rows(values, first, frames, edge, scratch):
    pieces = []
    for k in range(edge.shape[1] // 128):
        scratch[k] = values[:, k * 128 : (k + 1) * 128]
        scratch[k, pl.ds(first, edge.shape[0], stride=frames), :] = edge[:, k * 128 : (k + 1) * 128]
        pieces.append(scratch[k])
    return jnp.concatenate(pieces, axis=1) if len(pieces) > 1 else pieces[0]


def before_rows(scratch, values, edge, frames):
    return put_rows(pltpu.roll(values, 1, 0), 0, frames, edge, scratch)


def after_rows(scratch, values, edge, frames):
    return put_rows(pltpu.roll(values, values.shape[0] - 1, 0), frames - 1, frames, edge, scratch)


def banded(w_ref, matrix):
    taps, wide = 3, w_ref.shape[1]
    inner = w_ref.shape[0] // taps
    matrix[...] = jnp.zeros(matrix.shape, jnp.float32)
    for q in range(GROUP):
        for k in range(taps):
            r = q + k - 1
            start = q * inner + (0 if 0 <= r < GROUP else GROUP * inner)
            r = r % GROUP
            matrix[start : start + inner, r * wide : (r + 1) * wide] = w_ref[k * inner : (k + 1) * inner]
    return matrix[...]


def diagonal(tile, inner):
    frame = lax.broadcasted_iota(jnp.int32, (1, tile.shape[1]), 1) // inner
    return jnp.concatenate([jnp.where(frame == r, tile, 0.0) for r in range(GROUP)], axis=0)


def undiagonal(square, inner):
    count = square.shape[0] // GROUP
    frame = lax.broadcasted_iota(jnp.int32, (1, square.shape[1]), 1) // inner
    total = sum(
        jnp.where(frame == r, square[r * count : (r + 1) * count], 0.0) for r in range(GROUP)
    )
    total = around(total, inner)
    count = count // GROUP
    return sum(
        jnp.where(frame == r, total[r * count : (r + 1) * count], 0.0) for r in range(GROUP)
    )


def tap(k_ref, k, inner):
    if not inner:
        return k_ref[k]
    return diagonal(k_ref[k * inner : (k + 1) * inner], inner)


def fast_first_kernel(
    own_ref, x_ref, m_ref, w_ref, x_out, y_ref, low_ref, high_ref, scratch, matrix, *, frames
):
    rows, wide = m_ref.shape[0], x_ref.shape[1]
    for r in range(GROUP):
        x_out[:, r * wide : (r + 1) * wide] = (
            x_ref[pl.ds(r, rows, stride=GROUP), :] * rowwise(m_ref[...], wide)
        )
    y = dot_nt(x_out[...], banded(w_ref, matrix))
    y_ref[...] = y
    take_rows(low_ref, y[:, y.shape[1] // 2 :], 0, frames, scratch)
    take_rows(high_ref, y[:, y.shape[1] // 2 :], frames - 1, frames, scratch)


def fast_join_kernel(y_ref, p_ref, n_ref, m_ref, o_ref, st_ref, sp_ref, sn_ref, *, frames, inner):
    width = o_ref.shape[1]
    edge = y_ref[:, width:]
    before = before_rows(sp_ref, edge, p_ref[...], frames)
    after = after_rows(sn_ref, edge, n_ref[...], frames)
    lane = lax.broadcasted_iota(jnp.int32, (1, width), 1)
    out = y_ref[:, :width] + jnp.where(
        lane < inner, before, jnp.where(lane >= width - inner, after, 0.0)
    )
    o_ref[...] = out
    store_sums(st_ref, out, m_ref[...])
    put_sums(st_ref, 2 * width, jnp.sum(m_ref[...], axis=0, keepdims=True))


def fill_shifts(values, x0, xl, xr, side, frames):
    rows, width = values.shape
    pad = (x0.shape[0] - rows) // 2
    blank = jnp.zeros((pad + 8, width), jnp.float32)
    for ref in (x0, xl, xr):
        ref[0 : pad + 8] = blank
        ref[pad + rows - 8 : 2 * pad + rows] = blank
    row = lax.broadcasted_iota(jnp.int32, (rows, 1), 0)
    column = lax.rem(lax.div(row, frames), side)
    x0[pad : pad + rows] = values
    xl[pad + frames : pad + frames + rows] = jnp.where(column == side - 1, 0.0, values)
    xr[pad - frames : pad - frames + rows] = jnp.where(column == 0, 0.0, values)


def shifted(k, x0, xl, xr, rows, side, frames):
    pad = (x0.shape[0] - rows) // 2
    start = pad + (k // 3 - 1) * side * frames
    return (xl, x0, xr)[k % 3][start : start + rows]


def conv_kernel(
    v_ref, r_ref, c_ref, g_ref, b_ref, m_ref, k_ref, o_ref, act_ref, st_ref, x0, xl, xr,
    *, offset, fold, side, frames
):
    rows, width = v_ref.shape
    mean, rstd = moments(r_ref, offset, width, c_ref[...], fold)
    mask = rowwise(m_ref[...], width)
    act = mask * silu(g_ref[...] * ((v_ref[...] - mean) * rstd) + b_ref[...])
    act_ref[...] = act
    fill_shifts(act, x0, xl, xr, side, frames)
    total = dot_nt(shifted(0, x0, xl, xr, rows, side, frames), tap(k_ref, 0, fold))
    for k in range(1, 9):
        total += dot_nt(shifted(k, x0, xl, xr, rows, side, frames), tap(k_ref, k, fold))
    o_ref[...] = total
    store_sums(st_ref, total, rowwise(m_ref[...], total.shape[1]))


def fast_expand_kernel(
    v_ref, r_ref, c_ref, g_ref, b_ref, m_ref, w_ref, o_ref, act_ref, st_ref, *, offset, fold
):
    width = v_ref.shape[1]
    mean, rstd = moments(r_ref, offset, width, c_ref[...], fold)
    act = rowwise(m_ref[...], width) * silu(g_ref[...] * ((v_ref[...] - mean) * rstd) + b_ref[...])
    act_ref[...] = act
    out = dot_nt(act, diagonal(w_ref[...], fold))
    o_ref[...] = out
    store_sums(st_ref, out, rowwise(m_ref[...], out.shape[1]), GROUP)


def fast_out_kernel(
    v_ref, x_ref, r_ref, c_ref, g_ref, b_ref, m_ref, l_ref, w_ref,
    out_ref, here_ref, next_ref, edge_ref, y_ref, low_ref, high_ref, scratch, matrix, *, offset, frames, more
):
    width = v_ref.shape[1]
    wide = width // GROUP
    mean, rstd = moments(r_ref, offset, wide, c_ref[...])
    mean, rstd = repeat(mean, GROUP), repeat(rstd, GROUP)
    pre = g_ref[...] * ((v_ref[...] - mean) * rstd) + b_ref[...] + x_ref[...]
    out = rowwise(m_ref[...], width) * silu(pre)
    out_ref[...] = out
    one, two, three, four = [out[:, r * wide : (r + 1) * wide] for r in range(GROUP)]
    here_ref[...] = dot_nt(one, l_ref[2]) + dot_nt(two, l_ref[3]) + dot_nt(three, l_ref[4])
    onward = dot_nt(three, l_ref[0]) + dot_nt(four, l_ref[1])
    next_ref[...] = onward
    take_rows(edge_ref, onward, frames - 1, frames, scratch)
    if more:
        y = dot_nt(out, banded(w_ref, matrix))
        y_ref[...] = y
        half = y.shape[1] // 2
        take_rows(low_ref, y[:, half:], 0, frames, scratch)
        take_rows(high_ref, y[:, half:], frames - 1, frames, scratch)
    else:
        for ref in (y_ref, low_ref, high_ref):
            ref[...] = jnp.zeros(ref.shape, jnp.float32)


def lateral_join_kernel(h_ref, n_ref, e_ref, m_ref, o_ref, st_ref, sp_ref, *, frames):
    out = h_ref[...] + before_rows(sp_ref, n_ref[...], e_ref[...], frames)
    o_ref[...] = out
    store_sums(st_ref, out, rowwise(m_ref[...], out.shape[1]))


def reduce_kernel(
    x_ref, v_ref, r_ref, c_ref, g_ref, b_ref, m_ref, w_ref, y_ref, low_ref, high_ref, act_ref, joined,
    scratch, *, offset, frames
):
    step = pl.program_id(0)
    wide, lateral = x_ref.shape[1], v_ref.shape[1]

    @pl.when(step == 0)
    def _():
        mean, rstd = moments(r_ref, offset, lateral, c_ref[...])
        joined[:, :wide] = x_ref[...]
        act = silu(g_ref[...] * ((v_ref[...] - mean) * rstd) + b_ref[...])
        act = act * rowwise(m_ref[...], lateral)
        joined[:, wide:] = act
        act_ref[...] = act

    y = dot_nt(joined[...], w_ref[...])
    y_ref[...] = y

    @pl.when(step == 0)
    def _():
        take_rows(high_ref, y, frames - 1, frames, scratch)

    @pl.when(step == 2)
    def _():
        take_rows(low_ref, y, 0, frames, scratch)


def shortcut_kernel(x_ref, a_ref, m_ref, w_ref, y_ref, st_ref):
    wide = x_ref.shape[1]
    out = dot_nt(x_ref[...], w_ref[:, :wide])
    out += dot_nt(a_ref[...], w_ref[:, wide:])
    y_ref[...] = out
    weighted = out * rowwise(m_ref[...], out.shape[1])
    put_part(st_ref, 0, jnp.sum(weighted, axis=0, keepdims=True))
    put_part(st_ref, st_ref.shape[1] // 2, jnp.sum(weighted * out, axis=0, keepdims=True))


def inner_join_kernel(y_ref, p_ref, n_ref, m_ref, o_ref, st_ref, sp_ref, sn_ref, *, frames):
    depth = o_ref.shape[1]
    out = y_ref[:, depth : 2 * depth]
    out += before_rows(sp_ref, y_ref[:, :depth], p_ref[...], frames)
    out += after_rows(sn_ref, y_ref[:, 2 * depth : 3 * depth], n_ref[...], frames)
    o_ref[...] = out
    store_sums(st_ref, out, rowwise(m_ref[...], depth))


def expand_kernel(
    v_ref, r_ref, c_ref, g_ref, b_ref, m_ref, w_ref, o_ref, act_ref, st_ref, *, offset
):
    width = v_ref.shape[1]

    @pl.when(pl.program_id(0) == 0)
    def _():
        mean, rstd = moments(r_ref, offset, width, c_ref[...])
        act = silu(g_ref[...] * ((v_ref[...] - mean) * rstd) + b_ref[...])
        act_ref[...] = act * rowwise(m_ref[...], width)

    out = dot_nt(act_ref[...], w_ref[...])
    o_ref[...] = out
    weighted = out * rowwise(m_ref[...], out.shape[1])
    put_part(st_ref, 0, jnp.sum(weighted, axis=0, keepdims=True))
    put_part(st_ref, st_ref.shape[1] // 2, jnp.sum(weighted * out, axis=0, keepdims=True))


def slow_out_kernel(
    e_ref, k_ref, r6_ref, r7_ref, c_ref, g6_ref, b6_ref, g7_ref, b7_ref, m_ref, o_ref,
    *, offset6, offset7, total
):
    pre, _, _ = slow_pre(
        e_ref, k_ref, r6_ref, r7_ref, c_ref, g6_ref, b6_ref, g7_ref, b7_ref, offset6, offset7, total
    )
    o_ref[...] = rowwise(m_ref[...], pre.shape[1]) * silu(pre)


def part(r_ref, offset, width):
    start = pl.multiple_of(offset + pl.program_id(0) * width, 128)
    return jnp.sum(r_ref[:, pl.ds(start, width)], axis=0, keepdims=True)


def moments_part(r_ref, offset, total, width, count):
    mean = part(r_ref, offset, width) / count
    square = part(r_ref, offset + total, width) / count
    return mean, lax.rsqrt(square - mean * mean + EPSILON)


def slow_pre(
    e_ref, k_ref, r6_ref, r7_ref, c_ref, g6_ref, b6_ref, g7_ref, b7_ref, offset6, offset7, total
):
    width = e_ref.shape[1]
    mean6, rstd6 = moments_part(r6_ref, offset6, total, width, c_ref[...])
    mean7, rstd7 = moments_part(r7_ref, offset7, total, width, c_ref[...])
    n6 = (e_ref[...] - mean6) * rstd6
    n7 = (k_ref[...] - mean7) * rstd7
    pre = (g6_ref[...] * n6 + b6_ref[...]) + (g7_ref[...] * n7 + b7_ref[...])
    return pre, (n6, rstd6), (n7, rstd7)


def slow_slope_kernel(
    d_ref, e_ref, k_ref, r6_ref, r7_ref, c_ref, g6_ref, b6_ref, g7_ref, b7_ref, m_ref,
    p_ref, st_ref, *, offset6, offset7, total
):
    pre, (n6, _), (n7, _) = slow_pre(
        e_ref, k_ref, r6_ref, r7_ref, c_ref, g6_ref, b6_ref, g7_ref, b7_ref, offset6, offset7, total
    )
    grad = rowwise(m_ref[...], pre.shape[1]) * d_ref[...] * silu_slope(pre)
    p_ref[...] = grad
    put_part(st_ref, 0, jnp.sum(grad, axis=0, keepdims=True))
    put_part(st_ref, total, jnp.sum(grad * n6, axis=0, keepdims=True))
    put_part(st_ref, 2 * total, jnp.sum(grad * n7, axis=0, keepdims=True))


def expand_back_kernel(
    p_ref, e_ref, k_ref, r6_ref, r7_ref, rb_ref, c_ref, g6_ref, g7_ref, m_ref, w_ref, act_ref,
    v_ref, r5_ref, g5_ref, b5_ref,
    skip_ref, dw_ref, o_ref, st_ref, acc, *, offset6, offset7, offsetb, offset5, total
):
    step, steps = pl.program_id(0), pl.num_programs(0)
    width, depth = p_ref.shape[1], v_ref.shape[1]
    count, mask = c_ref[...], rowwise(m_ref[...], width)
    mean6, rstd6 = moments_part(r6_ref, offset6, total, width, count)
    mean7, rstd7 = moments_part(r7_ref, offset7, total, width, count)
    low = part(rb_ref, offsetb, width) / count
    q6 = part(rb_ref, offsetb + total, width) / count
    q7 = part(rb_ref, offsetb + 2 * total, width) / count
    pre = p_ref[...]
    grad = mask * ((g6_ref[...] * rstd6) * (pre - low - (e_ref[...] - mean6) * rstd6 * q6))
    skip_ref[...] = mask * ((g7_ref[...] * rstd7) * (pre - low - (k_ref[...] - mean7) * rstd7 * q7))
    dw_ref[...] = dot_tn(grad, act_ref[...])
    product = dot_nn(grad, w_ref[...])

    @pl.when(step == 0)
    def _():
        acc[...] = product

    @pl.when(step > 0)
    def _():
        acc[...] += product

    @pl.when(step == steps - 1)
    def _():
        mean, rstd = moments(r5_ref, offset5, depth, count)
        normed = (v_ref[...] - mean) * rstd
        out = rowwise(m_ref[...], depth) * acc[...]
        out = out * silu_slope(g5_ref[...] * normed + b5_ref[...])
        o_ref[...] = out
        store_back_sums(st_ref, out, normed)


def store_weight(dw_ref, grad, x_ref, a_ref):
    count, _, width = dw_ref.shape
    for k in range(count - 1):
        dw_ref[k] = dot_tn(grad, x_ref[:, k * width : (k + 1) * width])
    dw_ref[count - 1] = dot_tn(grad, a_ref[...])


def back_sums(rb_ref, offset, width, count, fold=0):
    low = jnp.sum(rb_ref[:, offset : offset + width], axis=0, keepdims=True)
    slope = jnp.sum(rb_ref[:, offset + width : offset + 2 * width], axis=0, keepdims=True)
    if fold:
        low, slope = around(low, fold), around(slope, fold)
    return low / count, slope / count


def norm_back(pre, values, mean, rstd, gain, low, slope, mask):
    return mask * ((gain * rstd) * (pre - low - (values - mean) * rstd * slope))


def store_back_sums(st_ref, grad, normed, fold=1):
    low = folded(jnp.sum(grad, axis=0, keepdims=True), fold)
    put_sums(st_ref, 0, low)
    put_sums(st_ref, low.shape[1], folded(jnp.sum(grad * normed, axis=0, keepdims=True), fold))


def conv_back_kernel(
    p_ref, v_ref, r_ref, rb_ref, c_ref, g_ref, u_ref, ru_ref, gu_ref, bu_ref, m_ref, k_ref,
    d_ref, o_ref, st_ref, x0, xl, xr, *, offset, offsetb, offsetu, fold, side, frames
):
    rows, width = v_ref.shape
    count, mask = c_ref[...], rowwise(m_ref[...], width)
    mean, rstd = moments(r_ref, offset, width, count, fold)
    low, slope = back_sums(rb_ref, offsetb, width, count, fold)
    grad = norm_back(p_ref[...], v_ref[...], mean, rstd, g_ref[...], low, slope, mask)
    d_ref[...] = grad
    fill_shifts(grad, x0, xl, xr, side, frames)
    total = dot_nn(shifted(0, x0, xl, xr, rows, side, frames), tap(k_ref, 8, fold))
    for k in range(1, 9):
        total += dot_nn(shifted(k, x0, xl, xr, rows, side, frames), tap(k_ref, 8 - k, fold))
    mean, rstd = moments(ru_ref, offsetu, u_ref.shape[1], count, fold)
    normed = (u_ref[...] - mean) * rstd
    out = rowwise(m_ref[...], u_ref.shape[1]) * total
    out = out * silu_slope(gu_ref[...] * normed + bu_ref[...])
    o_ref[...] = out
    store_back_sums(st_ref, out, normed)


def conv_weight_kernel(x_ref, d_ref, dw_ref, x0, xl, xr, *, fold, side, frames):
    rows = x_ref.shape[0]
    fill_shifts(x_ref[...], x0, xl, xr, side, frames)
    grad = d_ref[...]
    for k in range(9):
        out = dot_tn(grad, shifted(k, x0, xl, xr, rows, side, frames))
        if fold:
            out = undiagonal(out, fold)
            dw_ref[k * out.shape[0] : (k + 1) * out.shape[0]] = out
        else:
            dw_ref[k] = out


def norm_back_kernel(
    p_ref, v_ref, r_ref, rb_ref, c_ref, g_ref, m_ref, o_ref, low_ref, high_ref, scratch,
    *, offset, offsetb, fold, frames
):
    width = v_ref.shape[1]
    count = c_ref[...]
    mean, rstd = moments(r_ref, offset, width, count, fold)
    low, slope = back_sums(rb_ref, offsetb, width, count, fold)
    mask = rowwise(m_ref[...], width)
    out = norm_back(p_ref[...], v_ref[...], mean, rstd, g_ref[...], low, slope, mask)
    o_ref[...] = out
    take_rows(low_ref, out, 0, frames, scratch)
    take_rows(high_ref, out, frames - 1, frames, scratch)


def joined_back_kernel(
    d_ref, p_ref, n_ref, k_ref, w_ref, wk_ref, m_ref, v_ref, r_ref, c_ref, g_ref, b_ref,
    x_ref, o_ref, all_ref, st_ref, scratch, *, offset, frames
):
    step, steps = pl.program_id(0), pl.num_programs(0)
    depth = d_ref.shape[1]

    @pl.when(step == 0)
    def _():
        grad = d_ref[...]
        all_ref[:, :depth] = after_rows(scratch, grad, n_ref[...], frames)
        all_ref[:, depth : 2 * depth] = grad
        all_ref[:, 2 * depth :] = before_rows(scratch, grad, p_ref[...], frames)

    mask = rowwise(m_ref[...], o_ref.shape[1])
    out = mask * (dot_nn(all_ref[...], w_ref[...]) + dot_nn(k_ref[...], wk_ref[...]))

    @pl.when(step < steps - 1)
    def _():
        x_ref[...] = out

    @pl.when(step == steps - 1)
    def _():
        mean, rstd = moments(r_ref, offset, v_ref.shape[1], c_ref[...])
        normed = (v_ref[...] - mean) * rstd
        grad = out * silu_slope(g_ref[...] * normed + b_ref[...])
        o_ref[...] = grad
        store_back_sums(st_ref, grad, normed)


def joined_weight_kernel(d_ref, x_ref, a_ref, dw_ref):
    store_weight(dw_ref, d_ref[...], x_ref, a_ref)


def lateral_back_kernel(
    d_ref, n_ref, f_ref, v_ref, x_ref, r_ref, c_ref, g_ref, b_ref, m_ref, l_ref,
    o_ref, on_ref, st_ref, scratch, *, offset, frames
):
    width = v_ref.shape[1]
    wide = width // GROUP
    here = d_ref[...]
    onward = after_rows(scratch, here, n_ref[...], frames)
    on_ref[...] = onward
    back = jnp.concatenate(
        [
            dot_nn(here, l_ref[2]),
            dot_nn(here, l_ref[3]),
            dot_nn(here, l_ref[4]) + dot_nn(onward, l_ref[0]),
            dot_nn(onward, l_ref[1]),
        ],
        axis=1,
    )
    mean, rstd = moments(r_ref, offset, wide, c_ref[...])
    normed = (v_ref[...] - repeat(mean, GROUP)) * repeat(rstd, GROUP)
    mask = rowwise(m_ref[...], width)
    pre = g_ref[...] * normed + b_ref[...] + x_ref[...]
    grad = mask * (f_ref[...] + back) * silu_slope(pre)
    o_ref[...] = grad
    store_back_sums(st_ref, grad, normed, GROUP)


def lateral_weight_kernel(d_ref, on_ref, x_ref, dw_ref):
    wide = dw_ref.shape[2] // 2
    here, onward = d_ref[...], on_ref[...]
    for k, (grad, r) in enumerate(((onward, 2), (onward, 3), (here, 0), (here, 1), (here, 2))):
        side = (k % 2) * wide
        dw_ref[k // 2, :, side : side + wide] = dot_tn(grad, x_ref[:, r * wide : (r + 1) * wide])
    dw_ref[2, :, wide:] = jnp.zeros((dw_ref.shape[1], wide), jnp.float32)


def fast_expand_back_kernel(
    p_ref, v_ref, r_ref, rb_ref, c_ref, g_ref, u_ref, ru_ref, gu_ref, bu_ref, m_ref, w_ref,
    d_ref, o_ref, st_ref, *, offset, offsetb, offsetu, fold
):
    width = v_ref.shape[1]
    wide, inner = width // GROUP, u_ref.shape[1]
    count = c_ref[...]
    mean, rstd = moments(r_ref, offset, wide, count)
    low, slope = back_sums(rb_ref, offsetb, wide, count)
    mean, rstd, low, slope = [repeat(row, GROUP) for row in (mean, rstd, low, slope)]
    mask = rowwise(m_ref[...], width)
    grad = norm_back(p_ref[...], v_ref[...], mean, rstd, g_ref[...], low, slope, mask)
    d_ref[...] = grad
    mean, rstd = moments(ru_ref, offsetu, inner, count, fold)
    normed = (u_ref[...] - mean) * rstd
    out = rowwise(m_ref[...], inner) * dot_nn(grad, diagonal(w_ref[...], fold))
    out = out * silu_slope(gu_ref[...] * normed + bu_ref[...])
    o_ref[...] = out
    store_back_sums(st_ref, out, normed)


def fast_expand_weight_kernel(d_ref, x_ref, dw_ref, *, fold):
    dw_ref[...] = undiagonal(dot_tn(d_ref[...], x_ref[...]), fold)


def fast_first_back_kernel(
    d_ref, p_ref, n_ref, res_ref, w_ref, m_ref, x_ref, o_ref, dw_ref, sp_ref, sn_ref,
    matrix, *, frames, inner
):
    grad = d_ref[...]
    width = grad.shape[1]
    before = before_rows(sp_ref, grad, p_ref[...], frames)
    after = after_rows(sn_ref, grad, n_ref[...], frames)
    lane = lax.broadcasted_iota(jnp.int32, (1, width), 1)
    edge = jnp.where(lane < inner, after, jnp.where(lane >= width - inner, before, 0.0))
    both = jnp.concatenate([grad, edge], axis=1)
    mask = rowwise(m_ref[...], o_ref.shape[1])
    o_ref[...] = mask * (dot_nn(both, banded(w_ref, matrix)) + res_ref[...])
    full = dot_tn(both, x_ref[...])
    wide = full.shape[1] // GROUP
    for k in range(3):
        total = None
        for q in range(GROUP):
            r = q + k - 1
            start = q * inner + (0 if 0 <= r < GROUP else GROUP * inner)
            r = r % GROUP
            piece = full[start : start + inner, r * wide : (r + 1) * wide]
            total = piece if total is None else total + piece
        dw_ref[k * inner : (k + 1) * inner] = total


def load_rows_kernel(own_ref, x_ref, m_ref, o_ref):
    o_ref[...] = x_ref[...].reshape(o_ref.shape) * rowwise(m_ref[...], o_ref.shape[1])


def load_packed_kernel(own_ref, x_ref, o_ref):
    wide = x_ref.shape[1]
    for r in range(GROUP):
        o_ref[:, r * wide : (r + 1) * wide] = x_ref[pl.ds(r, o_ref.shape[0], stride=GROUP), :]


def place_rows_kernel(own_ref, a_ref, b_ref, c_ref, d_ref, o_ref):
    for slot, refs in ((0, (a_ref, c_ref)), (1, (b_ref, d_ref))):
        for own in range(2):

            @pl.when((pl.program_id(0) == slot) & (own_ref[0] == own))
            def _():
                o_ref[...] = refs[own][...].reshape(o_ref.shape)


def place_packed_kernel(own_ref, a_ref, b_ref, c_ref, d_ref, o_ref):
    wide = o_ref.shape[1]
    for slot, refs in ((0, (a_ref, c_ref)), (1, (b_ref, d_ref))):
        for own in range(2):

            @pl.when((pl.program_id(0) == slot) & (own_ref[0] == own))
            def _():
                for r in range(GROUP):
                    o_ref[pl.ds(r, refs[own].shape[0], stride=GROUP), :] = refs[own][
                        :, r * wide : (r + 1) * wide
                    ]


def chosen(kernel, own, grid, ins, in_specs, out, out_spec):
    return pl.pallas_call(
        kernel,
        out_shape=jax.ShapeDtypeStruct(out, jnp.float32),
        grid_spec=pltpu.PrefetchScalarGridSpec(
            num_scalar_prefetch=1, grid=grid, in_specs=in_specs, out_specs=out_spec
        ),
        compiler_params=pltpu.CompilerParams(vmem_limit_bytes=VMEM_BYTES),
    )(own, *ins)


def place_early_kernel(own_ref, a_ref, b_ref, c_ref, d_ref, shortcut_ref, expand_ref):
    count, rows, width = a_ref.shape
    for own, refs in enumerate(((a_ref, b_ref), (c_ref, d_ref))):

        @pl.when(own_ref[0] == own)
        def _():
            for half, ref in enumerate(refs):
                start = half * rows
                for k in range(count - 1):
                    shortcut_ref[start : start + rows, k * width : (k + 1) * width] = ref[k]
                expand_ref[start : start + rows] = ref[count - 1]


def place_late_kernel(own_ref, a_ref, b_ref, c_ref, d_ref, spatial_ref, reduce_ref, lateral_ref):
    _, rows, width = a_ref.shape
    taps, blocks = spatial_ref.shape[0], reduce_ref.shape[1] // width
    runs = reduce_ref.shape[0] // (2 * rows)
    wide = lateral_ref.shape[2]
    for own, refs in enumerate(((a_ref, b_ref), (c_ref, d_ref))):

        @pl.when(own_ref[0] == own)
        def _():
            for half, ref in enumerate(refs):
                start = half * rows
                for k in range(taps):
                    spatial_ref[k, start : start + rows] = ref[k]
                for k in range(blocks):
                    for j in range(runs):
                        first = (half * runs + j) * rows
                        reduce_ref[first : first + rows, k * width : (k + 1) * width] = ref[
                            taps + k * runs + j
                        ]
                for k in range(lateral_ref.shape[0]):
                    side = (k % 2) * wide
                    lateral_ref[k, start : start + rows] = ref[
                        taps + blocks * runs + k // 2, :, side : side + wide
                    ]


def place_weights(kernel, low, high, rows, own, outs):
    views = [x.reshape(-1, rows, x.shape[1]) for x in (low, *cross(low, high), high)]

    def whole(shape):
        zeros = (0,) * len(shape)
        return pl.BlockSpec(shape, lambda j, o: zeros, pipeline_mode=pl.Buffered(1))

    return pl.pallas_call(
        kernel,
        out_shape=[jax.ShapeDtypeStruct(shape, jnp.float32) for shape in outs],
        grid_spec=pltpu.PrefetchScalarGridSpec(
            num_scalar_prefetch=1,
            grid=(1,),
            in_specs=[whole(x.shape) for x in views],
            out_specs=[pl.BlockSpec(memory_space=pltpu.VMEM)] * len(outs),
        ),
        compiler_params=pltpu.CompilerParams(vmem_limit_bytes=VMEM_BYTES),
    )(own, *views)


def pieces_of(places):
    return max(n for n in range(1, 9) if places % (4 * n) == 0 or n == 1)


def load_rows(values, mask, own):
    grid = jnp.transpose(values[:, 0], (0, 3, 1, 2))
    _, places, frames, wide = grid.shape
    steps = pieces_of(places)
    size = places // steps
    return chosen(
        load_rows_kernel,
        own,
        (steps,),
        [grid, mask],
        [
            pl.BlockSpec((None, size, frames, wide), lambda j, o: (o[0], j, 0, 0)),
            pl.BlockSpec((size * frames, 128), lambda j, o: (j, 0)),
        ],
        (places * frames, wide),
        pl.BlockSpec((size * frames, wide), lambda j, o: (j, 0)),
    )


def packed_view(values):
    grid = jnp.transpose(values[:, 0], (0, 3, 1, 2))
    return grid.reshape(grid.shape[0], -1, grid.shape[3])


def load_packed(values, own):
    grid = packed_view(values)
    _, rows, wide = grid.shape
    out = (rows // GROUP, GROUP * wide)
    return chosen(
        load_packed_kernel,
        own,
        (1,),
        [grid],
        [pl.BlockSpec((None, rows, wide), lambda j, o: (o[0], 0, 0))],
        out,
        pl.BlockSpec(out, lambda j, o: (0, 0)),
    )


def cross(first, second):
    return (
        lax.ppermute(first, "section", [(1, 0)]),
        lax.ppermute(second, "section", [(0, 1)]),
    )


def place_rows(first, second, own, frames):
    to_zero, to_one = cross(first, second)
    rows, wide = first.shape
    places = rows // frames
    steps = pieces_of(places)
    size = places // steps

    def spec(slot, core):
        def where(t, j, o):
            used = (t == slot) & (o[0] == core)
            return (jnp.where(used, j, jnp.where(t > slot, steps - 1, 0)), 0)

        return pl.BlockSpec((size * frames, wide), where)

    out = chosen(
        place_rows_kernel,
        own,
        (2, steps),
        [first, to_zero, to_one, second],
        [spec(0, 0), spec(1, 0), spec(0, 1), spec(1, 1)],
        (2, places, frames, wide),
        pl.BlockSpec((None, size, frames, wide), lambda t, j, o: (t, j, 0, 0)),
    )
    return jnp.transpose(out, (0, 2, 3, 1))[None, :, None]


def place_packed(first, second, own, frames):
    to_zero, to_one = cross(first, second)
    rows, full = first.shape
    wide = full // GROUP
    out = chosen(
        place_packed_kernel,
        own,
        (2,),
        [first, to_zero, to_one, second],
        [pl.BlockSpec((rows, full), lambda t, o: (0, 0))] * 4,
        (2, rows * GROUP, wide),
        pl.BlockSpec((None, rows * GROUP, wide), lambda t, o: (t, 0, 0)),
    )
    grid = out.reshape(2, rows // frames, GROUP * frames, wide)
    return jnp.transpose(grid, (0, 2, 3, 1))[None, :, None]


def bits_of(axis):
    size, stride, found = lax.axis_size(axis), 1, []
    while stride < size:
        found.append((axis, stride))
        stride *= 2
    return found


def routes():
    near, far, deep = bits_of("tm"), [], bits_of("clip")
    middle = len(near) // 2
    near, far = near[:middle], near[middle:]
    one, two, three = near + far + deep, far + deep + near, deep + near + far
    return [list(zip(one, two)), list(zip(two, three)), list(zip(three, one))]


def halves(values, bit, axis=0):
    rows = values.shape[axis] // 2
    kept = lax.dynamic_slice_in_dim(values, bit * rows, rows, axis)
    return kept, lax.dynamic_slice_in_dim(values, (1 - bit) * rows, rows, axis)


def core_half(arrays):
    core = lax.axis_index("section")
    pairs = [halves(x, core, 1) for x in arrays]
    kept, sent = [
        jnp.concatenate([p[k].reshape(-1, p[k].shape[2]) for p in pairs]) for k in range(2)
    ]
    return kept + swap(sent)


def reduction(arrays, route):
    arrays = yield arrays
    total = core_half(arrays)
    bits = [side_of(pair) for pair in route]
    for pair, bit in zip(route, bits):
        (total,) = yield (total,)
        kept, sent = halves(total, bit)
        total = kept + trade(sent, pair)
    for pair, bit in reversed(list(zip(route, bits))):
        (total,) = yield (total,)
        taken = trade(total, pair)
        low, high = jnp.where(bit == 0, total, taken), jnp.where(bit == 0, taken, total)
        total = jnp.concatenate([low, high], axis=0)
    return total


def summed(arrays):
    arrays = yield arrays
    total = core_half(arrays)
    (total,) = yield (total,)
    return half_pieces(lax.psum(total, AXES), arrays)


def summed(groups):
    totals = lax.psum(tuple(core_half(arrays) for arrays in groups), AXES)
    totals = yield totals
    return totals


def worked(values):
    values = yield values
    return values


def held_grads(block, names):
    found = yield [block.grads[n] for n in names]
    for name, value in zip(names, found):
        block.grads[name] = value


def side_of(pair):
    sides = [(lax.axis_index(axis) // stride) % 2 for axis, stride in pair]
    return jnp.where(lax.axis_index("section") == 0, sides[0], sides[1])


def trade(values, pair):
    sizes = {axis: lax.axis_size(axis) for axis in AXES}
    partners = []
    for core, (axis, stride) in enumerate(pair):
        for clip in range(sizes["clip"]):
            for tm in range(sizes["tm"]):
                to = {"clip": clip, "tm": tm}
                to[axis] ^= stride
                partners.append(
                    tuple(
                        (core * sizes["clip"] + c) * sizes["tm"] + t
                        for c, t in ((clip, tm), (to["clip"], to["tm"]))
                    )
                )
    return lax.ppermute(values, ("section",) + AXES, partners)


def small_reduction(values):
    axes = ("section",) + AXES
    count = lax.axis_size("section") * lax.axis_size("clip") * lax.axis_size("tm")
    rows = -(-values.shape[0] // count) * count
    shares = jnp.pad(values, ((0, rows - values.shape[0]), (0, 0))).reshape(count, -1, values.shape[1])
    (shares,) = yield (shares,)
    share = jnp.sum(lax.all_to_all(shares, axes, 0, 0), axis=0)
    (share,) = yield (share,)
    copies = jnp.broadcast_to(share[None], (count,) + share.shape)
    out = lax.all_to_all(copies, axes, 0, 0).reshape(rows, -1)
    return out[: values.shape[0]]


class Job:
    def __init__(self, steps, paces=(1,)):
        self.steps, self.paces, self.result = steps, list(paces), None
        self.held = next(steps)

    def resume(self, held):
        for _ in range(self.paces.pop(0) if len(self.paces) > 1 else self.paces[0]):
            try:
                held = self.steps.send(held)
            except StopIteration as end:
                self.held, self.result = None, end.value
                return
        self.held = held

    def waits(self):
        if self.paces[0] == 0 and len(self.paces) > 1:
            self.paces.pop(0)
            return True
        return self.paces[0] == 0

    def finish(self):
        self.paces = [1]
        while self.held is not None:
            self.resume(self.held)
        return self.result


class Section:
    def __init__(self, index, small, norms, sizes, large):
        self.lateral, self.slow_reduce, self.slow_spatial, self.slow_expand, self.shortcut = [
            Stacked(x, index) for x in large
        ]
        self.inner, self.wide, self.depth = sizes["inner"], sizes["wide"], self.slow_expand.shape[1]
        start = 0
        for name in ("fast_spatial", "fast_reduce", "fast_expand"):
            setattr(self, name, Window(small, (index,), start, (sizes[name], 128)))
            start += sizes[name]
        self.widths = [
            self.inner, self.inner, self.wide, self.lateral.shape[1], self.depth, self.depth,
            self.slow_expand.shape[0], self.shortcut.shape[0],
        ]
        self.gains, self.biases = [None] * 8, [None] * 8
        cursor = 0
        for j in NORM_ORDER:
            width = self.widths[j] * (GROUP if j < 3 else 1)
            self.gains[j] = Window(norms, (index, 0), cursor, (1, width))
            self.biases[j] = Window(norms, (index, 1), cursor, (1, width))
            cursor += width


def norm_row(vector, widths):
    starts = [sum(widths[:j]) for j in range(8)]
    pieces = []
    for j in NORM_ORDER:
        piece = vector[starts[j] : starts[j] + widths[j]]
        pieces += [piece] * (GROUP if j < 3 else 1)
    return jnp.concatenate(pieces)


class Block:
    def __init__(self, section, mask, frames, shared):
        self.s, self.mask, self.frames, self.shared = section, mask, frames, shared
        self.rows = mask.shape[0]
        self.places = self.rows // frames
        self.side = math.isqrt(self.places)
        self.pad = -(-(self.side + 1) * frames // 8) * 8
        self.grads, self.sums, self.back = {}, {}, {}
        self.copies = lax.axis_size("clip") * lax.axis_size("tm")

    def window(self, width):
        return [(self.rows + 2 * self.pad, width)] * 3

    def lanes(self, width):
        return (width // 128, self.rows, 128)

    def fast_first(self, fast_input, own):
        rows, places, width = self.rows, self.places, GROUP * self.s.inner
        grid, full = packed_view(fast_input), GROUP * self.s.wide
        outs = [(rows, full), (rows, 2 * width), (places, width), (places, width)]
        return pl.pallas_call(
            partial(fast_first_kernel, frames=self.frames),
            out_shape=[jax.ShapeDtypeStruct(s, jnp.float32) for s in outs],
            grid_spec=pltpu.PrefetchScalarGridSpec(
                num_scalar_prefetch=1,
                grid=(1,),
                in_specs=[
                    pl.BlockSpec((None,) + grid.shape[1:], lambda j, o: (o[0], 0, 0)),
                    pl.BlockSpec((rows, 128), lambda j, o: (0, 0)),
                    self.s.fast_reduce.whole(),
                ],
                out_specs=[pl.BlockSpec(s, lambda j, o: (0, 0)) for s in outs],
                scratch_shapes=[
                    pltpu.VMEM(self.lanes(width), jnp.float32),
                    pltpu.VMEM((2 * width, full), jnp.float32),
                ],
            ),
            compiler_params=pltpu.CompilerParams(vmem_limit_bytes=VMEM_BYTES),
        )(own, grid, self.mask, array_of(self.s.fast_reduce))

    def fast_forward(self, fast_in, parts):
        s, mask, frames, rows, places = self.s, self.mask, self.frames, self.rows, self.places
        c4 = self.shared
        self.fast_in = fast_in
        width, full = GROUP * s.inner, GROUP * s.wide
        both, low, high = parts
        self.first, sums = call(
            fast_join_kernel,
            [(rows, width), (self.copies, 2 * width + 128)],
            [both, from_previous(high), from_next(low), mask],
            [self.lanes(width)] * 2,
            frames=frames,
            inner=s.inner,
        )
        self.sums[0] = yield sums
        second, self.first_act, sums = call(
            conv_kernel,
            [(rows, width), (rows, width), (self.copies, 2 * width)],
            [self.first, self.sums[0][0], c4["fast"], s.gains[0], s.biases[0], mask, s.fast_spatial],
            self.window(width),
            offset=self.sums[0][1], fold=s.inner, side=self.side, frames=frames,
        )
        self.second = second
        self.sums[1] = yield sums
        self.third, self.second_act, sums = call(
            fast_expand_kernel,
            [(rows, full), (rows, width), (self.copies, 2 * s.wide)],
            [second, self.sums[1][0], c4["fast"], s.gains[1], s.biases[1], mask, s.fast_expand],
            offset=self.sums[1][1], fold=s.inner,
        )
        self.sums[2] = yield sums
        following = (self.following or self).s.fast_reduce
        lateral = s.widths[3]
        shapes = [(rows, full), (rows, lateral), (rows, lateral), (places, lateral)]
        if self.following:
            shapes += [(rows, 2 * width), (places, width), (places, width)]
        else:
            shapes += [(8, 256), (8, 128), (8, 128)]
        self.fast_out, here, onward, edge, *self.parts = call(
            fast_out_kernel,
            shapes,
            [
                self.third, fast_in, self.sums[2][0], c4["fast"], s.gains[2], s.biases[2], mask,
                s.lateral, following,
            ],
            [self.lanes(lateral), (2 * width, full)],
            offset=self.sums[2][1], frames=frames, more=self.following is not None,
        )
        self.lateral, sums = call(
            lateral_join_kernel,
            [(rows, lateral), (self.copies, 2 * lateral)],
            [here, onward, from_previous(edge), mask],
            [self.lanes(lateral)],
            frames=frames,
        )
        self.sums[3] = yield sums

    def slow_forward(self, slow_in):
        s, mask, frames, rows, places = self.s, self.mask, self.frames, self.rows, self.places
        count = self.shared["slow"]
        depth, lateral, wide, out_wide = s.depth, s.widths[3], slow_in.shape[1], s.widths[7]
        full = wide + lateral
        self.slow_in = slow_in
        r3, offset = self.sums[3]
        reduced, low, high, self.lateral_act = call_steps(
            reduce_kernel,
            3,
            [(rows, 3 * depth), (places, depth), (places, depth), (rows, lateral)],
            [columns(rows, depth), fixed((places, depth)), fixed((places, depth)), fixed((rows, lateral))],
            [slow_in, self.lateral, r3, count, s.gains[3], s.biases[3], mask, s.slow_reduce],
            [
                fixed((rows, wide)), fixed((rows, lateral)), fixed(r3.shape), fixed((1, 1)),
                s.gains[3].whole(), s.biases[3].whole(), fixed((rows, 128)),
                s.slow_reduce.block((depth, full), lambda j: (j, 0)),
            ],
            [(rows, full), self.lanes(depth)],
            offset=offset, frames=frames,
        )
        steps = out_wide // depth
        self.skipped, skip_sums = call_steps(
            shortcut_kernel,
            steps,
            [(rows, out_wide), (self.copies, 2 * out_wide)],
            [columns(rows, depth), fixed((self.copies, 2 * out_wide))],
            [slow_in, self.lateral_act, mask, s.shortcut],
            [
                fixed((rows, wide)), fixed((rows, lateral)), fixed((rows, 128)),
                s.shortcut.block((depth, full), lambda j: (j, 0)),
            ],
        )
        self.inner, sums = call(
            inner_join_kernel,
            [(rows, depth), (self.copies, 2 * depth)],
            [reduced, from_previous(high), from_next(low), mask],
            [self.lanes(depth)] * 2,
            frames=frames,
        )
        r, offset = yield jnp.concatenate([sums, skip_sums], axis=1)
        self.sums[4], self.sums[7] = (r, offset), (r, offset + 2 * depth)
        self.middle, self.inner_act, sums = call(
            conv_kernel,
            [(rows, depth), (rows, depth), (self.copies, 2 * depth)],
            [self.inner, r, count, s.gains[4], s.biases[4], mask, s.slow_spatial],
            self.window(depth),
            offset=offset, fold=0, side=self.side, frames=frames,
        )
        self.sums[5] = yield sums
        r5, offset = self.sums[5]
        self.expanded, self.middle_act, sums = call_steps(
            expand_kernel,
            steps,
            [(rows, out_wide), (rows, depth), (self.copies, 2 * out_wide)],
            [columns(rows, depth), fixed((rows, depth)), fixed((self.copies, 2 * out_wide))],
            [self.middle, r5, count, s.gains[5], s.biases[5], mask, s.slow_expand],
            [
                fixed((rows, depth)), fixed(r5.shape), fixed((1, 1)), s.gains[5].whole(),
                s.biases[5].whole(), fixed((rows, 128)),
                s.slow_expand.block((depth, depth), lambda j: (j, 0)),
            ],
            offset=offset,
        )
        self.sums[6] = yield sums
        self.slow_out = call_steps(
            slow_out_kernel,
            steps,
            [(rows, out_wide)],
            [columns(rows, depth)],
            *self.slow_pre_inputs(),
            offset6=self.sums[6][1], offset7=self.sums[7][1], total=out_wide,
        )[0]

    def slow_pre_inputs(self):
        s, rows, depth = self.s, self.rows, self.s.depth
        r6, r7 = self.sums[6][0], self.sums[7][0]
        wide = columns(rows, depth)
        gains = [x.parts(depth) for x in (s.gains[6], s.biases[6], s.gains[7], s.biases[7])]
        return (
            [
                self.expanded, self.skipped, r6, r7, self.shared["slow"], s.gains[6], s.biases[6],
                s.gains[7], s.biases[7], self.mask,
            ],
            [
                wide, wide, fixed(r6.shape), fixed(r7.shape), fixed((1, 1)), *gains,
                fixed((rows, 128)),
            ],
        )

    def slow_backward(self, slow_grad):
        s, mask, frames, rows, places = self.s, self.mask, self.frames, self.rows, self.places
        count = self.shared["slow"]
        depth, lateral, out_wide, wide = s.depth, s.widths[3], s.widths[7], self.slow_in.shape[1]
        full, steps = wide + lateral, out_wide // depth
        (r6, offset6), (r7, offset7) = self.sums[6], self.sums[7]
        ins, specs = self.slow_pre_inputs()
        pre, sums = call_steps(
            slow_slope_kernel,
            steps,
            [(rows, out_wide), (self.copies, 3 * out_wide)],
            [columns(rows, depth), fixed((self.copies, 3 * out_wide))],
            [slow_grad] + ins,
            [columns(rows, depth)] + specs,
            offset6=offset6, offset7=offset7, total=out_wide,
        )
        rb, offsetb = yield sums
        self.back[6], self.back[7] = (rb, offsetb, offsetb + out_wide), (rb, offsetb, offsetb + 2 * out_wide)
        r5, offset5 = self.sums[5]
        skip_grad, self.grads["slow_expand"], pre, sums = call_steps(
            expand_back_kernel,
            steps,
            [(rows, out_wide), (out_wide, depth), (rows, depth), (self.copies, 2 * depth)],
            [columns(rows, depth), bands(depth, depth), fixed((rows, depth)), fixed((self.copies, 2 * depth))],
            [
                pre, self.expanded, self.skipped, r6, r7, rb, count, s.gains[6], s.gains[7], mask,
                s.slow_expand, self.middle_act, self.middle, r5, s.gains[5], s.biases[5],
            ],
            [columns(rows, depth)] * 3
            + [fixed(r6.shape), fixed(r7.shape), fixed(rb.shape), fixed((1, 1))]
            + [s.gains[6].parts(depth), s.gains[7].parts(depth)]
            + [fixed((rows, 128)), s.slow_expand.block((depth, depth), lambda j: (j, 0))]
            + [fixed((rows, depth)), fixed((rows, depth))]
            + [fixed(r5.shape), s.gains[5].whole(), s.biases[5].whole()],
            [(rows, depth)],
            offset6=offset6, offset7=offset7, offsetb=offsetb, offset5=offset5, total=out_wide,
        )
        self.grads["shortcut"] = call_steps(
            joined_weight_kernel,
            steps,
            [(full // lateral, out_wide, lateral)],
            [pl.BlockSpec((full // lateral, depth, lateral), lambda j: (0, j, 0))],
            [skip_grad, self.slow_in, self.lateral_act],
            [columns(rows, depth), fixed((rows, wide)), fixed((rows, lateral))],
        )[0]
        rb, offsetb = yield sums
        self.back[5] = (rb, offsetb, offsetb + depth)
        r4, offset4 = self.sums[4]
        middle_grad, pre, sums = call(
            conv_back_kernel,
            [(rows, depth), (rows, depth), (self.copies, 2 * depth)],
            [
                pre, self.middle, r5, rb, count, s.gains[5], self.inner, r4, s.gains[4], s.biases[4],
                mask, s.slow_spatial,
            ],
            self.window(depth),
            offset=offset5, offsetb=offsetb, offsetu=offset4, fold=0, side=self.side, frames=frames,
        )
        self.grads["slow_spatial"] = call(
            conv_weight_kernel,
            [s.slow_spatial.shape],
            [self.inner_act, middle_grad],
            self.window(depth),
            fold=0, side=self.side, frames=frames,
        )[0]
        rb, offsetb = yield sums
        self.back[4] = (rb, offsetb, offsetb + depth)
        inner_grad, low, high = call(
            norm_back_kernel,
            [(rows, depth), (places, depth), (places, depth)],
            [pre, self.inner, r4, rb, count, s.gains[4], mask],
            [self.lanes(depth)],
            offset=offset4, offsetb=offsetb, fold=0, frames=frames,
        )
        r3, offset3 = self.sums[3]
        last = wide // lateral
        self.slow_in_grad, self.lateral_pre, reduced_grad, self.lateral_sums = call_steps(
            joined_back_kernel,
            last + 1,
            [(rows, wide), (rows, lateral), (rows, 3 * depth), (self.copies, 2 * lateral)],
            [
                pl.BlockSpec((rows, lateral), lambda j: (0, jnp.minimum(j, last - 1))),
                fixed((rows, lateral)), fixed((rows, 3 * depth)), fixed((self.copies, 2 * lateral)),
            ],
            [
                inner_grad, from_previous(high), from_next(low), skip_grad, s.slow_reduce,
                s.shortcut, mask,
                self.lateral, r3, count, s.gains[3], s.biases[3],
            ],
            [
                fixed((rows, depth)), fixed((places, depth)), fixed((places, depth)),
                fixed((rows, out_wide)), s.slow_reduce.block((3 * depth, lateral), lambda j: (0, j)),
                s.shortcut.block((out_wide, lateral), lambda j: (0, j)), fixed((rows, 128)),
                fixed((rows, lateral)), fixed(r3.shape), fixed((1, 1)), s.gains[3].whole(),
                s.biases[3].whole(),
            ],
            [self.lanes(depth)],
            offset=offset3, frames=frames,
        )
        self.grads["slow_reduce"] = call_steps(
            joined_weight_kernel,
            3,
            [(full // lateral, 3 * depth, lateral)],
            [pl.BlockSpec((full // lateral, depth, lateral), lambda j: (0, j, 0))],
            [reduced_grad, self.slow_in, self.lateral_act],
            [columns(rows, depth), fixed((rows, wide)), fixed((rows, lateral))],
        )[0]

    def fast_backward(self, fast_grad):
        s, mask, frames, rows, places = self.s, self.mask, self.frames, self.rows, self.places
        count, count4 = self.shared["slow"], self.shared["fast"]
        wide, inner, lateral = s.wide, s.inner, s.widths[3]
        width, full = GROUP * inner, GROUP * wide
        rb, offsetb = yield self.lateral_sums
        self.back[3] = (rb, offsetb, offsetb + lateral)
        r3, offset3 = self.sums[3]
        here, low, _ = call(
            norm_back_kernel,
            [(rows, lateral), (places, lateral), (places, lateral)],
            [self.lateral_pre, self.lateral, r3, rb, count, s.gains[3], mask],
            [self.lanes(lateral)],
            offset=offset3, offsetb=offsetb, fold=0, frames=frames,
        )
        r2, offset2 = self.sums[2]
        residual, onward, sums = call(
            lateral_back_kernel,
            [(rows, full), (rows, lateral), (self.copies, 2 * wide)],
            [
                here, from_next(low), fast_grad(), self.third, self.fast_in, r2, count4, s.gains[2],
                s.biases[2], mask, s.lateral,
            ],
            [self.lanes(lateral)],
            offset=offset2, frames=frames,
        )
        self.grads["lateral"] = call(
            lateral_weight_kernel, [(3, lateral, 2 * wide)], [here, onward, self.fast_out]
        )[0]
        rb, offsetb = yield sums
        self.back[2] = (rb, offsetb, offsetb + wide)
        r1, offset1 = self.sums[1]
        third_grad, pre, sums = call(
            fast_expand_back_kernel,
            [(rows, full), (rows, width), (self.copies, 2 * width)],
            [
                residual, self.third, r2, rb, count4, s.gains[2], self.second, r1, s.gains[1],
                s.biases[1], mask, s.fast_expand,
            ],
            offset=offset2, offsetb=offsetb, offsetu=offset1, fold=inner,
        )
        self.grads["fast_expand"] = call(
            fast_expand_weight_kernel,
            [(wide // GROUP, width)],
            [third_grad, self.second_act],
            fold=inner,
        )[0]
        rb, offsetb = yield sums
        self.back[1] = (rb, offsetb, offsetb + width)
        r0, offset0 = self.sums[0]
        second_grad, pre, sums = call(
            conv_back_kernel,
            [(rows, width), (rows, width), (self.copies, 2 * width)],
            [
                pre, self.second, r1, rb, count4, s.gains[1], self.first, r0, s.gains[0], s.biases[0],
                mask, s.fast_spatial,
            ],
            self.window(width),
            offset=offset1, offsetb=offsetb, offsetu=offset0, fold=inner, side=self.side,
            frames=frames,
        )
        self.grads["fast_spatial"] = call(
            conv_weight_kernel,
            [(9 * inner // GROUP, width)],
            [self.first_act, second_grad],
            self.window(width),
            fold=inner, side=self.side, frames=frames,
        )[0]
        rb, offsetb = yield sums
        self.back[0] = (rb, offsetb, offsetb + width)
        first_grad, low, high = call(
            norm_back_kernel,
            [(rows, width), (places, width), (places, width)],
            [pre, self.first, r0, rb, count4, s.gains[0], mask],
            [self.lanes(width)],
            offset=offset0, offsetb=offsetb, fold=inner, frames=frames,
        )
        self.fast_in_grad, self.grads["fast_reduce"] = call(
            fast_first_back_kernel,
            [(rows, full), (3 * inner, wide)],
            [
                first_grad, from_previous(high), from_next(low), residual, s.fast_reduce, mask,
                self.fast_in,
            ],
            [self.lanes(width)] * 2 + [(2 * width, full)],
            frames=frames, inner=inner,
        )

    def blocked(self, name):
        grad = self.grads[name]
        return grad if grad.ndim == 3 else grad[None]

    def fast_flat(self):
        return jnp.concatenate([self.grads[n] for n in ("fast_spatial", "fast_reduce", "fast_expand")])

    def norm_grads(self):
        gains, biases = [], []
        for j, width in enumerate(self.s.widths):
            rb, low, slope = self.back[j]
            span = GROUP * width if j < 2 else width
            for start, found in ((slope, gains), (low, biases)):
                total = jnp.sum(rb[:, start : start + span], axis=0)
                found.append(jnp.sum(total.reshape(-1, width), axis=0))
        return jnp.stack([jnp.concatenate(gains), jnp.concatenate(biases)])


class Task:
    def __init__(self, steps):
        self.steps = steps
        self.wanted = next(steps)

    def resume(self, totals):
        self.wanted = next(self.steps, None) if totals is None else self.send(totals)

    def send(self, totals):
        try:
            return self.steps.send(totals)
        except StopIteration:
            return None


def advance(*tasks, jobs=()):
    wanted = [task.wanted for task in tasks]
    r = sums_everywhere(jnp.concatenate(wanted, axis=1) if len(wanted) > 1 else wanted[0])
    jobs = [job for job in jobs if job.held is not None and not job.waits()]
    if jobs:
        r, held = lax.optimization_barrier((r, [job.held for job in jobs]))
        for job, values in zip(jobs, held):
            job.resume(values)
    offsets = [sum(w.shape[1] for w in wanted[:k]) for k in range(len(wanted))]
    return [(r, offset) for offset in offsets]


def body(
    slow_input,
    fast_input,
    frame_counts,
    fast_reduce,
    fast_spatial,
    fast_expand,
    lateral_conv,
    slow_reduce,
    slow_spatial,
    slow_expand,
    shortcut,
    norm_gain,
    norm_bias,
    slow_cotangent,
    fast_cotangent,
):
    own = lax.axis_index("section")
    lower = own == 0
    frames, positions = slow_input.shape[2], slow_input.shape[4]
    rows = frames * positions
    wide = fast_input.shape[3]

    which = jnp.reshape(own, (1,)).astype(jnp.int32)
    inner, depth = fast_reduce.shape[2], slow_expand.shape[2]
    widths = [
        inner, inner, wide, lateral_conv.shape[2], depth, depth, slow_expand.shape[1], shortcut.shape[1]
    ]
    rows_of = {
        "fast_spatial": jnp.tile(fast_spatial[0], (1, 1, GROUP)).reshape(-1, 128),
        "fast_reduce": fast_reduce[0].reshape(-1, 128),
        "fast_expand": jnp.tile(fast_expand[0], (1, GROUP)),
    }
    sizes = {name: x.shape[0] for name, x in rows_of.items()}
    sizes.update(inner=inner, wide=wide)
    norms = jnp.concatenate([norm_row(norm_gain[0], widths), norm_row(norm_bias[0], widths)])
    small = jnp.concatenate(list(rows_of.values()) + [norms.reshape(-1, 128)])
    small = lax.all_gather(small, "section")
    norms = small[:, small.shape[1] - norms.size // 128 :].reshape(2, 2, 1, -1)
    large = [
        lateral_conv[0],
        slow_reduce[0].reshape(-1, slow_reduce.shape[3]),
        slow_spatial[0],
        slow_expand[0],
        shortcut[0],
    ]
    large = [lax.all_gather(x, "section") for x in large]
    sections = [Section(index, small, norms, sizes, large) for index in range(2)]

    count_here = lax.dynamic_index_in_dim(frame_counts, own, 0, keepdims=False)
    frame = lax.axis_index("clip") * frames + lax.broadcasted_iota(
        jnp.int32, (positions, frames, 128), 1
    )
    mask = (frame < count_here).astype(jnp.float32).reshape(rows, 128)
    shared = {}
    blocks = [Block(section, mask, frames, shared) for section in sections]
    blocks[0].following, blocks[1].following = blocks[1], None

    fast_in, *parts = blocks[0].fast_first(fast_input, which)
    fast = [Task(blocks[0].fast_forward(fast_in, parts)), None]
    got = advance(fast[0])
    r = got[0][0]
    shared["slow"] = jnp.sum(r[:, r.shape[1] - 128 : r.shape[1] - 127], axis=0, keepdims=True)
    shared["fast"] = GROUP * shared["slow"]
    fast[0].resume(got[0])
    for step in range(2):
        fast[0].resume(advance(fast[0])[0])
    fast[1] = Task(blocks[1].fast_forward(blocks[0].fast_out, blocks[0].parts))
    got = advance(fast[0], fast[1])
    fast[0].resume(got[0])
    fast[1].resume(got[1])
    slow = [Task(blocks[0].slow_forward(load_rows(slow_input, mask, which))), None]
    for step in range(3):
        got = advance(slow[0], fast[1])
        slow[0].resume(got[0])
        fast[1].resume(got[1])
    slow[1] = Task(blocks[1].slow_forward(blocks[0].slow_out))
    out_fast = Job(worked([place_packed(blocks[0].fast_out, blocks[1].fast_out, which, frames)]))
    for step in range(3):
        slow[1].resume(advance(slow[1], jobs=[out_fast] if step == 0 else [])[0])

    zero, one = blocks
    ways = routes()
    jobs = []
    early_names, late_names = ("shortcut", "slow_expand"), ("slow_spatial", "slow_reduce", "lateral")

    def start(steps, paces=(1,)):
        jobs.append(Job(steps, paces))
        return jobs[-1]

    tasks = Task(one.slow_backward(load_rows(slow_cotangent, mask, which)))
    tasks.resume(advance(tasks)[0])
    start(held_grads(one, early_names))
    tasks.resume(advance(tasks, jobs=jobs)[0])
    start(held_grads(one, ("slow_spatial",)))
    tasks.resume(advance(tasks, jobs=jobs)[0])
    start(held_grads(one, ("slow_reduce",)))
    late = Task(one.fast_backward(lambda: load_packed(fast_cotangent, which)))
    soon = Task(zero.slow_backward(one.slow_in_grad))
    for step in range(3):
        got = advance(late, soon, jobs=jobs)
        late.resume(got[0])
        soon.resume(got[1])
        if step == 0:
            held_one = start(held_grads(one, ("lateral",)))
            early = start(reduction([zero.blocked(n) for n in early_names], ways[2]), PLANS[1])
        if step == 1:
            groups = [[one.blocked(n) for n in names] for names in (early_names, late_names)]
            whole = start(summed(groups), PLANS[0])
            start(held_grads(zero, ("slow_spatial",)))
        if step == 2:
            start(held_grads(zero, ("slow_reduce",)))
    last = Task(zero.fast_backward(lambda: one.fast_in_grad))
    got = advance(late, last, jobs=jobs)
    late.resume(got[0])
    last.resume(got[1])
    late_job = start(reduction([zero.blocked(n) for n in late_names], ways[0]), PLANS[2])
    late_job.resume(late_job.held)
    for step in range(3):
        last.resume(advance(last, jobs=jobs)[0])
    rest = Job(small_reduction(jnp.concatenate([zero.fast_flat(), one.fast_flat()]))).finish()

    totals = {}
    highs = whole.finish()
    highs, zero.fast_in_grad = lax.optimization_barrier((highs, zero.fast_in_grad))
    low, high = early.finish(), highs[0]
    totals["shortcut"], totals["slow_expand"] = place_weights(
        place_early_kernel, low, high, slow_expand.shape[1] // 2, which,
        [shortcut.shape[1:], slow_expand.shape[1:]],
    )
    low, high = late_job.finish(), highs[1]
    totals["slow_spatial"], totals["slow_reduce"], totals["lateral"] = place_weights(
        place_late_kernel, low, high, depth // 2, which,
        [slow_spatial.shape[1:], (3 * depth, slow_reduce.shape[3]), lateral_conv.shape[1:]],
    )
    half = rest.shape[0] // 2
    flat, cursor = jnp.where(lower, rest[:half], rest[half:]), 0
    for name in ("fast_spatial", "fast_reduce", "fast_expand"):
        size = sizes[name] if name == "fast_reduce" else sizes[name] // GROUP
        piece = flat[cursor : cursor + size]
        if name != "fast_reduce":
            count = inner if name == "fast_spatial" else wide
            piece = piece.reshape(-1, count // GROUP, GROUP, inner)
            piece = jnp.swapaxes(piece, 1, 2)
        totals[name] = piece
        cursor += size
    names = (
        "fast_reduce",
        "fast_spatial",
        "fast_expand",
        "lateral",
        "slow_reduce",
        "slow_spatial",
        "slow_expand",
        "shortcut",
    )
    norm_grads = [block.norm_grads() for block in blocks]
    kept = jnp.where(lower, norm_grads[0], norm_grads[1])
    kept = kept + swap(jnp.where(lower, norm_grads[1], norm_grads[0]))
    shapes = [
        x.shape
        for x in (
            fast_reduce, fast_spatial, fast_expand, lateral_conv, slow_reduce, slow_spatial,
            slow_expand, shortcut,
        )
    ]
    totals = [totals[name].reshape(shape) for name, shape in zip(names, shapes)]
    return (
        place_rows(zero.slow_out, one.slow_out, which, frames),
        out_fast.finish()[0],
        place_rows(zero.slow_in_grad, one.slow_in_grad, which, frames),
        place_packed(zero.fast_in_grad, one.fast_in_grad, which, frames),
        *totals,
        kept[None, 0],
        kept[None, 1],
    )


def solution(mesh):
    acts = P(None, "tm", "clip", None, None)
    outs = P("section", None, "tm", "clip", None, None)
    four, three, two = P("section", None, None, None), P("section", None, None), P("section", None)
    weights = (four, four, three, four, four, four, three, three)
    return jax.shard_map(
        body,
        mesh=mesh,
        in_specs=(acts, acts, P(None, "tm"), *weights, two, two, acts, acts),
        out_specs=(outs, outs, outs, outs, *weights, two, two),
        check_vma=False,
    )
```

```python
from functools import partial
import math

import jax
import jax.numpy as jnp
from jax import lax
from jax.experimental import pallas as pl
from jax.experimental.pallas import tpu as pltpu
from jax.sharding import PartitionSpec as P

EPSILON = 1e-05
PLANS = ((0, 0, 0, 0, 0, 0), (1, 2, 2, 2, 2, 0), (2, 3, 3, 0))
FINE = lax.Precision.HIGH
GROUP = 4
AXES = ("clip", "tm")
NORM_ORDER = (2, 0, 1, 3, 4, 5, 6, 7)


def dot_nn(a, b):
    return lax.dot_general(a, b, (((1,), (0,)), ((), ())), precision=FINE)


def dot_nt(a, b):
    return lax.dot_general(a, b, (((1,), (1,)), ((), ())), precision=FINE)


def dot_tn(a, b):
    return lax.dot_general(a, b, (((0,), (0,)), ((), ())), precision=FINE)


def sums_everywhere(vector):
    return lax.all_to_all(vector, AXES, 0, 0)


def from_previous(edge):
    count = lax.axis_size("clip")
    return lax.ppermute(edge, "clip", [(i, i + 1) for i in range(count - 1)])


def from_next(edge):
    count = lax.axis_size("clip")
    return lax.ppermute(edge, "clip", [(i + 1, i) for i in range(count - 1)])


def swap(values):
    return lax.ppermute(values, "section", [(0, 1), (1, 0)])


def silu(v):
    return v * jax.nn.sigmoid(v)


def silu_slope(v):
    s = jax.nn.sigmoid(v)
    return s * (1.0 + v * (1.0 - s))


VMEM_BYTES = 36 * 2**20


def rowwise(mask, width):
    return jnp.concatenate([mask] * (width // mask.shape[1]), axis=1)


def moments(r_ref, offset, width, count, fold=0):
    total = jnp.sum(r_ref[:, offset : offset + width], axis=0, keepdims=True)
    square = jnp.sum(r_ref[:, offset + width : offset + 2 * width], axis=0, keepdims=True)
    if fold:
        total, square = around(total, fold), around(square, fold)
    mean = total / count
    return mean, lax.rsqrt(square / count - mean * mean + EPSILON)


def around(row, fold):
    out = row
    for step in range(fold, row.shape[1], fold):
        out = out + pltpu.roll(row, step, 1)
    return out


def repeat(row, times):
    return row if times == 1 else jnp.concatenate([row] * times, axis=1)


def put_sums(st_ref, start, row):
    st_ref[:, start : start + row.shape[1]] = jnp.broadcast_to(row, (st_ref.shape[0], row.shape[1]))


def put_part(st_ref, offset, row):
    width = row.shape[1]
    start = pl.multiple_of(offset + pl.program_id(0) * width, 128)
    st_ref[:, pl.ds(start, width)] = jnp.broadcast_to(row, (st_ref.shape[0], width))


def folded(row, fold):
    width = row.shape[1] // fold
    return sum(row[:, k * width : (k + 1) * width] for k in range(fold))


def store_sums(st_ref, values, mask, fold=1):
    weighted = values * mask
    total = folded(jnp.sum(weighted, axis=0, keepdims=True), fold)
    put_sums(st_ref, 0, total)
    square = folded(jnp.sum(weighted * values, axis=0, keepdims=True), fold)
    put_sums(st_ref, total.shape[1], square)


class Stacked:
    def __init__(self, both, index):
        self.both, self.index, self.shape = both, index, both.shape[1:]

    def block(self, shape, place):
        def where(*step):
            return (self.index,) + place(*step)

        return pl.BlockSpec((None,) + shape, where)

    def whole(self):
        zeros = (0,) * len(self.shape)
        return self.block(self.shape, lambda *step: zeros)


class Window:
    def __init__(self, both, place, offset, shape):
        self.both, self.place, self.offset, self.shape = both, place, offset, shape

    def whole(self):
        lead = (None,) * len(self.place)
        if self.shape[0] == 1:
            where = self.place + (0, self.offset // self.shape[1])
        else:
            where = self.place + (self.offset // self.shape[0], 0)
        return pl.BlockSpec(lead + self.shape, lambda *step: where)

    def parts(self, width):
        lead = (None,) * len(self.place)
        first = self.offset // width
        return pl.BlockSpec(lead + (1, width), lambda j: self.place + (0, first + j))


def array_of(value):
    if isinstance(value, Stacked):
        return pltpu.with_memory_space_constraint(value.both, pltpu.HBM)
    return value.both if isinstance(value, Window) else value


def call(kernel, outs, ins, scratch=(), **static):
    vmem = pl.BlockSpec(memory_space=pltpu.VMEM)
    return pl.pallas_call(
        partial(kernel, **static),
        grid=(1,),
        out_shape=[jax.ShapeDtypeStruct(s, jnp.float32) for s in outs],
        in_specs=[x.whole() if isinstance(x, (Stacked, Window)) else vmem for x in ins],
        out_specs=[vmem] * len(outs),
        scratch_shapes=[pltpu.VMEM(s, jnp.float32) for s in scratch],
        compiler_params=pltpu.CompilerParams(vmem_limit_bytes=VMEM_BYTES),
    )(*[array_of(x) for x in ins])


def fixed(shape):
    return pl.BlockSpec(shape, lambda j: (0,) * len(shape))


def columns(rows, width):
    return pl.BlockSpec((rows, width), lambda j: (0, j))


def bands(height, width):
    return pl.BlockSpec((height, width), lambda j: (j, 0))


def streamed(value, spec):
    value = array_of(value)
    pieces = [n for n in spec.block_shape if n is not None]
    if math.prod(pieces) < value.size and value.size * 4 > 2**20:
        return pltpu.with_memory_space_constraint(value, pltpu.HBM)
    return value


def result(shape, spec):
    pieces = [n for n in spec.block_shape if n is not None]
    if math.prod(pieces) < math.prod(shape) and math.prod(shape) * 4 > 2**20:
        return pltpu.HBM(shape, jnp.float32)
    return jax.ShapeDtypeStruct(shape, jnp.float32)


def call_steps(kernel, steps, outs, out_specs, ins, in_specs, scratch=(), **static):
    return pl.pallas_call(
        partial(kernel, **static),
        grid=(steps,),
        out_shape=[result(shape, spec) for shape, spec in zip(outs, out_specs)],
        in_specs=in_specs,
        out_specs=out_specs,
        scratch_shapes=[pltpu.VMEM(s, jnp.float32) for s in scratch],
        compiler_params=pltpu.CompilerParams(
            dimension_semantics=("arbitrary",), vmem_limit_bytes=VMEM_BYTES
        ),
    )(*[streamed(x, spec) for x, spec in zip(ins, in_specs)])


def take_rows(out_ref, values, first, frames, scratch):
    for k in range(out_ref.shape[1] // 128):
        scratch[k] = values[:, k * 128 : (k + 1) * 128]
        out_ref[:, k * 128 : (k + 1) * 128] = scratch[k, pl.ds(first, out_ref.shape[0], stride=frames), :]


def put_rows(values, first, frames, edge, scratch):
    pieces = []
    for k in range(edge.shape[1] // 128):
        scratch[k] = values[:, k * 128 : (k + 1) * 128]
        scratch[k, pl.ds(first, edge.shape[0], stride=frames), :] = edge[:, k * 128 : (k + 1) * 128]
        pieces.append(scratch[k])
    return jnp.concatenate(pieces, axis=1) if len(pieces) > 1 else pieces[0]


def before_rows(scratch, values, edge, frames):
    return put_rows(pltpu.roll(values, 1, 0), 0, frames, edge, scratch)


def after_rows(scratch, values, edge, frames):
    return put_rows(pltpu.roll(values, values.shape[0] - 1, 0), frames - 1, frames, edge, scratch)


def banded(w_ref, matrix):
    taps, wide = 3, w_ref.shape[1]
    inner = w_ref.shape[0] // taps
    matrix[...] = jnp.zeros(matrix.shape, jnp.float32)
    for q in range(GROUP):
        for k in range(taps):
            r = q + k - 1
            start = q * inner + (0 if 0 <= r < GROUP else GROUP * inner)
            r = r % GROUP
            matrix[start : start + inner, r * wide : (r + 1) * wide] = w_ref[k * inner : (k + 1) * inner]
    return matrix[...]


def diagonal(tile, inner):
    frame = lax.broadcasted_iota(jnp.int32, (1, tile.shape[1]), 1) // inner
    return jnp.concatenate([jnp.where(frame == r, tile, 0.0) for r in range(GROUP)], axis=0)


def undiagonal(square, inner):
    count = square.shape[0] // GROUP
    frame = lax.broadcasted_iota(jnp.int32, (1, square.shape[1]), 1) // inner
    total = sum(
        jnp.where(frame == r, square[r * count : (r + 1) * count], 0.0) for r in range(GROUP)
    )
    total = around(total, inner)
    count = count // GROUP
    return sum(
        jnp.where(frame == r, total[r * count : (r + 1) * count], 0.0) for r in range(GROUP)
    )


def tap(k_ref, k, inner):
    if not inner:
        return k_ref[k]
    return diagonal(k_ref[k * inner : (k + 1) * inner], inner)


def fast_first_kernel(
    own_ref, x_ref, m_ref, w_ref, x_out, y_ref, low_ref, high_ref, scratch, matrix, *, frames
):
    rows, wide = m_ref.shape[0], x_ref.shape[1]
    for r in range(GROUP):
        x_out[:, r * wide : (r + 1) * wide] = (
            x_ref[pl.ds(r, rows, stride=GROUP), :] * rowwise(m_ref[...], wide)
        )
    y = dot_nt(x_out[...], banded(w_ref, matrix))
    y_ref[...] = y
    take_rows(low_ref, y[:, y.shape[1] // 2 :], 0, frames, scratch)
    take_rows(high_ref, y[:, y.shape[1] // 2 :], frames - 1, frames, scratch)


def fast_join_kernel(y_ref, p_ref, n_ref, m_ref, o_ref, st_ref, sp_ref, sn_ref, *, frames, inner):
    width = o_ref.shape[1]
    edge = y_ref[:, width:]
    before = before_rows(sp_ref, edge, p_ref[...], frames)
    after = after_rows(sn_ref, edge, n_ref[...], frames)
    lane = lax.broadcasted_iota(jnp.int32, (1, width), 1)
    out = y_ref[:, :width] + jnp.where(
        lane < inner, before, jnp.where(lane >= width - inner, after, 0.0)
    )
    o_ref[...] = out
    store_sums(st_ref, out, m_ref[...])
    put_sums(st_ref, 2 * width, jnp.sum(m_ref[...], axis=0, keepdims=True))


def fill_shifts(values, x0, xl, xr, side, frames):
    rows, width = values.shape
    pad = (x0.shape[0] - rows) // 2
    blank = jnp.zeros((pad + 8, width), jnp.float32)
    for ref in (x0, xl, xr):
        ref[0 : pad + 8] = blank
        ref[pad + rows - 8 : 2 * pad + rows] = blank
    row = lax.broadcasted_iota(jnp.int32, (rows, 1), 0)
    column = lax.rem(lax.div(row, frames), side)
    x0[pad : pad + rows] = values
    xl[pad + frames : pad + frames + rows] = jnp.where(column == side - 1, 0.0, values)
    xr[pad - frames : pad - frames + rows] = jnp.where(column == 0, 0.0, values)


def shifted(k, x0, xl, xr, rows, side, frames):
    pad = (x0.shape[0] - rows) // 2
    start = pad + (k // 3 - 1) * side * frames
    return (xl, x0, xr)[k % 3][start : start + rows]


def conv_kernel(
    v_ref, r_ref, c_ref, g_ref, b_ref, m_ref, k_ref, o_ref, act_ref, st_ref, x0, xl, xr,
    *, offset, fold, side, frames
):
    rows, width = v_ref.shape
    mean, rstd = moments(r_ref, offset, width, c_ref[...], fold)
    mask = rowwise(m_ref[...], width)
    act = mask * silu(g_ref[...] * ((v_ref[...] - mean) * rstd) + b_ref[...])
    act_ref[...] = act
    fill_shifts(act, x0, xl, xr, side, frames)
    total = dot_nt(shifted(0, x0, xl, xr, rows, side, frames), tap(k_ref, 0, fold))
    for k in range(1, 9):
        total += dot_nt(shifted(k, x0, xl, xr, rows, side, frames), tap(k_ref, k, fold))
    o_ref[...] = total
    store_sums(st_ref, total, rowwise(m_ref[...], total.shape[1]))


def fast_expand_kernel(
    v_ref, r_ref, c_ref, g_ref, b_ref, m_ref, w_ref, o_ref, act_ref, st_ref, *, offset, fold
):
    width = v_ref.shape[1]
    mean, rstd = moments(r_ref, offset, width, c_ref[...], fold)
    act = rowwise(m_ref[...], width) * silu(g_ref[...] * ((v_ref[...] - mean) * rstd) + b_ref[...])
    act_ref[...] = act
    out = dot_nt(act, diagonal(w_ref[...], fold))
    o_ref[...] = out
    store_sums(st_ref, out, rowwise(m_ref[...], out.shape[1]), GROUP)


def fast_out_kernel(
    v_ref, x_ref, r_ref, c_ref, g_ref, b_ref, m_ref, l_ref, w_ref,
    out_ref, here_ref, next_ref, edge_ref, y_ref, low_ref, high_ref, scratch, matrix, *, offset, frames, more
):
    width = v_ref.shape[1]
    wide = width // GROUP
    mean, rstd = moments(r_ref, offset, wide, c_ref[...])
    mean, rstd = repeat(mean, GROUP), repeat(rstd, GROUP)
    pre = g_ref[...] * ((v_ref[...] - mean) * rstd) + b_ref[...] + x_ref[...]
    out = rowwise(m_ref[...], width) * silu(pre)
    out_ref[...] = out
    one, two, three, four = [out[:, r * wide : (r + 1) * wide] for r in range(GROUP)]
    here_ref[...] = dot_nt(one, l_ref[2]) + dot_nt(two, l_ref[3]) + dot_nt(three, l_ref[4])
    onward = dot_nt(three, l_ref[0]) + dot_nt(four, l_ref[1])
    next_ref[...] = onward
    take_rows(edge_ref, onward, frames - 1, frames, scratch)
    if more:
        y = dot_nt(out, banded(w_ref, matrix))
        y_ref[...] = y
        half = y.shape[1] // 2
        take_rows(low_ref, y[:, half:], 0, frames, scratch)
        take_rows(high_ref, y[:, half:], frames - 1, frames, scratch)
    else:
        for ref in (y_ref, low_ref, high_ref):
            ref[...] = jnp.zeros(ref.shape, jnp.float32)


def lateral_join_kernel(h_ref, n_ref, e_ref, m_ref, o_ref, st_ref, sp_ref, *, frames):
    out = h_ref[...] + before_rows(sp_ref, n_ref[...], e_ref[...], frames)
    o_ref[...] = out
    store_sums(st_ref, out, rowwise(m_ref[...], out.shape[1]))


def reduce_kernel(
    x_ref, v_ref, r_ref, c_ref, g_ref, b_ref, m_ref, w_ref, y_ref, low_ref, high_ref, act_ref, joined,
    scratch, *, offset, frames
):
    step = pl.program_id(0)
    wide, lateral = x_ref.shape[1], v_ref.shape[1]

    @pl.when(step == 0)
    def _():
        mean, rstd = moments(r_ref, offset, lateral, c_ref[...])
        joined[:, :wide] = x_ref[...]
        act = silu(g_ref[...] * ((v_ref[...] - mean) * rstd) + b_ref[...])
        act = act * rowwise(m_ref[...], lateral)
        joined[:, wide:] = act
        act_ref[...] = act

    y = dot_nt(joined[...], w_ref[...])
    y_ref[...] = y

    @pl.when(step == 0)
    def _():
        take_rows(high_ref, y, frames - 1, frames, scratch)

    @pl.when(step == 2)
    def _():
        take_rows(low_ref, y, 0, frames, scratch)


def shortcut_kernel(x_ref, a_ref, m_ref, w_ref, y_ref, st_ref):
    wide = x_ref.shape[1]
    out = dot_nt(x_ref[...], w_ref[:, :wide])
    out += dot_nt(a_ref[...], w_ref[:, wide:])
    y_ref[...] = out
    weighted = out * rowwise(m_ref[...], out.shape[1])
    put_part(st_ref, 0, jnp.sum(weighted, axis=0, keepdims=True))
    put_part(st_ref, st_ref.shape[1] // 2, jnp.sum(weighted * out, axis=0, keepdims=True))


def inner_join_kernel(y_ref, p_ref, n_ref, m_ref, o_ref, st_ref, sp_ref, sn_ref, *, frames):
    depth = o_ref.shape[1]
    out = y_ref[:, depth : 2 * depth]
    out += before_rows(sp_ref, y_ref[:, :depth], p_ref[...], frames)
    out += after_rows(sn_ref, y_ref[:, 2 * depth : 3 * depth], n_ref[...], frames)
    o_ref[...] = out
    store_sums(st_ref, out, rowwise(m_ref[...], depth))


def expand_kernel(
    v_ref, r_ref, c_ref, g_ref, b_ref, m_ref, w_ref, o_ref, act_ref, st_ref, *, offset
):
    width = v_ref.shape[1]

    @pl.when(pl.program_id(0) == 0)
    def _():
        mean, rstd = moments(r_ref, offset, width, c_ref[...])
        act = silu(g_ref[...] * ((v_ref[...] - mean) * rstd) + b_ref[...])
        act_ref[...] = act * rowwise(m_ref[...], width)

    out = dot_nt(act_ref[...], w_ref[...])
    o_ref[...] = out
    weighted = out * rowwise(m_ref[...], out.shape[1])
    put_part(st_ref, 0, jnp.sum(weighted, axis=0, keepdims=True))
    put_part(st_ref, st_ref.shape[1] // 2, jnp.sum(weighted * out, axis=0, keepdims=True))


def slow_out_kernel(
    e_ref, k_ref, r6_ref, r7_ref, c_ref, g6_ref, b6_ref, g7_ref, b7_ref, m_ref, o_ref,
    *, offset6, offset7, total
):
    pre, _, _ = slow_pre(
        e_ref, k_ref, r6_ref, r7_ref, c_ref, g6_ref, b6_ref, g7_ref, b7_ref, offset6, offset7, total
    )
    o_ref[...] = rowwise(m_ref[...], pre.shape[1]) * silu(pre)


def part(r_ref, offset, width):
    start = pl.multiple_of(offset + pl.program_id(0) * width, 128)
    return jnp.sum(r_ref[:, pl.ds(start, width)], axis=0, keepdims=True)


def moments_part(r_ref, offset, total, width, count):
    mean = part(r_ref, offset, width) / count
    square = part(r_ref, offset + total, width) / count
    return mean, lax.rsqrt(square - mean * mean + EPSILON)


def slow_pre(
    e_ref, k_ref, r6_ref, r7_ref, c_ref, g6_ref, b6_ref, g7_ref, b7_ref, offset6, offset7, total
):
    width = e_ref.shape[1]
    mean6, rstd6 = moments_part(r6_ref, offset6, total, width, c_ref[...])
    mean7, rstd7 = moments_part(r7_ref, offset7, total, width, c_ref[...])
    n6 = (e_ref[...] - mean6) * rstd6
    n7 = (k_ref[...] - mean7) * rstd7
    pre = (g6_ref[...] * n6 + b6_ref[...]) + (g7_ref[...] * n7 + b7_ref[...])
    return pre, (n6, rstd6), (n7, rstd7)


def slow_slope_kernel(
    d_ref, e_ref, k_ref, r6_ref, r7_ref, c_ref, g6_ref, b6_ref, g7_ref, b7_ref, m_ref,
    p_ref, st_ref, *, offset6, offset7, total
):
    pre, (n6, _), (n7, _) = slow_pre(
        e_ref, k_ref, r6_ref, r7_ref, c_ref, g6_ref, b6_ref, g7_ref, b7_ref, offset6, offset7, total
    )
    grad = rowwise(m_ref[...], pre.shape[1]) * d_ref[...] * silu_slope(pre)
    p_ref[...] = grad
    put_part(st_ref, 0, jnp.sum(grad, axis=0, keepdims=True))
    put_part(st_ref, total, jnp.sum(grad * n6, axis=0, keepdims=True))
    put_part(st_ref, 2 * total, jnp.sum(grad * n7, axis=0, keepdims=True))


def expand_back_kernel(
    p_ref, e_ref, k_ref, r6_ref, r7_ref, rb_ref, c_ref, g6_ref, g7_ref, m_ref, w_ref, act_ref,
    v_ref, r5_ref, g5_ref, b5_ref,
    skip_ref, dw_ref, o_ref, st_ref, acc, *, offset6, offset7, offsetb, offset5, total
):
    step, steps = pl.program_id(0), pl.num_programs(0)
    width, depth = p_ref.shape[1], v_ref.shape[1]
    count, mask = c_ref[...], rowwise(m_ref[...], width)
    mean6, rstd6 = moments_part(r6_ref, offset6, total, width, count)
    mean7, rstd7 = moments_part(r7_ref, offset7, total, width, count)
    low = part(rb_ref, offsetb, width) / count
    q6 = part(rb_ref, offsetb + total, width) / count
    q7 = part(rb_ref, offsetb + 2 * total, width) / count
    pre = p_ref[...]
    grad = mask * ((g6_ref[...] * rstd6) * (pre - low - (e_ref[...] - mean6) * rstd6 * q6))
    skip_ref[...] = mask * ((g7_ref[...] * rstd7) * (pre - low - (k_ref[...] - mean7) * rstd7 * q7))
    dw_ref[...] = dot_tn(grad, act_ref[...])
    product = dot_nn(grad, w_ref[...])

    @pl.when(step == 0)
    def _():
        acc[...] = product

    @pl.when(step > 0)
    def _():
        acc[...] += product

    @pl.when(step == steps - 1)
    def _():
        mean, rstd = moments(r5_ref, offset5, depth, count)
        normed = (v_ref[...] - mean) * rstd
        out = rowwise(m_ref[...], depth) * acc[...]
        out = out * silu_slope(g5_ref[...] * normed + b5_ref[...])
        o_ref[...] = out
        store_back_sums(st_ref, out, normed)


def store_weight(dw_ref, grad, x_ref, a_ref):
    count, _, width = dw_ref.shape
    for k in range(count - 1):
        dw_ref[k] = dot_tn(grad, x_ref[:, k * width : (k + 1) * width])
    dw_ref[count - 1] = dot_tn(grad, a_ref[...])


def back_sums(rb_ref, offset, width, count, fold=0):
    low = jnp.sum(rb_ref[:, offset : offset + width], axis=0, keepdims=True)
    slope = jnp.sum(rb_ref[:, offset + width : offset + 2 * width], axis=0, keepdims=True)
    if fold:
        low, slope = around(low, fold), around(slope, fold)
    return low / count, slope / count


def norm_back(pre, values, mean, rstd, gain, low, slope, mask):
    return mask * ((gain * rstd) * (pre - low - (values - mean) * rstd * slope))


def store_back_sums(st_ref, grad, normed, fold=1):
    low = folded(jnp.sum(grad, axis=0, keepdims=True), fold)
    put_sums(st_ref, 0, low)
    put_sums(st_ref, low.shape[1], folded(jnp.sum(grad * normed, axis=0, keepdims=True), fold))


def conv_back_kernel(
    p_ref, v_ref, r_ref, rb_ref, c_ref, g_ref, u_ref, ru_ref, gu_ref, bu_ref, m_ref, k_ref,
    d_ref, o_ref, st_ref, x0, xl, xr, *, offset, offsetb, offsetu, fold, side, frames
):
    rows, width = v_ref.shape
    count, mask = c_ref[...], rowwise(m_ref[...], width)
    mean, rstd = moments(r_ref, offset, width, count, fold)
    low, slope = back_sums(rb_ref, offsetb, width, count, fold)
    grad = norm_back(p_ref[...], v_ref[...], mean, rstd, g_ref[...], low, slope, mask)
    d_ref[...] = grad
    fill_shifts(grad, x0, xl, xr, side, frames)
    total = dot_nn(shifted(0, x0, xl, xr, rows, side, frames), tap(k_ref, 8, fold))
    for k in range(1, 9):
        total += dot_nn(shifted(k, x0, xl, xr, rows, side, frames), tap(k_ref, 8 - k, fold))
    mean, rstd = moments(ru_ref, offsetu, u_ref.shape[1], count, fold)
    normed = (u_ref[...] - mean) * rstd
    out = rowwise(m_ref[...], u_ref.shape[1]) * total
    out = out * silu_slope(gu_ref[...] * normed + bu_ref[...])
    o_ref[...] = out
    store_back_sums(st_ref, out, normed)


def conv_weight_kernel(x_ref, d_ref, dw_ref, x0, xl, xr, *, fold, side, frames):
    rows = x_ref.shape[0]
    fill_shifts(x_ref[...], x0, xl, xr, side, frames)
    grad = d_ref[...]
    for k in range(9):
        out = dot_tn(grad, shifted(k, x0, xl, xr, rows, side, frames))
        if fold:
            out = undiagonal(out, fold)
            dw_ref[k * out.shape[0] : (k + 1) * out.shape[0]] = out
        else:
            dw_ref[k] = out


def norm_back_kernel(
    p_ref, v_ref, r_ref, rb_ref, c_ref, g_ref, m_ref, o_ref, low_ref, high_ref, scratch,
    *, offset, offsetb, fold, frames
):
    width = v_ref.shape[1]
    count = c_ref[...]
    mean, rstd = moments(r_ref, offset, width, count, fold)
    low, slope = back_sums(rb_ref, offsetb, width, count, fold)
    mask = rowwise(m_ref[...], width)
    out = norm_back(p_ref[...], v_ref[...], mean, rstd, g_ref[...], low, slope, mask)
    o_ref[...] = out
    take_rows(low_ref, out, 0, frames, scratch)
    take_rows(high_ref, out, frames - 1, frames, scratch)


def joined_back_kernel(
    d_ref, p_ref, n_ref, k_ref, w_ref, wk_ref, m_ref, v_ref, r_ref, c_ref, g_ref, b_ref,
    x_ref, o_ref, all_ref, st_ref, scratch, *, offset, frames
):
    step, steps = pl.program_id(0), pl.num_programs(0)
    depth = d_ref.shape[1]

    @pl.when(step == 0)
    def _():
        grad = d_ref[...]
        all_ref[:, :depth] = after_rows(scratch, grad, n_ref[...], frames)
        all_ref[:, depth : 2 * depth] = grad
        all_ref[:, 2 * depth :] = before_rows(scratch, grad, p_ref[...], frames)

    mask = rowwise(m_ref[...], o_ref.shape[1])
    out = mask * (dot_nn(all_ref[...], w_ref[...]) + dot_nn(k_ref[...], wk_ref[...]))

    @pl.when(step < steps - 1)
    def _():
        x_ref[...] = out

    @pl.when(step == steps - 1)
    def _():
        mean, rstd = moments(r_ref, offset, v_ref.shape[1], c_ref[...])
        normed = (v_ref[...] - mean) * rstd
        grad = out * silu_slope(g_ref[...] * normed + b_ref[...])
        o_ref[...] = grad
        store_back_sums(st_ref, grad, normed)


def joined_weight_kernel(d_ref, x_ref, a_ref, dw_ref):
    store_weight(dw_ref, d_ref[...], x_ref, a_ref)


def lateral_back_kernel(
    d_ref, n_ref, f_ref, v_ref, x_ref, r_ref, c_ref, g_ref, b_ref, m_ref, l_ref,
    o_ref, on_ref, st_ref, scratch, *, offset, frames
):
    width = v_ref.shape[1]
    wide = width // GROUP
    here = d_ref[...]
    onward = after_rows(scratch, here, n_ref[...], frames)
    on_ref[...] = onward
    back = jnp.concatenate(
        [
            dot_nn(here, l_ref[2]),
            dot_nn(here, l_ref[3]),
            dot_nn(here, l_ref[4]) + dot_nn(onward, l_ref[0]),
            dot_nn(onward, l_ref[1]),
        ],
        axis=1,
    )
    mean, rstd = moments(r_ref, offset, wide, c_ref[...])
    normed = (v_ref[...] - repeat(mean, GROUP)) * repeat(rstd, GROUP)
    mask = rowwise(m_ref[...], width)
    pre = g_ref[...] * normed + b_ref[...] + x_ref[...]
    grad = mask * (f_ref[...] + back) * silu_slope(pre)
    o_ref[...] = grad
    store_back_sums(st_ref, grad, normed, GROUP)


def lateral_weight_kernel(d_ref, on_ref, x_ref, dw_ref):
    wide = dw_ref.shape[2] // 2
    here, onward = d_ref[...], on_ref[...]
    for k, (grad, r) in enumerate(((onward, 2), (onward, 3), (here, 0), (here, 1), (here, 2))):
        side = (k % 2) * wide
        dw_ref[k // 2, :, side : side + wide] = dot_tn(grad, x_ref[:, r * wide : (r + 1) * wide])
    dw_ref[2, :, wide:] = jnp.zeros((dw_ref.shape[1], wide), jnp.float32)


def fast_expand_back_kernel(
    p_ref, v_ref, r_ref, rb_ref, c_ref, g_ref, u_ref, ru_ref, gu_ref, bu_ref, m_ref, w_ref,
    d_ref, o_ref, st_ref, *, offset, offsetb, offsetu, fold
):
    width = v_ref.shape[1]
    wide, inner = width // GROUP, u_ref.shape[1]
    count = c_ref[...]
    mean, rstd = moments(r_ref, offset, wide, count)
    low, slope = back_sums(rb_ref, offsetb, wide, count)
    mean, rstd, low, slope = [repeat(row, GROUP) for row in (mean, rstd, low, slope)]
    mask = rowwise(m_ref[...], width)
    grad = norm_back(p_ref[...], v_ref[...], mean, rstd, g_ref[...], low, slope, mask)
    d_ref[...] = grad
    mean, rstd = moments(ru_ref, offsetu, inner, count, fold)
    normed = (u_ref[...] - mean) * rstd
    out = rowwise(m_ref[...], inner) * dot_nn(grad, diagonal(w_ref[...], fold))
    out = out * silu_slope(gu_ref[...] * normed + bu_ref[...])
    o_ref[...] = out
    store_back_sums(st_ref, out, normed)


def fast_expand_weight_kernel(d_ref, x_ref, dw_ref, *, fold):
    dw_ref[...] = undiagonal(dot_tn(d_ref[...], x_ref[...]), fold)


def fast_first_back_kernel(
    d_ref, p_ref, n_ref, res_ref, w_ref, m_ref, x_ref, o_ref, dw_ref, sp_ref, sn_ref,
    matrix, *, frames, inner
):
    grad = d_ref[...]
    width = grad.shape[1]
    before = before_rows(sp_ref, grad, p_ref[...], frames)
    after = after_rows(sn_ref, grad, n_ref[...], frames)
    lane = lax.broadcasted_iota(jnp.int32, (1, width), 1)
    edge = jnp.where(lane < inner, after, jnp.where(lane >= width - inner, before, 0.0))
    both = jnp.concatenate([grad, edge], axis=1)
    mask = rowwise(m_ref[...], o_ref.shape[1])
    o_ref[...] = mask * (dot_nn(both, banded(w_ref, matrix)) + res_ref[...])
    full = dot_tn(both, x_ref[...])
    wide = full.shape[1] // GROUP
    for k in range(3):
        total = None
        for q in range(GROUP):
            r = q + k - 1
            start = q * inner + (0 if 0 <= r < GROUP else GROUP * inner)
            r = r % GROUP
            piece = full[start : start + inner, r * wide : (r + 1) * wide]
            total = piece if total is None else total + piece
        dw_ref[k * inner : (k + 1) * inner] = total


def load_rows_kernel(own_ref, x_ref, m_ref, o_ref):
    o_ref[...] = x_ref[...].reshape(o_ref.shape) * rowwise(m_ref[...], o_ref.shape[1])


def load_packed_kernel(own_ref, x_ref, o_ref):
    wide = x_ref.shape[1]
    for r in range(GROUP):
        o_ref[:, r * wide : (r + 1) * wide] = x_ref[pl.ds(r, o_ref.shape[0], stride=GROUP), :]


def place_rows_kernel(own_ref, a_ref, b_ref, c_ref, d_ref, o_ref):
    for slot, refs in ((0, (a_ref, c_ref)), (1, (b_ref, d_ref))):
        for own in range(2):

            @pl.when((pl.program_id(0) == slot) & (own_ref[0] == own))
            def _():
                o_ref[...] = refs[own][...].reshape(o_ref.shape)


def place_packed_kernel(own_ref, a_ref, b_ref, c_ref, d_ref, o_ref):
    wide = o_ref.shape[1]
    for slot, refs in ((0, (a_ref, c_ref)), (1, (b_ref, d_ref))):
        for own in range(2):

            @pl.when((pl.program_id(0) == slot) & (own_ref[0] == own))
            def _():
                for r in range(GROUP):
                    o_ref[pl.ds(r, refs[own].shape[0], stride=GROUP), :] = refs[own][
                        :, r * wide : (r + 1) * wide
                    ]


def chosen(kernel, own, grid, ins, in_specs, out, out_spec):
    ins = [streamed(x, spec) for x, spec in zip(ins, in_specs)]
    return pl.pallas_call(
        kernel,
        out_shape=result(out, out_spec),
        grid_spec=pltpu.PrefetchScalarGridSpec(
            num_scalar_prefetch=1, grid=grid, in_specs=in_specs, out_specs=out_spec
        ),
        compiler_params=pltpu.CompilerParams(vmem_limit_bytes=VMEM_BYTES),
    )(own, *ins)


def place_early_kernel(own_ref, a_ref, b_ref, c_ref, d_ref, shortcut_ref, expand_ref):
    count, rows, width = a_ref.shape
    for own, refs in enumerate(((a_ref, b_ref), (c_ref, d_ref))):

        @pl.when(own_ref[0] == own)
        def _():
            for half, ref in enumerate(refs):
                start = half * rows
                for k in range(count - 1):
                    shortcut_ref[start : start + rows, k * width : (k + 1) * width] = ref[k]
                expand_ref[start : start + rows] = ref[count - 1]


def place_late_kernel(own_ref, a_ref, b_ref, c_ref, d_ref, spatial_ref, reduce_ref, lateral_ref):
    _, rows, width = a_ref.shape
    taps, blocks = spatial_ref.shape[0], reduce_ref.shape[1] // width
    runs = reduce_ref.shape[0] // (2 * rows)
    wide = lateral_ref.shape[2]
    for own, refs in enumerate(((a_ref, b_ref), (c_ref, d_ref))):

        @pl.when(own_ref[0] == own)
        def _():
            for half, ref in enumerate(refs):
                start = half * rows
                for k in range(taps):
                    spatial_ref[k, start : start + rows] = ref[k]
                for k in range(blocks):
                    for j in range(runs):
                        first = (half * runs + j) * rows
                        reduce_ref[first : first + rows, k * width : (k + 1) * width] = ref[
                            taps + k * runs + j
                        ]
                for k in range(lateral_ref.shape[0]):
                    side = (k % 2) * wide
                    lateral_ref[k, start : start + rows] = ref[
                        taps + blocks * runs + k // 2, :, side : side + wide
                    ]


def place_weights(kernel, low, high, rows, own, outs):
    views = [x.reshape(-1, rows, x.shape[1]) for x in (low, *cross(low, high), high)]

    def whole(shape):
        zeros = (0,) * len(shape)
        return pl.BlockSpec(shape, lambda j, o: zeros, pipeline_mode=pl.Buffered(1))

    return pl.pallas_call(
        kernel,
        out_shape=[jax.ShapeDtypeStruct(shape, jnp.float32) for shape in outs],
        grid_spec=pltpu.PrefetchScalarGridSpec(
            num_scalar_prefetch=1,
            grid=(1,),
            in_specs=[whole(x.shape) for x in views],
            out_specs=[pl.BlockSpec(memory_space=pltpu.VMEM)] * len(outs),
        ),
        compiler_params=pltpu.CompilerParams(vmem_limit_bytes=VMEM_BYTES),
    )(own, *views)


def pieces_of(places):
    return max(n for n in range(1, 9) if places % (4 * n) == 0 or n == 1)


def load_rows(values, mask, own):
    grid = jnp.transpose(values[:, 0], (0, 3, 1, 2))
    _, places, frames, wide = grid.shape
    steps = pieces_of(places)
    size = places // steps
    return chosen(
        load_rows_kernel,
        own,
        (steps,),
        [grid, mask],
        [
            pl.BlockSpec((None, size, frames, wide), lambda j, o: (o[0], j, 0, 0)),
            pl.BlockSpec((size * frames, 128), lambda j, o: (j, 0)),
        ],
        (places * frames, wide),
        pl.BlockSpec((size * frames, wide), lambda j, o: (j, 0)),
    )


def packed_view(values):
    grid = jnp.transpose(values[:, 0], (0, 3, 1, 2))
    return grid.reshape(grid.shape[0], -1, grid.shape[3])


def load_packed(values, own):
    grid = packed_view(values)
    _, rows, wide = grid.shape
    out = (rows // GROUP, GROUP * wide)
    return chosen(
        load_packed_kernel,
        own,
        (1,),
        [grid],
        [pl.BlockSpec((None, rows, wide), lambda j, o: (o[0], 0, 0))],
        out,
        pl.BlockSpec(out, lambda j, o: (0, 0)),
    )


def cross(first, second):
    return (
        lax.ppermute(first, "section", [(1, 0)]),
        lax.ppermute(second, "section", [(0, 1)]),
    )


def place_rows(first, second, own, frames):
    to_zero, to_one = cross(first, second)
    rows, wide = first.shape
    places = rows // frames
    steps = pieces_of(places)
    size = places // steps

    def spec(slot, core):
        def where(t, j, o):
            used = (t == slot) & (o[0] == core)
            return (jnp.where(used, j, jnp.where(t > slot, steps - 1, 0)), 0)

        return pl.BlockSpec((size * frames, wide), where)

    out = chosen(
        place_rows_kernel,
        own,
        (2, steps),
        [first, to_zero, to_one, second],
        [spec(0, 0), spec(1, 0), spec(0, 1), spec(1, 1)],
        (2, places, frames, wide),
        pl.BlockSpec((None, size, frames, wide), lambda t, j, o: (t, j, 0, 0)),
    )
    return jnp.transpose(out, (0, 2, 3, 1))[None, :, None]


def place_packed(first, second, own, frames):
    to_zero, to_one = cross(first, second)
    rows, full = first.shape
    wide = full // GROUP
    out = chosen(
        place_packed_kernel,
        own,
        (2,),
        [first, to_zero, to_one, second],
        [pl.BlockSpec((rows, full), lambda t, o: (0, 0))] * 4,
        (2, rows * GROUP, wide),
        pl.BlockSpec((None, rows * GROUP, wide), lambda t, o: (t, 0, 0)),
    )
    grid = out.reshape(2, rows // frames, GROUP * frames, wide)
    return jnp.transpose(grid, (0, 2, 3, 1))[None, :, None]


def bits_of(axis):
    size, stride, found = lax.axis_size(axis), 1, []
    while stride < size:
        found.append((axis, stride))
        stride *= 2
    return found


def routes():
    near, far, deep = bits_of("tm"), [], bits_of("clip")
    middle = len(near) // 2
    near, far = near[:middle], near[middle:]
    one, two, three = near + far + deep, far + deep + near, deep + near + far
    return [list(zip(one, two)), list(zip(two, three)), list(zip(three, one))]


def halves(values, bit, axis=0):
    rows = values.shape[axis] // 2
    kept = lax.dynamic_slice_in_dim(values, bit * rows, rows, axis)
    return kept, lax.dynamic_slice_in_dim(values, (1 - bit) * rows, rows, axis)


def core_half(arrays):
    core = lax.axis_index("section")
    pairs = [halves(x, core, 1) for x in arrays]
    kept, sent = [
        jnp.concatenate([p[k].reshape(-1, p[k].shape[2]) for p in pairs]) for k in range(2)
    ]
    return kept + swap(sent)


def reduction(arrays, route):
    arrays = yield arrays
    total = core_half(arrays)
    bits = [side_of(pair) for pair in route]
    for pair, bit in zip(route, bits):
        (total,) = yield (total,)
        kept, sent = halves(total, bit)
        total = kept + trade(sent, pair)
    for pair, bit in reversed(list(zip(route, bits))):
        (total,) = yield (total,)
        taken = trade(total, pair)
        low, high = jnp.where(bit == 0, total, taken), jnp.where(bit == 0, taken, total)
        total = jnp.concatenate([low, high], axis=0)
    return total


def summed(arrays):
    arrays = yield arrays
    total = core_half(arrays)
    (total,) = yield (total,)
    return half_pieces(lax.psum(total, AXES), arrays)


def summed(groups):
    totals = lax.psum(tuple(core_half(arrays) for arrays in groups), AXES)
    totals = yield totals
    return totals


def worked(values):
    values = yield values
    return values


def held_grads(block, names):
    found = yield [block.grads[n] for n in names]
    for name, value in zip(names, found):
        block.grads[name] = value


def side_of(pair):
    sides = [(lax.axis_index(axis) // stride) % 2 for axis, stride in pair]
    return jnp.where(lax.axis_index("section") == 0, sides[0], sides[1])


def trade(values, pair):
    sizes = {axis: lax.axis_size(axis) for axis in AXES}
    partners = []
    for core, (axis, stride) in enumerate(pair):
        for clip in range(sizes["clip"]):
            for tm in range(sizes["tm"]):
                to = {"clip": clip, "tm": tm}
                to[axis] ^= stride
                partners.append(
                    tuple(
                        (core * sizes["clip"] + c) * sizes["tm"] + t
                        for c, t in ((clip, tm), (to["clip"], to["tm"]))
                    )
                )
    return lax.ppermute(values, ("section",) + AXES, partners)


def small_reduction(values):
    axes = ("section",) + AXES
    count = lax.axis_size("section") * lax.axis_size("clip") * lax.axis_size("tm")
    rows = -(-values.shape[0] // count) * count
    shares = jnp.pad(values, ((0, rows - values.shape[0]), (0, 0))).reshape(count, -1, values.shape[1])
    (shares,) = yield (shares,)
    share = jnp.sum(lax.all_to_all(shares, axes, 0, 0), axis=0)
    (share,) = yield (share,)
    copies = jnp.broadcast_to(share[None], (count,) + share.shape)
    out = lax.all_to_all(copies, axes, 0, 0).reshape(rows, -1)
    return out[: values.shape[0]]


class Job:
    def __init__(self, steps, paces=(1,)):
        self.steps, self.paces, self.result = steps, list(paces), None
        self.held = next(steps)

    def resume(self, held):
        for _ in range(self.paces.pop(0) if len(self.paces) > 1 else self.paces[0]):
            try:
                held = self.steps.send(held)
            except StopIteration as end:
                self.held, self.result = None, end.value
                return
        self.held = held

    def waits(self):
        if self.paces[0] == 0 and len(self.paces) > 1:
            self.paces.pop(0)
            return True
        return self.paces[0] == 0

    def finish(self):
        self.paces = [1]
        while self.held is not None:
            self.resume(self.held)
        return self.result


class Section:
    def __init__(self, index, small, norms, sizes, large):
        self.lateral, self.slow_reduce, self.slow_spatial, self.slow_expand, self.shortcut = [
            Stacked(x, index) for x in large
        ]
        self.inner, self.wide, self.depth = sizes["inner"], sizes["wide"], self.slow_expand.shape[1]
        start = 0
        for name in ("fast_spatial", "fast_reduce", "fast_expand"):
            setattr(self, name, Window(small, (index,), start, (sizes[name], 128)))
            start += sizes[name]
        self.widths = [
            self.inner, self.inner, self.wide, self.lateral.shape[1], self.depth, self.depth,
            self.slow_expand.shape[0], self.shortcut.shape[0],
        ]
        self.gains, self.biases = [None] * 8, [None] * 8
        cursor = 0
        for j in NORM_ORDER:
            width = self.widths[j] * (GROUP if j < 3 else 1)
            self.gains[j] = Window(norms, (index, 0), cursor, (1, width))
            self.biases[j] = Window(norms, (index, 1), cursor, (1, width))
            cursor += width


def norm_row(vector, widths):
    starts = [sum(widths[:j]) for j in range(8)]
    pieces = []
    for j in NORM_ORDER:
        piece = vector[starts[j] : starts[j] + widths[j]]
        pieces += [piece] * (GROUP if j < 3 else 1)
    return jnp.concatenate(pieces)


class Block:
    def __init__(self, section, mask, frames, shared):
        self.s, self.mask, self.frames, self.shared = section, mask, frames, shared
        self.rows = mask.shape[0]
        self.places = self.rows // frames
        self.side = math.isqrt(self.places)
        self.pad = -(-(self.side + 1) * frames // 8) * 8
        self.grads, self.sums, self.back = {}, {}, {}
        self.copies = lax.axis_size("clip") * lax.axis_size("tm")

    def window(self, width):
        return [(self.rows + 2 * self.pad, width)] * 3

    def lanes(self, width):
        return (width // 128, self.rows, 128)

    def fast_first(self, fast_input, own):
        rows, places, width = self.rows, self.places, GROUP * self.s.inner
        grid, full = packed_view(fast_input), GROUP * self.s.wide
        outs = [(rows, full), (rows, 2 * width), (places, width), (places, width)]
        return pl.pallas_call(
            partial(fast_first_kernel, frames=self.frames),
            out_shape=[jax.ShapeDtypeStruct(s, jnp.float32) for s in outs],
            grid_spec=pltpu.PrefetchScalarGridSpec(
                num_scalar_prefetch=1,
                grid=(1,),
                in_specs=[
                    pl.BlockSpec((None,) + grid.shape[1:], lambda j, o: (o[0], 0, 0)),
                    pl.BlockSpec((rows, 128), lambda j, o: (0, 0)),
                    self.s.fast_reduce.whole(),
                ],
                out_specs=[pl.BlockSpec(s, lambda j, o: (0, 0)) for s in outs],
                scratch_shapes=[
                    pltpu.VMEM(self.lanes(width), jnp.float32),
                    pltpu.VMEM((2 * width, full), jnp.float32),
                ],
            ),
            compiler_params=pltpu.CompilerParams(vmem_limit_bytes=VMEM_BYTES),
        )(own, pltpu.with_memory_space_constraint(grid, pltpu.HBM), self.mask, array_of(self.s.fast_reduce))

    def fast_forward(self, fast_in, parts):
        s, mask, frames, rows, places = self.s, self.mask, self.frames, self.rows, self.places
        c4 = self.shared
        self.fast_in = fast_in
        width, full = GROUP * s.inner, GROUP * s.wide
        both, low, high = parts
        self.first, sums = call(
            fast_join_kernel,
            [(rows, width), (self.copies, 2 * width + 128)],
            [both, from_previous(high), from_next(low), mask],
            [self.lanes(width)] * 2,
            frames=frames,
            inner=s.inner,
        )
        self.sums[0] = yield sums
        second, self.first_act, sums = call(
            conv_kernel,
            [(rows, width), (rows, width), (self.copies, 2 * width)],
            [self.first, self.sums[0][0], c4["fast"], s.gains[0], s.biases[0], mask, s.fast_spatial],
            self.window(width),
            offset=self.sums[0][1], fold=s.inner, side=self.side, frames=frames,
        )
        self.second = second
        self.sums[1] = yield sums
        self.third, self.second_act, sums = call(
            fast_expand_kernel,
            [(rows, full), (rows, width), (self.copies, 2 * s.wide)],
            [second, self.sums[1][0], c4["fast"], s.gains[1], s.biases[1], mask, s.fast_expand],
            offset=self.sums[1][1], fold=s.inner,
        )
        self.sums[2] = yield sums
        following = (self.following or self).s.fast_reduce
        lateral = s.widths[3]
        shapes = [(rows, full), (rows, lateral), (rows, lateral), (places, lateral)]
        if self.following:
            shapes += [(rows, 2 * width), (places, width), (places, width)]
        else:
            shapes += [(8, 256), (8, 128), (8, 128)]
        self.fast_out, here, onward, edge, *self.parts = call(
            fast_out_kernel,
            shapes,
            [
                self.third, fast_in, self.sums[2][0], c4["fast"], s.gains[2], s.biases[2], mask,
                s.lateral, following,
            ],
            [self.lanes(lateral), (2 * width, full)],
            offset=self.sums[2][1], frames=frames, more=self.following is not None,
        )
        self.lateral, sums = call(
            lateral_join_kernel,
            [(rows, lateral), (self.copies, 2 * lateral)],
            [here, onward, from_previous(edge), mask],
            [self.lanes(lateral)],
            frames=frames,
        )
        self.sums[3] = yield sums

    def slow_forward(self, slow_in):
        s, mask, frames, rows, places = self.s, self.mask, self.frames, self.rows, self.places
        count = self.shared["slow"]
        depth, lateral, wide, out_wide = s.depth, s.widths[3], slow_in.shape[1], s.widths[7]
        full = wide + lateral
        self.slow_in = slow_in
        r3, offset = self.sums[3]
        reduced, low, high, self.lateral_act = call_steps(
            reduce_kernel,
            3,
            [(rows, 3 * depth), (places, depth), (places, depth), (rows, lateral)],
            [columns(rows, depth), fixed((places, depth)), fixed((places, depth)), fixed((rows, lateral))],
            [slow_in, self.lateral, r3, count, s.gains[3], s.biases[3], mask, s.slow_reduce],
            [
                fixed((rows, wide)), fixed((rows, lateral)), fixed(r3.shape), fixed((1, 1)),
                s.gains[3].whole(), s.biases[3].whole(), fixed((rows, 128)),
                s.slow_reduce.block((depth, full), lambda j: (j, 0)),
            ],
            [(rows, full), self.lanes(depth)],
            offset=offset, frames=frames,
        )
        steps = out_wide // depth
        self.skipped, skip_sums = call_steps(
            shortcut_kernel,
            steps,
            [(rows, out_wide), (self.copies, 2 * out_wide)],
            [columns(rows, depth), fixed((self.copies, 2 * out_wide))],
            [slow_in, self.lateral_act, mask, s.shortcut],
            [
                fixed((rows, wide)), fixed((rows, lateral)), fixed((rows, 128)),
                s.shortcut.block((depth, full), lambda j: (j, 0)),
            ],
        )
        self.inner, sums = call(
            inner_join_kernel,
            [(rows, depth), (self.copies, 2 * depth)],
            [reduced, from_previous(high), from_next(low), mask],
            [self.lanes(depth)] * 2,
            frames=frames,
        )
        r, offset = yield jnp.concatenate([sums, skip_sums], axis=1)
        self.sums[4], self.sums[7] = (r, offset), (r, offset + 2 * depth)
        self.middle, self.inner_act, sums = call(
            conv_kernel,
            [(rows, depth), (rows, depth), (self.copies, 2 * depth)],
            [self.inner, r, count, s.gains[4], s.biases[4], mask, s.slow_spatial],
            self.window(depth),
            offset=offset, fold=0, side=self.side, frames=frames,
        )
        self.sums[5] = yield sums
        r5, offset = self.sums[5]
        self.expanded, self.middle_act, sums = call_steps(
            expand_kernel,
            steps,
            [(rows, out_wide), (rows, depth), (self.copies, 2 * out_wide)],
            [columns(rows, depth), fixed((rows, depth)), fixed((self.copies, 2 * out_wide))],
            [self.middle, r5, count, s.gains[5], s.biases[5], mask, s.slow_expand],
            [
                fixed((rows, depth)), fixed(r5.shape), fixed((1, 1)), s.gains[5].whole(),
                s.biases[5].whole(), fixed((rows, 128)),
                s.slow_expand.block((depth, depth), lambda j: (j, 0)),
            ],
            offset=offset,
        )
        self.sums[6] = yield sums
        self.slow_out = call_steps(
            slow_out_kernel,
            steps,
            [(rows, out_wide)],
            [columns(rows, depth)],
            *self.slow_pre_inputs(),
            offset6=self.sums[6][1], offset7=self.sums[7][1], total=out_wide,
        )[0]

    def slow_pre_inputs(self):
        s, rows, depth = self.s, self.rows, self.s.depth
        r6, r7 = self.sums[6][0], self.sums[7][0]
        wide = columns(rows, depth)
        gains = [x.parts(depth) for x in (s.gains[6], s.biases[6], s.gains[7], s.biases[7])]
        return (
            [
                self.expanded, self.skipped, r6, r7, self.shared["slow"], s.gains[6], s.biases[6],
                s.gains[7], s.biases[7], self.mask,
            ],
            [
                wide, wide, fixed(r6.shape), fixed(r7.shape), fixed((1, 1)), *gains,
                fixed((rows, 128)),
            ],
        )

    def slow_backward(self, slow_grad):
        s, mask, frames, rows, places = self.s, self.mask, self.frames, self.rows, self.places
        count = self.shared["slow"]
        depth, lateral, out_wide, wide = s.depth, s.widths[3], s.widths[7], self.slow_in.shape[1]
        full, steps = wide + lateral, out_wide // depth
        (r6, offset6), (r7, offset7) = self.sums[6], self.sums[7]
        ins, specs = self.slow_pre_inputs()
        pre, sums = call_steps(
            slow_slope_kernel,
            steps,
            [(rows, out_wide), (self.copies, 3 * out_wide)],
            [columns(rows, depth), fixed((self.copies, 3 * out_wide))],
            [slow_grad] + ins,
            [columns(rows, depth)] + specs,
            offset6=offset6, offset7=offset7, total=out_wide,
        )
        rb, offsetb = yield sums
        self.back[6], self.back[7] = (rb, offsetb, offsetb + out_wide), (rb, offsetb, offsetb + 2 * out_wide)
        r5, offset5 = self.sums[5]
        skip_grad, self.grads["slow_expand"], pre, sums = call_steps(
            expand_back_kernel,
            steps,
            [(rows, out_wide), (out_wide, depth), (rows, depth), (self.copies, 2 * depth)],
            [columns(rows, depth), bands(depth, depth), fixed((rows, depth)), fixed((self.copies, 2 * depth))],
            [
                pre, self.expanded, self.skipped, r6, r7, rb, count, s.gains[6], s.gains[7], mask,
                s.slow_expand, self.middle_act, self.middle, r5, s.gains[5], s.biases[5],
            ],
            [columns(rows, depth)] * 3
            + [fixed(r6.shape), fixed(r7.shape), fixed(rb.shape), fixed((1, 1))]
            + [s.gains[6].parts(depth), s.gains[7].parts(depth)]
            + [fixed((rows, 128)), s.slow_expand.block((depth, depth), lambda j: (j, 0))]
            + [fixed((rows, depth)), fixed((rows, depth))]
            + [fixed(r5.shape), s.gains[5].whole(), s.biases[5].whole()],
            [(rows, depth)],
            offset6=offset6, offset7=offset7, offsetb=offsetb, offset5=offset5, total=out_wide,
        )
        self.grads["shortcut"] = call_steps(
            joined_weight_kernel,
            steps,
            [(full // lateral, out_wide, lateral)],
            [pl.BlockSpec((full // lateral, depth, lateral), lambda j: (0, j, 0))],
            [skip_grad, self.slow_in, self.lateral_act],
            [columns(rows, depth), fixed((rows, wide)), fixed((rows, lateral))],
        )[0]
        rb, offsetb = yield sums
        self.back[5] = (rb, offsetb, offsetb + depth)
        r4, offset4 = self.sums[4]
        middle_grad, pre, sums = call(
            conv_back_kernel,
            [(rows, depth), (rows, depth), (self.copies, 2 * depth)],
            [
                pre, self.middle, r5, rb, count, s.gains[5], self.inner, r4, s.gains[4], s.biases[4],
                mask, s.slow_spatial,
            ],
            self.window(depth),
            offset=offset5, offsetb=offsetb, offsetu=offset4, fold=0, side=self.side, frames=frames,
        )
        self.grads["slow_spatial"] = call(
            conv_weight_kernel,
            [s.slow_spatial.shape],
            [self.inner_act, middle_grad],
            self.window(depth),
            fold=0, side=self.side, frames=frames,
        )[0]
        rb, offsetb = yield sums
        self.back[4] = (rb, offsetb, offsetb + depth)
        inner_grad, low, high = call(
            norm_back_kernel,
            [(rows, depth), (places, depth), (places, depth)],
            [pre, self.inner, r4, rb, count, s.gains[4], mask],
            [self.lanes(depth)],
            offset=offset4, offsetb=offsetb, fold=0, frames=frames,
        )
        r3, offset3 = self.sums[3]
        last = wide // lateral
        self.slow_in_grad, self.lateral_pre, reduced_grad, self.lateral_sums = call_steps(
            joined_back_kernel,
            last + 1,
            [(rows, wide), (rows, lateral), (rows, 3 * depth), (self.copies, 2 * lateral)],
            [
                pl.BlockSpec((rows, lateral), lambda j: (0, jnp.minimum(j, last - 1))),
                fixed((rows, lateral)), fixed((rows, 3 * depth)), fixed((self.copies, 2 * lateral)),
            ],
            [
                inner_grad, from_previous(high), from_next(low), skip_grad, s.slow_reduce,
                s.shortcut, mask,
                self.lateral, r3, count, s.gains[3], s.biases[3],
            ],
            [
                fixed((rows, depth)), fixed((places, depth)), fixed((places, depth)),
                fixed((rows, out_wide)), s.slow_reduce.block((3 * depth, lateral), lambda j: (0, j)),
                s.shortcut.block((out_wide, lateral), lambda j: (0, j)), fixed((rows, 128)),
                fixed((rows, lateral)), fixed(r3.shape), fixed((1, 1)), s.gains[3].whole(),
                s.biases[3].whole(),
            ],
            [self.lanes(depth)],
            offset=offset3, frames=frames,
        )
        self.grads["slow_reduce"] = call_steps(
            joined_weight_kernel,
            3,
            [(full // lateral, 3 * depth, lateral)],
            [pl.BlockSpec((full // lateral, depth, lateral), lambda j: (0, j, 0))],
            [reduced_grad, self.slow_in, self.lateral_act],
            [columns(rows, depth), fixed((rows, wide)), fixed((rows, lateral))],
        )[0]

    def fast_backward(self, fast_grad):
        s, mask, frames, rows, places = self.s, self.mask, self.frames, self.rows, self.places
        count, count4 = self.shared["slow"], self.shared["fast"]
        wide, inner, lateral = s.wide, s.inner, s.widths[3]
        width, full = GROUP * inner, GROUP * wide
        rb, offsetb = yield self.lateral_sums
        self.back[3] = (rb, offsetb, offsetb + lateral)
        r3, offset3 = self.sums[3]
        here, low, _ = call(
            norm_back_kernel,
            [(rows, lateral), (places, lateral), (places, lateral)],
            [self.lateral_pre, self.lateral, r3, rb, count, s.gains[3], mask],
            [self.lanes(lateral)],
            offset=offset3, offsetb=offsetb, fold=0, frames=frames,
        )
        r2, offset2 = self.sums[2]
        residual, onward, sums = call(
            lateral_back_kernel,
            [(rows, full), (rows, lateral), (self.copies, 2 * wide)],
            [
                here, from_next(low), fast_grad(), self.third, self.fast_in, r2, count4, s.gains[2],
                s.biases[2], mask, s.lateral,
            ],
            [self.lanes(lateral)],
            offset=offset2, frames=frames,
        )
        self.grads["lateral"] = call(
            lateral_weight_kernel, [(3, lateral, 2 * wide)], [here, onward, self.fast_out]
        )[0]
        rb, offsetb = yield sums
        self.back[2] = (rb, offsetb, offsetb + wide)
        r1, offset1 = self.sums[1]
        third_grad, pre, sums = call(
            fast_expand_back_kernel,
            [(rows, full), (rows, width), (self.copies, 2 * width)],
            [
                residual, self.third, r2, rb, count4, s.gains[2], self.second, r1, s.gains[1],
                s.biases[1], mask, s.fast_expand,
            ],
            offset=offset2, offsetb=offsetb, offsetu=offset1, fold=inner,
        )
        self.grads["fast_expand"] = call(
            fast_expand_weight_kernel,
            [(wide // GROUP, width)],
            [third_grad, self.second_act],
            fold=inner,
        )[0]
        rb, offsetb = yield sums
        self.back[1] = (rb, offsetb, offsetb + width)
        r0, offset0 = self.sums[0]
        second_grad, pre, sums = call(
            conv_back_kernel,
            [(rows, width), (rows, width), (self.copies, 2 * width)],
            [
                pre, self.second, r1, rb, count4, s.gains[1], self.first, r0, s.gains[0], s.biases[0],
                mask, s.fast_spatial,
            ],
            self.window(width),
            offset=offset1, offsetb=offsetb, offsetu=offset0, fold=inner, side=self.side,
            frames=frames,
        )
        self.grads["fast_spatial"] = call(
            conv_weight_kernel,
            [(9 * inner // GROUP, width)],
            [self.first_act, second_grad],
            self.window(width),
            fold=inner, side=self.side, frames=frames,
        )[0]
        rb, offsetb = yield sums
        self.back[0] = (rb, offsetb, offsetb + width)
        first_grad, low, high = call(
            norm_back_kernel,
            [(rows, width), (places, width), (places, width)],
            [pre, self.first, r0, rb, count4, s.gains[0], mask],
            [self.lanes(width)],
            offset=offset0, offsetb=offsetb, fold=inner, frames=frames,
        )
        self.fast_in_grad, self.grads["fast_reduce"] = call(
            fast_first_back_kernel,
            [(rows, full), (3 * inner, wide)],
            [
                first_grad, from_previous(high), from_next(low), residual, s.fast_reduce, mask,
                self.fast_in,
            ],
            [self.lanes(width)] * 2 + [(2 * width, full)],
            frames=frames, inner=inner,
        )

    def blocked(self, name):
        grad = self.grads[name]
        return grad if grad.ndim == 3 else grad[None]

    def fast_flat(self):
        return jnp.concatenate([self.grads[n] for n in ("fast_spatial", "fast_reduce", "fast_expand")])

    def norm_grads(self):
        gains, biases = [], []
        for j, width in enumerate(self.s.widths):
            rb, low, slope = self.back[j]
            span = GROUP * width if j < 2 else width
            for start, found in ((slope, gains), (low, biases)):
                total = jnp.sum(rb[:, start : start + span], axis=0)
                found.append(jnp.sum(total.reshape(-1, width), axis=0))
        return jnp.stack([jnp.concatenate(gains), jnp.concatenate(biases)])


class Task:
    def __init__(self, steps):
        self.steps = steps
        self.wanted = next(steps)

    def resume(self, totals):
        self.wanted = next(self.steps, None) if totals is None else self.send(totals)

    def send(self, totals):
        try:
            return self.steps.send(totals)
        except StopIteration:
            return None


def advance(*tasks, jobs=()):
    wanted = [task.wanted for task in tasks]
    r = sums_everywhere(jnp.concatenate(wanted, axis=1) if len(wanted) > 1 else wanted[0])
    jobs = [job for job in jobs if job.held is not None and not job.waits()]
    if jobs:
        r, held = lax.optimization_barrier((r, [job.held for job in jobs]))
        for job, values in zip(jobs, held):
            job.resume(values)
    offsets = [sum(w.shape[1] for w in wanted[:k]) for k in range(len(wanted))]
    return [(r, offset) for offset in offsets]


def body(
    slow_input,
    fast_input,
    frame_counts,
    fast_reduce,
    fast_spatial,
    fast_expand,
    lateral_conv,
    slow_reduce,
    slow_spatial,
    slow_expand,
    shortcut,
    norm_gain,
    norm_bias,
    slow_cotangent,
    fast_cotangent,
):
    own = lax.axis_index("section")
    lower = own == 0
    frames, positions = slow_input.shape[2], slow_input.shape[4]
    rows = frames * positions
    wide = fast_input.shape[3]

    which = jnp.reshape(own, (1,)).astype(jnp.int32)
    inner, depth = fast_reduce.shape[2], slow_expand.shape[2]
    widths = [
        inner, inner, wide, lateral_conv.shape[2], depth, depth, slow_expand.shape[1], shortcut.shape[1]
    ]
    rows_of = {
        "fast_spatial": jnp.tile(fast_spatial[0], (1, 1, GROUP)).reshape(-1, 128),
        "fast_reduce": fast_reduce[0].reshape(-1, 128),
        "fast_expand": jnp.tile(fast_expand[0], (1, GROUP)),
    }
    sizes = {name: x.shape[0] for name, x in rows_of.items()}
    sizes.update(inner=inner, wide=wide)
    norms = jnp.concatenate([norm_row(norm_gain[0], widths), norm_row(norm_bias[0], widths)])
    small = jnp.concatenate(list(rows_of.values()) + [norms.reshape(-1, 128)])
    small = lax.all_gather(small, "section")
    norms = small[:, small.shape[1] - norms.size // 128 :].reshape(2, 2, 1, -1)
    large = [
        lateral_conv[0],
        slow_reduce[0].reshape(-1, slow_reduce.shape[3]),
        slow_spatial[0],
        slow_expand[0],
        shortcut[0],
    ]
    large = [lax.all_gather(x, "section") for x in large]
    sections = [Section(index, small, norms, sizes, large) for index in range(2)]

    count_here = lax.dynamic_index_in_dim(frame_counts, own, 0, keepdims=False)
    frame = lax.axis_index("clip") * frames + lax.broadcasted_iota(
        jnp.int32, (positions, frames, 128), 1
    )
    mask = (frame < count_here).astype(jnp.float32).reshape(rows, 128)
    shared = {}
    blocks = [Block(section, mask, frames, shared) for section in sections]
    blocks[0].following, blocks[1].following = blocks[1], None

    fast_in, *parts = blocks[0].fast_first(fast_input, which)
    fast = [Task(blocks[0].fast_forward(fast_in, parts)), None]
    got = advance(fast[0])
    r = got[0][0]
    shared["slow"] = jnp.sum(r[:, r.shape[1] - 128 : r.shape[1] - 127], axis=0, keepdims=True)
    shared["fast"] = GROUP * shared["slow"]
    fast[0].resume(got[0])
    for step in range(2):
        fast[0].resume(advance(fast[0])[0])
    fast[1] = Task(blocks[1].fast_forward(blocks[0].fast_out, blocks[0].parts))
    got = advance(fast[0], fast[1])
    fast[0].resume(got[0])
    fast[1].resume(got[1])
    slow = [Task(blocks[0].slow_forward(load_rows(slow_input, mask, which))), None]
    for step in range(3):
        got = advance(slow[0], fast[1])
        slow[0].resume(got[0])
        fast[1].resume(got[1])
    slow[1] = Task(blocks[1].slow_forward(blocks[0].slow_out))
    out_fast = Job(worked([place_packed(blocks[0].fast_out, blocks[1].fast_out, which, frames)]))
    for step in range(3):
        slow[1].resume(advance(slow[1], jobs=[out_fast] if step == 0 else [])[0])

    zero, one = blocks
    ways = routes()
    jobs = []
    early_names, late_names = ("shortcut", "slow_expand"), ("slow_spatial", "slow_reduce", "lateral")

    def start(steps, paces=(1,)):
        jobs.append(Job(steps, paces))
        return jobs[-1]

    tasks = Task(one.slow_backward(load_rows(slow_cotangent, mask, which)))
    tasks.resume(advance(tasks)[0])
    start(held_grads(one, early_names))
    tasks.resume(advance(tasks, jobs=jobs)[0])
    start(held_grads(one, ("slow_spatial",)))
    tasks.resume(advance(tasks, jobs=jobs)[0])
    start(held_grads(one, ("slow_reduce",)))
    late = Task(one.fast_backward(lambda: load_packed(fast_cotangent, which)))
    soon = Task(zero.slow_backward(one.slow_in_grad))
    for step in range(3):
        got = advance(late, soon, jobs=jobs)
        late.resume(got[0])
        soon.resume(got[1])
        if step == 0:
            held_one = start(held_grads(one, ("lateral",)))
            early = start(reduction([zero.blocked(n) for n in early_names], ways[2]), PLANS[1])
        if step == 1:
            groups = [[one.blocked(n) for n in names] for names in (early_names, late_names)]
            whole = start(summed(groups), PLANS[0])
            start(held_grads(zero, ("slow_spatial",)))
        if step == 2:
            start(held_grads(zero, ("slow_reduce",)))
    last = Task(zero.fast_backward(lambda: one.fast_in_grad))
    got = advance(late, last, jobs=jobs)
    late.resume(got[0])
    last.resume(got[1])
    late_job = start(reduction([zero.blocked(n) for n in late_names], ways[0]), PLANS[2])
    late_job.resume(late_job.held)
    for step in range(3):
        last.resume(advance(last, jobs=jobs)[0])
    rest = Job(small_reduction(jnp.concatenate([zero.fast_flat(), one.fast_flat()]))).finish()

    totals = {}
    highs = whole.finish()
    placed = [
        place_rows(zero.slow_out, one.slow_out, which, frames),
        place_rows(zero.slow_in_grad, one.slow_in_grad, which, frames),
        place_packed(zero.fast_in_grad, one.fast_in_grad, which, frames),
    ]
    highs, placed, rest = lax.optimization_barrier((highs, placed, rest))
    low, high = early.finish(), highs[0]
    totals["shortcut"], totals["slow_expand"] = place_weights(
        place_early_kernel, low, high, slow_expand.shape[1] // 2, which,
        [shortcut.shape[1:], slow_expand.shape[1:]],
    )
    low, high = late_job.finish(), highs[1]
    totals["slow_spatial"], totals["slow_reduce"], totals["lateral"] = place_weights(
        place_late_kernel, low, high, depth // 2, which,
        [slow_spatial.shape[1:], (3 * depth, slow_reduce.shape[3]), lateral_conv.shape[1:]],
    )
    half = rest.shape[0] // 2
    flat, cursor = jnp.where(lower, rest[:half], rest[half:]), 0
    for name in ("fast_spatial", "fast_reduce", "fast_expand"):
        size = sizes[name] if name == "fast_reduce" else sizes[name] // GROUP
        piece = flat[cursor : cursor + size]
        if name != "fast_reduce":
            count = inner if name == "fast_spatial" else wide
            piece = piece.reshape(-1, count // GROUP, GROUP, inner)
            piece = jnp.swapaxes(piece, 1, 2)
        totals[name] = piece
        cursor += size
    names = (
        "fast_reduce",
        "fast_spatial",
        "fast_expand",
        "lateral",
        "slow_reduce",
        "slow_spatial",
        "slow_expand",
        "shortcut",
    )
    norm_grads = [block.norm_grads() for block in blocks]
    kept = jnp.where(lower, norm_grads[0], norm_grads[1])
    kept = kept + swap(jnp.where(lower, norm_grads[1], norm_grads[0]))
    shapes = [
        x.shape
        for x in (
            fast_reduce, fast_spatial, fast_expand, lateral_conv, slow_reduce, slow_spatial,
            slow_expand, shortcut,
        )
    ]
    totals = [totals[name].reshape(shape) for name, shape in zip(names, shapes)]
    return (
        placed[0],
        out_fast.finish()[0],
        placed[1],
        placed[2],
        *totals,
        kept[None, 0],
        kept[None, 1],
    )


def solution(mesh):
    acts = P(None, "tm", "clip", None, None)
    outs = P("section", None, "tm", "clip", None, None)
    four, three, two = P("section", None, None, None), P("section", None, None), P("section", None)
    weights = (four, four, three, four, four, four, three, three)
    return jax.shard_map(
        body,
        mesh=mesh,
        in_specs=(acts, acts, P(None, "tm"), *weights, two, two, acts, acts),
        out_specs=(outs, outs, outs, outs, *weights, two, two),
        check_vma=False,
    )
```
